256 devices in a mesh: row: 8 (over y, core), col: 16 (over z, x_hi), slab: 2 (over x_lo).
Axes of the slice: x: 4 (x_hi: 2, x_lo: 2; x = x_hi * 2 + x_lo), y: 4, z: 8, core: 2. Of those that a mesh axis runs over, the one named last changes fastest.
Arguments:
- feats: bfloat16 [65536, 256], P(('slab', 'col', 'row')), parts along dimension 0, may hold values from -6 to 6
- weight: bfloat16 [256, 256], replicated, may hold values from -0.375 to 0.375
- bias: float32 [256], replicated, may hold values from -4 to 4
- grad_out: bfloat16 [65536, 256], P(('slab', 'row', 'col')), parts along dimension 0, may hold values from -20 to 20
- tile_vals: bfloat16 [16, 16, 192, 128, 128], P(('slab', 'row'), 'col'), parts along dimension 0, may hold values from 0 to 1, as said below
- tile_rows: int32 [16, 16, 192], P(('slab', 'row'), 'col'), parts along dimension 0, may hold values from 0 to 31, as said below
- tile_cols: int32 [16, 16, 192], P(('slab', 'row'), 'col'), parts along dimension 0, may hold values from 0 to 15, as said below
- tile_count: int32 [16, 16], P(('slab', 'row'), 'col'), parts along dimension 0, may hold values from 1 to 192, as said below
Outputs:
- hidden_out: bfloat16 [65536, 256], P(('slab', 'row', 'col')), parts along dimension 0
- grad_feats: bfloat16 [65536, 256], P(('slab', 'col', 'row')), parts along dimension 0
- grad_weight: float32 [512, 256], P('slab'), parts along dimension 0
- grad_bias: float32 [512], P('slab'), parts along dimension 0
The draws below stay inside these ranges and needn't reach their ends.
There are 2 independent parts, one for each index of `slab`. The reference program is written for one: setup_inputs(seed, part) draws one part's arguments, and reference() takes and returns one part's arrays. A program takes and returns all parts, laid end to end along the dimension named above; an argument that names none is the same for every part. Nothing has to cross between parts.
Inputs may be any that keep to these rules, and one draw needn't show every extreme that they name: `tile_count`: each block's live tile count; some block has exactly 192 in every draw. `tile_rows`: tile rows within a block; positions of a block's tiles may repeat. `tile_cols`: tile columns within a block. `tile_vals`: nonnegative edge weights.
All inputs are finite; a program needn't handle non-finite values.
Results may differ from the reference program's by a relative error of at most 0.023.
Values may be sent and summed in bfloat16 or wider, within the bound.
No kernel may reach another device: no remote copies, remote signals or barrier semaphores. Data moves between devices by JAX's collectives and lax.ppermute only.
A program may use at most 128 MiB of HBM per device.

```python
import math
import jax
import jax.numpy as jnp
from jax import lax

H = 256
S = 256
MAXT = 192
TILE = 128
TB = 32
NODES = 32768
CT_ROWS = 32
CT_COLS = 16
N_ROW = 8
N_COL = 16


def draw_tile_count(key, part):
    key = jax.random.fold_in(key, 1)
    pick_key, level_key = jax.random.split(key)
    levels = jax.random.randint(level_key, (N_ROW, N_COL), 1, 9)
    counts = jnp.maximum(1, MAXT * levels * levels // 64)
    busiest = jax.random.randint(pick_key, (), 0, N_ROW * N_COL)
    flat_index = jnp.arange(N_ROW * N_COL, dtype=jnp.int32).reshape(N_ROW, N_COL)
    return jnp.where(flat_index == busiest, MAXT, counts).astype(jnp.int32)


def draw_tile_rows(key, part):
    key = jax.random.fold_in(key, 2)
    return jax.random.randint(key, (N_ROW, N_COL, MAXT), 0, S * N_COL // TILE).astype(jnp.int32)


def draw_tile_cols(key, part):
    key = jax.random.fold_in(key, 3)
    return jax.random.randint(key, (N_ROW, N_COL, MAXT), 0, S * N_ROW // TILE).astype(jnp.int32)


def draw_tile_vals(key, part):
    key = jax.random.fold_in(key, 4)
    first_key = jax.random.fold_in(key, 0)
    reach = 0.4 * MAXT * TILE / S
    entries = jax.random.uniform(first_key, (N_ROW, N_COL, MAXT, TILE, TILE), jnp.float32, 0.0, 1.0)
    values = entries * (3.0 / (reach * TILE)) ** 0.5
    return jnp.minimum(values, 1.0).astype(jnp.bfloat16)


def draw_grad_out(key, part):
    key = jax.random.fold_in(key, 5)
    base_key, level_key = jax.random.split(key, 2)
    position = jnp.arange(NODES, dtype=jnp.float32) / NODES
    level = jax.random.uniform(level_key, (NODES, 1), jnp.float32, 0.0, 1.0)
    row_scale = (1.0 + 2.0 * position)[:, None] * 10.0 ** level / 6.0
    values = row_scale * jnp.clip(jax.random.normal(base_key, (NODES, H), jnp.float32), -4.0, 4.0)
    return values.astype(jnp.bfloat16)


def block_levels(own_key, shape, pieces, low, largest):
    def one(dim, shards_of):
        steps = jax.random.uniform(jax.random.fold_in(jax.random.fold_in(own_key, 6), dim), (shards_of,), jnp.float32, low / len(pieces), largest / len(pieces))
        return jnp.repeat(jnp.exp(steps), shape[dim] // shards_of).reshape((-1,) + (1,) * (len(shape) - dim - 1))

    factor_of = one(*pieces[0])
    for cut in pieces[1:]:
        factor_of = factor_of * one(*cut)
    return factor_of


def scatter_about(own_key, dims, width, bound, cuts=(), kind=jnp.bfloat16):
    level = block_levels(own_key, dims, cuts, -0.22, 0.18) if cuts else 1.0
    array = jax.random.normal(own_key, dims, jnp.float32) * width * level
    return jnp.minimum(jnp.maximum(array, -bound), bound).astype(kind)


def setup_inputs(seed: int = 0, part: int = 0) -> dict:
    key_of = jax.random.split(jax.random.key(seed), 9)
    part_keys = jax.random.split(jax.random.fold_in(key_of[8], part), 9)
    feats = scatter_about(part_keys[0], (NODES, H), 1.0, 6.0, ((0, 128),))
    weight = scatter_about(key_of[1], (H, H), H ** -0.5, 0.375)
    bias = scatter_about(key_of[2], (H,), 1.0, 4.0, (), jnp.float32)
    grad_out = draw_grad_out(jax.random.fold_in(jax.random.fold_in(key_of[8], part), 71), part)
    tile_vals = draw_tile_vals(jax.random.fold_in(jax.random.fold_in(key_of[8], part), 71), part)
    tile_rows = draw_tile_rows(jax.random.fold_in(jax.random.fold_in(key_of[8], part), 71), part)
    tile_cols = draw_tile_cols(jax.random.fold_in(jax.random.fold_in(key_of[8], part), 71), part)
    tile_count = draw_tile_count(jax.random.fold_in(jax.random.fold_in(key_of[8], part), 71), part)
    return {"feats": feats, "weight": weight, "bias": bias, "grad_out": grad_out, "tile_vals": tile_vals, "tile_rows": tile_rows, "tile_cols": tile_cols, "tile_count": tile_count}


def forward_block(values, where_rows, where_cols, live_count, source):
    feature_width = source.shape[-1]

    def accumulate(batch_index, running):
        first_slot = batch_index * TB
        tile_block = lax.dynamic_slice_in_dim(values, first_slot, TB, 0).astype(jnp.float32)
        slot_rows = lax.dynamic_slice_in_dim(where_rows, first_slot, TB, 0)
        slot_cols = lax.dynamic_slice_in_dim(where_cols, first_slot, TB, 0)
        live_mask = (first_slot + jnp.arange(TB, dtype=jnp.int32) < live_count).astype(jnp.float32)
        picked = jnp.take(source, slot_cols, axis=0).astype(jnp.float32)
        product = jnp.einsum('tmn,tnh->tmh', tile_block, picked) * live_mask[:, None, None]
        return running.at[slot_rows].add(product)
    batches = (live_count + TB - 1) // TB
    return lax.fori_loop(0, batches, accumulate, jnp.zeros((CT_ROWS, TILE, feature_width), jnp.float32))

def backward_block(values, where_rows, where_cols, live_count, source):
    feature_width = source.shape[-1]

    def accumulate(batch_index, running):
        first_slot = batch_index * TB
        tile_block = lax.dynamic_slice_in_dim(values, first_slot, TB, 0).astype(jnp.float32)
        slot_rows = lax.dynamic_slice_in_dim(where_rows, first_slot, TB, 0)
        slot_cols = lax.dynamic_slice_in_dim(where_cols, first_slot, TB, 0)
        live_mask = (first_slot + jnp.arange(TB, dtype=jnp.int32) < live_count).astype(jnp.float32)
        picked = jnp.take(source, slot_rows, axis=0).astype(jnp.float32)
        product = jnp.einsum('tmn,tmh->tnh', tile_block, picked) * live_mask[:, None, None]
        return running.at[slot_cols].add(product)
    batches = (live_count + TB - 1) // TB
    return lax.fori_loop(0, batches, accumulate, jnp.zeros((CT_COLS, TILE, feature_width), jnp.float32))

def reference(feats, weight, bias, grad_out, tile_vals, tile_rows, tile_cols, tile_count):
    feature_width = feats.shape[1]
    projected = jnp.dot(feats, weight, preferred_element_type=jnp.float32).astype(jnp.bfloat16)
    col_blocks = projected.reshape(N_COL, CT_COLS, TILE, feature_width)

    def row_block(row_index):

        def add_term(running, col_index):
            term = forward_block(tile_vals[row_index, col_index], tile_rows[row_index, col_index], tile_cols[row_index, col_index], tile_count[row_index, col_index], col_blocks[col_index])
            rounded = lax.optimization_barrier(term.astype(jnp.bfloat16))
            return (running + rounded.astype(jnp.float32), None)
        running, _ = lax.scan(add_term, jnp.zeros((CT_ROWS, TILE, feature_width), jnp.float32), jnp.arange(N_COL, dtype=jnp.int32))
        return running
    summed = lax.map(row_block, jnp.arange(N_ROW, dtype=jnp.int32)).reshape(NODES, feature_width)
    pre_act = summed + bias[None, :]
    gate_value = jax.nn.sigmoid(pre_act)
    hidden_out = (pre_act * gate_value).astype(jnp.bfloat16)
    slope = gate_value * (1.0 + pre_act * (1.0 - gate_value))
    out_grad = (grad_out.astype(jnp.float32) * slope).astype(jnp.bfloat16)
    row_blocks = out_grad.reshape(N_ROW, CT_ROWS, TILE, feature_width)

    def col_block(col_index):

        def add_term(running, row_index):
            term = backward_block(tile_vals[row_index, col_index], tile_rows[row_index, col_index], tile_cols[row_index, col_index], tile_count[row_index, col_index], row_blocks[row_index])
            rounded = lax.optimization_barrier(term.astype(jnp.bfloat16))
            return (running + rounded.astype(jnp.float32), None)
        running, _ = lax.scan(add_term, jnp.zeros((CT_COLS, TILE, feature_width), jnp.float32), jnp.arange(N_ROW, dtype=jnp.int32))
        return running
    back = lax.map(col_block, jnp.arange(N_COL, dtype=jnp.int32)).reshape(NODES, feature_width)
    back_bf = back.astype(jnp.bfloat16)
    grad_feats = jnp.dot(back_bf, weight.T, preferred_element_type=jnp.float32).astype(jnp.bfloat16)
    grad_scale = 1.0 / math.sqrt(NODES)
    grad_weight = jnp.dot(feats.T, back_bf, preferred_element_type=jnp.float32) * grad_scale
    grad_bias = lax.optimization_barrier(jnp.sum(out_grad.astype(jnp.float32), axis=0)) * grad_scale
    return (hidden_out, grad_feats, grad_weight, grad_bias)
```

```python
import functools
import math

import jax
import jax.numpy as jnp
from jax import lax
from jax.experimental import pallas as pl
from jax.experimental.pallas import tpu as pltpu
from jax.sharding import PartitionSpec as P

TILE = 128
UNROLL = 8
NY = 4
NZ = 8
F32 = jnp.float32
BF16 = jnp.bfloat16
LIMIT = pltpu.CompilerParams(vmem_limit_bytes=32 * 2**20)


def vmem():
    return pl.BlockSpec(memory_space=pltpu.VMEM)


def smem():
    return pl.BlockSpec(memory_space=pltpu.SMEM)


def shape(rows, dtype):
    return jax.ShapeDtypeStruct((rows, 256), dtype)


def call(body, name, out_shape, args, scalars=0, scratch=(), flops=0, moved=0):
    return pl.pallas_call(
        body,
        name=name,
        out_shape=out_shape,
        in_specs=[smem()] * scalars + [vmem()] * (len(args) - scalars),
        out_specs=jax.tree.map(lambda _: vmem(), out_shape),
        scratch_shapes=scratch,
        compiler_params=LIMIT,
        cost_estimate=pl.CostEstimate(flops=flops, bytes_accessed=moved, transcendentals=0),
    )(*args)


def to_core(a):
    return lax.ppermute(a, "row", [(i, i ^ 1) for i in range(2 * NY)])


def to_y(a, step):
    return lax.ppermute(a, "row", [(i, (i + 2 * step) % (2 * NY)) for i in range(2 * NY)])


def to_x(a):
    return lax.ppermute(a, "col", [(i, i ^ 1) for i in range(2 * NZ)])


def to_z(a, step):
    return lax.ppermute(a, "col", [(i, (i + 2 * step) % (2 * NZ)) for i in range(2 * NZ)])


def flip_z(a, bit):
    return lax.ppermute(a, "col", [(i, i ^ (2 * bit)) for i in range(2 * NZ)])


def gather_row(own):
    got = {(0, 0): own}
    for step in (1, -1, 2):
        got[(-step) % NY, 0] = to_y(own, step)
    got[0, 1] = to_core(own)
    for dy in (1, 3, 2):
        got[dy, 1] = to_core(got[dy, 0])
    return got


def gather_col(own):
    got = {(0, 0): own}
    got[0, 1] = to_x(own)
    for step in (1, -1, 2, -2, 4):
        got[(-step) % NZ, 0] = to_z(own, step)
    got[3, 0] = to_z(got[2, 0], -1)
    got[5, 0] = to_z(got[6, 0], 1)
    for dz in (1, 7, 2, 6, 4):
        got[dz, 1] = to_x(got[dz, 0])
    got[3, 1] = to_z(got[0, 1], -3)
    got[5, 1] = to_z(got[0, 1], 3)
    return got


def place(ref, total, first, dtype):
    for half in range(2):
        ref[half * TILE : (half + 1) * TILE] = total[2 * first + half].astype(dtype)


def forward_body(rows, cols, count, vals, *rest):
    blocks, outs, (source, total) = rest[:8], rest[8:-2], rest[-2:]
    for k in range(8):
        for half in range(2):
            source[2 * k + half] = blocks[k][half * TILE : (half + 1) * TILE]
    total[...] = jnp.zeros_like(total)
    live = count[0]

    def batch(i, carry):
        terms = []
        for u in range(UNROLL):
            t = i * UNROLL + u
            terms.append(jnp.dot(vals[t], source[cols[t]], preferred_element_type=F32))
        for u in range(UNROLL):
            t = i * UNROLL + u
            r = jnp.where(t < live, rows[t], 32)
            total[r] = total[r] + terms[u]
        return carry

    lax.fori_loop(0, (live + UNROLL - 1) // UNROLL, batch, 0)
    own, kept, up, down, over, far_up, far_down = outs
    place(own, total, 0, F32)
    for n, (dz, dx) in enumerate(((0, 1), (1, 0), (7, 0), (2, 0), (6, 0), (4, 0))):
        place(kept.at[n], total, 2 * dz + dx, F32)
    place(up, total, 2 * 3, BF16)
    place(down, total, 2 * 5, BF16)
    for n, dz in enumerate((1, 7, 2, 6, 4)):
        place(over.at[n], total, 2 * dz + 1, BF16)
    place(far_up, total, 2 * 3 + 1, BF16)
    place(far_down, total, 2 * 5 + 1, BF16)


def relay_body(kept, up, down, over, far_up, far_down, *outs):
    def wide(ref):
        return ref[...].astype(F32)

    outs[0][...] = (kept[0] + wide(far_up) + wide(far_down)).astype(BF16)
    outs[1][...] = (kept[1] + wide(over.at[0])).astype(BF16)
    outs[2][...] = (kept[2] + wide(over.at[1])).astype(BF16)
    outs[3][...] = (kept[3] + wide(over.at[2]) + wide(up)).astype(BF16)
    outs[4][...] = (kept[4] + wide(over.at[3]) + wide(down)).astype(BF16)
    outs[5][...] = (kept[5] + wide(over.at[4])).astype(BF16)


def activate_body(own, a, b, c, d, e, f, weight, bias, given, hidden, grad, high, low):
    summed = own[...]
    for ref in (a, b, c, d, e, f):
        summed = summed + ref[...].astype(F32)
    top = summed.astype(BF16)
    rest = (summed - top.astype(F32)).astype(BF16)
    high[...] = top
    low[...] = rest
    pre_act = (
        jnp.dot(top, weight[...], preferred_element_type=F32)
        + jnp.dot(rest, weight[...], preferred_element_type=F32)
        + bias[...]
    )
    gate_value = jax.nn.sigmoid(pre_act)
    hidden[...] = (pre_act * gate_value).astype(BF16)
    slope = gate_value * (1.0 + pre_act * (1.0 - gate_value))
    grad[...] = (given[...].astype(F32) * slope).astype(BF16)


def terms_body(order, high, low, grad, kept, sent, whole):
    g = grad[...]
    dims = (((0,), (0,)), ((), ()))
    whole[...] = lax.dot_general(high[...], g, dims, preferred_element_type=F32) + lax.dot_general(
        low[...], g, dims, preferred_element_type=F32
    )
    sums = jnp.sum(g.astype(F32), axis=0, keepdims=True)
    for dy in range(NY):
        for dc, ref in enumerate((kept, sent)):
            first = pl.multiple_of(order[2 * dy + dc] * 32, 32)
            ref[dy, 0:32] = whole[pl.ds(first, 32)]
            ref[dy, 32:40] = jnp.broadcast_to(sums, (8, 256))


def backward_body(rows, cols, count, vals, *rest):
    blocks, outs, (source, total) = rest[:16], rest[16:-2], rest[-2:]
    for k in range(16):
        for half in range(2):
            source[2 * k + half] = blocks[k][half * TILE : (half + 1) * TILE]
    total[...] = jnp.zeros_like(total)
    live = count[0]

    def batch(i, carry):
        terms = []
        for u in range(UNROLL):
            t = i * UNROLL + u
            terms.append(
                lax.dot_general(
                    vals[t], source[rows[t]], (((0,), (0,)), ((), ())), preferred_element_type=F32
                )
            )
        for u in range(UNROLL):
            t = i * UNROLL + u
            c = jnp.where(t < live, cols[t], 16)
            total[c] = total[c] + terms[u]
        return carry

    lax.fori_loop(0, (live + UNROLL - 1) // UNROLL, batch, 0)
    own, kept, core, over = outs
    place(own, total, 0, F32)
    for n, dy in enumerate((1, 2, 3)):
        place(kept.at[n], total, 2 * dy, F32)
        place(over.at[n], total, 2 * dy + 1, BF16)
    place(core, total, 1, BF16)


def back_relay_body(kept, over, *outs):
    for n in range(3):
        outs[n][...] = (kept[n] + over[n].astype(F32)).astype(BF16)


def finish_body(own, a, b, c, d, weight, out):
    back = own[...]
    for ref in (a, b, c, d):
        back = back + ref[...].astype(F32)
    out[...] = lax.dot_general(
        back.astype(BF16), weight[...], (((1,), (1,)), ((), ())), preferred_element_type=F32
    ).astype(BF16)


def assemble_body(scale, order, same, other, weight, bias):
    for dy in range(NY):
        for dc, ref in enumerate((same, other)):
            first = pl.multiple_of(order[2 * dy + dc] * 32, 32)
            weight[pl.ds(first, 32)] = ref[dy, 0:32] * scale
    bias[...] = same[0, 32:40] * scale


def sum_terms(kept, sent, order, scale):
    mine = kept + to_core(sent)
    piece = mine[0]
    for step in (1, 3, 2):
        piece = piece + to_y(mine[step], step)
    piece = piece + to_x(piece)
    for bit in (1, 2, 4):
        piece = piece + flip_z(piece, bit)
    parts = [piece, None, None, None]
    for step in (1, 3, 2):
        parts[(-step) % NY] = to_y(piece, step)
    same = jnp.stack(parts)
    other = to_core(same)
    return call(
        functools.partial(assemble_body, scale),
        "assemble",
        (shape(256, F32), shape(8, F32)),
        (order, same, other),
        scalars=1,
    )


def per_device(feats, weight, bias, grad_out, tile_vals, tile_rows, tile_cols, tile_count):
    shard = feats.shape[0]
    scale = 1.0 / math.sqrt(shard * 2 * NY * 2 * NZ)
    vals = tile_vals[0, 0]
    count = tile_count[0]
    row, col = lax.axis_index("row"), lax.axis_index("col")
    y, core, z, x = row // 2, row % 2, col // 2, col % 2
    owner_row, owner_col = tile_rows[0, 0] // 2, tile_cols[0, 0] // 2
    rel_z = (owner_row // 2 - z) % NZ
    rel_x = (owner_row + x) % 2
    rows = (rel_z * 2 + rel_x) * 2 + tile_rows[0, 0] % 2
    rel_y = (owner_col // 2 - y) % NY
    rel_c = (owner_col + core) % 2
    cols = (rel_y * 2 + rel_c) * 2 + tile_cols[0, 0] % 2
    steps = jnp.arange(2 * NY, dtype=jnp.int32)
    order = (steps // 2 + y) % NY * 2 + (steps + core) % 2

    source = gather_row(feats)
    work = 2 * 192 * TILE * TILE * 256
    own, kept, up, down, over, far_up, far_down = call(
        forward_body,
        "forward_tiles",
        (
            shape(shard, F32),
            jax.ShapeDtypeStruct((6, shard, 256), F32),
            shape(shard, BF16),
            shape(shard, BF16),
            jax.ShapeDtypeStruct((5, shard, 256), BF16),
            shape(shard, BF16),
            shape(shard, BF16),
        ),
        (rows, cols, count, vals, *[source[k // 2, k % 2] for k in range(8)]),
        scalars=3,
        scratch=(pltpu.VMEM((16, TILE, 256), BF16), pltpu.VMEM((33, TILE, 256), F32)),
        flops=work,
        moved=16 * 2**20,
    )
    over = to_x(over)
    far_up, far_down = to_z(far_up, 3), to_z(far_down, -3)
    up, down = to_z(up, 1), to_z(down, -1)
    sends = call(
        relay_body,
        "relay",
        tuple(shape(shard, BF16) for _ in range(6)),
        (kept, up, down, over, far_up, far_down),
        moved=4 * 2**20,
    )
    got = [to_x(sends[0])] + [to_z(a, s) for a, s in zip(sends[1:], (1, -1, 2, -2, 4))]
    hidden_out, own_grad, high, low = call(
        activate_body,
        "activate",
        tuple(shape(shard, BF16) for _ in range(4)),
        (own, *got, weight, bias[None, :], grad_out),
        flops=4 * 256**3,
        moved=2 * 2**20,
    )
    grads = gather_col(own_grad)
    kept_terms, sent_terms = call(
        terms_body,
        "weight_terms",
        (jax.ShapeDtypeStruct((NY, 40, 256), F32), jax.ShapeDtypeStruct((NY, 40, 256), F32)),
        (order, high, low, own_grad),
        scalars=1,
        scratch=(pltpu.VMEM((256, 256), F32),),
        flops=4 * 256**3,
        moved=2**20,
    )
    grad_weight, grad_bias = sum_terms(kept_terms, sent_terms, order, scale)
    own, kept, same, over = call(
        backward_body,
        "backward_tiles",
        (
            shape(shard, F32),
            jax.ShapeDtypeStruct((3, shard, 256), F32),
            shape(shard, BF16),
            jax.ShapeDtypeStruct((3, shard, 256), BF16),
        ),
        (rows, cols, count, vals, *[grads[k // 2, k % 2] for k in range(16)]),
        scalars=3,
        scratch=(pltpu.VMEM((32, TILE, 256), BF16), pltpu.VMEM((17, TILE, 256), F32)),
        flops=work,
        moved=16 * 2**20,
    )
    over = to_core(over)
    same = to_core(same)
    sends = call(
        back_relay_body,
        "back_relay",
        tuple(shape(shard, BF16) for _ in range(3)),
        (kept, over),
        moved=2**20,
    )
    got = [to_y(a, s) for a, s in zip(sends, (1, 2, 3))]
    grad_feats = call(
        finish_body,
        "finish",
        shape(shard, BF16),
        (own, same, *got, weight),
        flops=2 * 256**3,
        moved=2**20,
    )
    return (hidden_out, grad_feats, grad_weight, grad_bias[0])


def solution(mesh):
    in_specs = (
        P(("slab", "col", "row"), None),
        P(),
        P(),
        P(("slab", "row", "col"), None),
        P(("slab", "row"), "col", None, None, None),
        P(("slab", "row"), "col", None),
        P(("slab", "row"), "col", None),
        P(("slab", "row"), "col"),
    )
    out_specs = (
        P(("slab", "row", "col"), None),
        P(("slab", "col", "row"), None),
        P("slab", None),
        P("slab"),
    )
    return jax.shard_map(
        per_device, mesh=mesh, in_specs=in_specs, out_specs=out_specs, check_vma=False
    )
```

```python
import functools
import math

import jax
import jax.numpy as jnp
from jax import lax
from jax.experimental import pallas as pl
from jax.experimental.pallas import tpu as pltpu
from jax.sharding import PartitionSpec as P

TILE = 128
UNROLL = 8
ORDER = (
    ((0, 0), (0, 1), (1, 0), (7, 0)),
    ((1, 1), (7, 1), (2, 0), (6, 0)),
    ((2, 1), (6, 1), (3, 0), (5, 0)),
    ((3, 1), (5, 1), (4, 0), (4, 1)),
)
NY = 4
NZ = 8
F32 = jnp.float32
BF16 = jnp.bfloat16
LIMIT = pltpu.CompilerParams(vmem_limit_bytes=32 * 2**20)


def vmem():
    return pl.BlockSpec(memory_space=pltpu.VMEM)


def smem():
    return pl.BlockSpec(memory_space=pltpu.SMEM)


def shape(rows, dtype):
    return jax.ShapeDtypeStruct((rows, 256), dtype)


def call(body, name, out_shape, args, scalars=0, scratch=(), flops=0, moved=0, specs=None):
    return pl.pallas_call(
        body,
        name=name,
        out_shape=out_shape,
        in_specs=specs or [smem()] * scalars + [vmem()] * (len(args) - scalars),
        out_specs=jax.tree.map(lambda _: vmem(), out_shape),
        scratch_shapes=scratch,
        compiler_params=LIMIT,
        cost_estimate=pl.CostEstimate(flops=flops, bytes_accessed=moved, transcendentals=0),
    )(*args)


def to_core(a):
    return lax.ppermute(a, "row", [(i, i ^ 1) for i in range(2 * NY)])


def to_y(a, step):
    return lax.ppermute(a, "row", [(i, (i + 2 * step) % (2 * NY)) for i in range(2 * NY)])


def to_x(a):
    return lax.ppermute(a, "col", [(i, i ^ 1) for i in range(2 * NZ)])


def to_z(a, step):
    return lax.ppermute(a, "col", [(i, (i + 2 * step) % (2 * NZ)) for i in range(2 * NZ)])


def gather_row(own):
    got = {(0, 0): own}
    for step in (1, -1, 2):
        got[(-step) % NY, 0] = to_y(own, step)
    got[0, 1] = to_core(own)
    for dy in (1, 3, 2):
        got[dy, 1] = to_core(got[dy, 0])
    return got


def load_body(source, out, sem):
    copy = pltpu.make_async_copy(source, out, sem)
    copy.start()
    copy.wait()


def collect_body(*refs):
    blocks, out = refs[:-1], refs[-1]
    for k, block in enumerate(blocks):
        for half in range(2):
            out[2 * k + half] = block[half * TILE : (half + 1) * TILE]


def place(ref, total, first, dtype):
    for half in range(2):
        ref[half * TILE : (half + 1) * TILE] = total[2 * first + half].astype(dtype)


def add_tiles(group, starts, order, to_slot, product, total, dummy):
    first, last = starts[group], starts[group + 1]

    def batch(i, carry):
        slots = [first + i * UNROLL + u for u in range(UNROLL)]
        safe = [jnp.minimum(t, 191) for t in slots]
        terms = [product(order[t], t) for t in safe]
        for slot, t, term in zip(slots, safe, terms):
            place_at = jnp.where(slot < last, to_slot(t), dummy)
            total[place_at] = total[place_at] + term
        return carry

    lax.fori_loop(0, (last - first + UNROLL - 1) // UNROLL, batch, 0)


def forward_body(group, starts, order, rows, cols, vals, source, *rest):
    outs, total = rest[:-1], rest[-1]
    total[...] = jnp.zeros_like(total)
    add_tiles(
        group,
        starts,
        order,
        lambda t: jnp.clip(rows[t] - 8 * group, 0, 7),
        lambda tile, t: jnp.dot(vals[tile], source[cols[t]], preferred_element_type=F32),
        total,
        8,
    )
    if group == 3:
        far, over, kept = outs
        place(far, total, 3, BF16)
        place(over.at[0], total, 0, BF16)
        place(over.at[1], total, 1, BF16)
        place(kept, total, 2, F32)
    elif group:
        over, kept = outs
        for n in range(2):
            place(over.at[n], total, n, BF16)
            place(kept.at[n], total, 2 + n, F32)
    else:
        own, over, kept = outs
        place(own, total, 0, F32)
        place(over, total, 1, BF16)
        for n in range(2):
            place(kept.at[n], total, 2 + n, F32)


def wide(ref):
    return ref[...].astype(F32)


def split_body(kept, got, low, high):
    total = (kept[...] + wide(got)).astype(BF16)
    low[...] = total[0:TILE]
    high[...] = total[TILE : 2 * TILE]


def relay_half_body(kept, over, up, down, up_out, down_out):
    top, rest = slice(0, TILE), slice(TILE, 2 * TILE)
    up_out[top] = (kept[0, top] + wide(over.at[0, top]) + wide(up)).astype(BF16)
    up_out[rest] = (kept[0, rest] + wide(over.at[0, rest])).astype(BF16)
    down_out[top] = (kept[1, top] + wide(over.at[1, top])).astype(BF16)
    down_out[rest] = (kept[1, rest] + wide(over.at[1, rest]) + wide(down)).astype(BF16)


def relay_body(kept, over, up, down, up_out, down_out):
    up_out[...] = (kept[0] + wide(over.at[0]) + wide(up)).astype(BF16)
    down_out[...] = (kept[1] + wide(over.at[1]) + wide(down)).astype(BF16)


def activate_body(own, over, up, down, weight, bias, given, hidden, grad, message):
    summed = own[...] + wide(over) + wide(up) + wide(down)
    top = summed.astype(BF16)
    rest = (summed - top.astype(F32)).astype(BF16)
    pre_act = (
        jnp.dot(top, weight[...], preferred_element_type=F32)
        + jnp.dot(rest, weight[...], preferred_element_type=F32)
        + bias[...]
    )
    gate_value = jax.nn.sigmoid(pre_act)
    hidden[...] = (pre_act * gate_value).astype(BF16)
    slope = gate_value * (1.0 + pre_act * (1.0 - gate_value))
    result = (given[...].astype(F32) * slope).astype(BF16)
    grad[...] = result
    message[0:256] = result
    message[256:512] = top


def terms_body(z, *refs):
    own, ups, downs, far_grad, far_sum, out, grads, sums = (
        refs[0],
        refs[1:4],
        refs[4:7],
        refs[7],
        refs[8],
        refs[9],
        refs[10],
        refs[11],
    )
    blocks = {0: own, 7: ups[0], 6: ups[1], 5: ups[2], 1: downs[0], 2: downs[1], 3: downs[2]}
    for dz in range(NZ):
        at = (z[0] + dz) % NZ
        if dz == 4:
            grads[at] = far_grad[...]
            sums[at] = far_sum[...]
        else:
            grads[at] = blocks[dz][0:256]
            sums[at] = blocks[dz][256:512]
    total = jnp.zeros((256, 256), F32)
    column = jnp.zeros((1, 256), F32)
    for k in range(NZ):
        total = total + lax.dot_general(
            sums[k], grads[k], (((0,), (0,)), ((), ())), preferred_element_type=F32
        )
        column = column + jnp.sum(grads[k].astype(F32), axis=0, keepdims=True)
    out[0:256] = total
    out[256:264] = jnp.broadcast_to(column, (8, 256))


def backward_body(group, starts, order, rows, cols, vals, *rest):
    count = 4 if group == 0 else 3 if group < 3 else 3
    blocks, rest = rest[:count], rest[count:]
    if group:
        before, rest = rest[0], rest[1:]
    if group == 3:
        own, kept, over, source, total = rest
    else:
        total, source = rest
    n = 0
    for block, size in zip(blocks, (1, 1, 1, 1) if group == 0 else (2, 1, 1)):
        for half in range(2 * size):
            source[n] = block[half * TILE : (half + 1) * TILE]
            n += 1
    if group:
        total[...] = before[...]
    else:
        total[...] = jnp.zeros_like(total)
    add_tiles(
        group,
        starts,
        order,
        lambda t: cols[t],
        lambda tile, t: lax.dot_general(
            vals[tile],
            source[jnp.clip(rows[t] - 8 * group, 0, 7)],
            (((0,), (0,)), ((), ())),
            preferred_element_type=F32,
        ),
        total,
        16,
    )
    if group == 3:
        place(own, total, 0, F32)
        for k, dy in enumerate((1, 2, 3)):
            place(kept.at[k], total, 2 * dy, F32)
            place(over.at[k], total, 2 * dy + 1, BF16)
        place(over.at[3], total, 1, BF16)


def back_relay_body(kept, over, mine, other, out_a, out_b, out_c, own_terms):
    terms = (mine[...] + other[...]).astype(BF16)
    own_terms[0:256] = terms[0:256]
    own_terms[256:272] = jnp.broadcast_to(terms[256:257], (16, 256))
    for k, out in enumerate((out_a, out_b, out_c)):
        out[0:256] = (kept[k] + over[k].astype(F32)).astype(BF16)
        out[256:512] = terms[0:256]
        out[512:528] = jnp.broadcast_to(terms[256:257], (16, 256))


def finish_body(scale, own, over, a, b, c, terms, weight, out, grad_weight, grad_bias):
    back = own[...] + over[3].astype(F32)
    for ref in (a, b, c):
        back = back + ref[0:256].astype(F32)
    out[...] = lax.dot_general(
        back.astype(BF16), weight[...], (((1,), (1,)), ((), ())), preferred_element_type=F32
    ).astype(BF16)
    total = (wide(terms) + b[256:528].astype(F32)) + (
        a[256:528].astype(F32) + c[256:528].astype(F32)
    )
    grad_weight[...] = total[0:256] * scale
    grad_bias[...] = total[256:264] * scale


def per_device(feats, weight, bias, grad_out, tile_vals, tile_rows, tile_cols, tile_count):
    shard = feats.shape[0]
    scale = 1.0 / math.sqrt(shard * 2 * NY * 2 * NZ)
    row, col = lax.axis_index("row"), lax.axis_index("col")
    y, core, z, x = row // 2, row % 2, col // 2, col % 2
    owner_row, owner_col = tile_rows[0, 0] // 2, tile_cols[0, 0] // 2
    where = (owner_row // 2 - z) % NZ * 2 + (owner_row + x) % 2
    ranks = [0] * (2 * NZ)
    for rank, (dz, dx) in enumerate(sum(ORDER, ())):
        ranks[dz * 2 + dx] = rank
    rank = sum(jnp.where(where == k, r, 0) for k, r in enumerate(ranks))
    rows = rank * 2 + tile_rows[0, 0] % 2
    rel_y = (owner_col // 2 - y) % NY
    cols = (rel_y * 2 + (owner_col + core) % 2) * 2 + tile_cols[0, 0] % 2
    slots = jnp.arange(rows.shape[0], dtype=jnp.int32)
    live = slots < tile_count[0, 0]
    key = jnp.where(live, rank // 4, 4) * rows.shape[0] + slots
    position = jnp.sum((key[None, :] < key[:, None]).astype(jnp.int32), axis=1)
    chosen = position[None, :] == slots[:, None]
    order, rows, cols = (
        jnp.sum(jnp.where(chosen, a[None, :], 0), axis=1) for a in (slots, rows, cols)
    )
    groups = jnp.arange(8, dtype=jnp.int32)
    starts = jnp.sum((key[None, :] < groups[:, None] * rows.shape[0]).astype(jnp.int32), axis=1)
    plan = (starts, order, rows, cols)

    tiles = tile_vals[0, 0]
    vals = call(
        load_body,
        "load_tiles",
        jax.ShapeDtypeStruct(tiles.shape, BF16),
        (tiles,),
        scratch=(pltpu.SemaphoreType.DMA,),
        moved=2 * tiles.size * 2,
        specs=[pl.BlockSpec(memory_space=pl.ANY)],
    )
    gathered = gather_row(feats)
    source = call(
        collect_body,
        "collect",
        jax.ShapeDtypeStruct((16, TILE, 256), BF16),
        tuple(gathered[k // 2, k % 2] for k in range(8)),
        moved=2**21,
    )
    work = 2 * 48 * TILE * TILE * 256

    one, two = shape(shard, F32), jax.ShapeDtypeStruct((2, shard, 256), F32)
    one16, two16 = shape(shard, BF16), jax.ShapeDtypeStruct((2, shard, 256), BF16)

    def forward(group, outs):
        return call(
            functools.partial(forward_body, group),
            f"forward_{group}",
            outs,
            (*plan, vals, source),
            scalars=4,
            scratch=(pltpu.VMEM((9, TILE, 256), F32),),
            flops=work,
            moved=4 * 2**20,
        )

    far, over3, kept4 = forward(3, (one16, two16, one))
    far, over3 = to_x(far), to_x(over3)
    over2, kept3 = forward(2, (two16, two))
    low, high = call(
        split_body, "split", (shape(TILE, BF16), shape(TILE, BF16)), (kept4, far), moved=2**19
    )
    over2 = to_x(over2)
    up, down = to_z(low, 1), to_z(high, -1)
    over1, kept2 = forward(1, (two16, two))
    over1 = to_x(over1)
    up, down = call(
        relay_half_body, "relay_3", (one16, one16), (kept3, over3, up, down), moved=2**20
    )
    up, down = to_z(up, 1), to_z(down, -1)
    own, over0, kept1 = forward(0, (one, one16, two))
    over0 = to_x(over0)
    up, down = call(relay_body, "relay_2", (one16, one16), (kept2, over2, up, down), moved=2**20)
    up, down = to_z(up, 1), to_z(down, -1)
    up, down = call(relay_body, "relay_1", (one16, one16), (kept1, over1, up, down), moved=2**20)
    up, down = to_z(up, 1), to_z(down, -1)
    hidden_out, grad, message = call(
        activate_body,
        "activate",
        (one16, one16, shape(2 * shard, BF16)),
        (own, over0, up, down, weight, bias[None, :], grad_out),
        flops=4 * 256**3,
        moved=2 * 2**20,
    )

    def backward(group, blocks, before, outs):
        return call(
            functools.partial(backward_body, group),
            f"backward_{group}",
            outs,
            (*plan, vals, *blocks, *before),
            scalars=4,
            scratch=(pltpu.VMEM((8, TILE, 256), BF16),)
            + ((pltpu.VMEM((17, TILE, 256), F32),) if group == 3 else ()),
            flops=work,
            moved=6 * 2**20,
        )

    running = jax.ShapeDtypeStruct((17, TILE, 256), F32)
    over = to_x(grad)
    up, down = to_z(message, 1), to_z(message, -1)
    ups, downs = [up], [down]
    blocks, before = (grad, over, down, up), ()
    for group in (0, 1, 2):
        over = to_x(jnp.concatenate([downs[-1][:shard], ups[-1][:shard]]))
        if group < 2:
            up, down = to_z(ups[-1], 1), to_z(downs[-1], -1)
        else:
            up, down = to_z(ups[-1][:shard], 1), to_z(downs[-1][shard:], -1)
        total = backward(group, blocks, before, running)
        up, down, total = lax.optimization_barrier((up, down, total))
        ups.append(up)
        downs.append(down)
        blocks, before = (over, down, up), (total,)
    far_grad, far_sum = ups.pop(), downs.pop()
    far_over = to_x(far_grad)
    terms = call(
        terms_body,
        "weight_terms",
        shape(264, F32),
        (z[None], message, *ups, *downs, far_grad, far_sum),
        scalars=1,
        scratch=(pltpu.VMEM((NZ, 256, 256), BF16), pltpu.VMEM((NZ, 256, 256), BF16)),
        flops=2 * 2048 * 256 * 256,
        moved=4 * 2**20,
    )
    terms = terms + to_x(terms)
    own, kept, over = backward(
        3,
        (over, far_grad, far_over),
        (total,),
        (
            one,
            jax.ShapeDtypeStruct((3, shard, 256), F32),
            jax.ShapeDtypeStruct((4, shard, 256), BF16),
        ),
    )
    over, other = to_core(over), to_core(terms)
    *sends, terms = call(
        back_relay_body,
        "back_relay",
        (*[shape(528, BF16)] * 3, shape(272, BF16)),
        (kept, over, terms, other),
        moved=2 * 2**20,
    )
    got = [to_y(a, s) for a, s in zip(sends, (1, 2, 3))]
    grad_feats, grad_weight, grad_bias = call(
        functools.partial(finish_body, scale),
        "finish",
        (one16, shape(256, F32), shape(8, F32)),
        (own, over, *got, terms, weight),
        flops=2 * 256**3,
        moved=2 * 2**20,
    )
    return (hidden_out, grad_feats, grad_weight, grad_bias[0])


def solution(mesh):
    in_specs = (
        P(("slab", "col", "row"), None),
        P(),
        P(),
        P(("slab", "row", "col"), None),
        P(("slab", "row"), "col", None, None, None),
        P(("slab", "row"), "col", None),
        P(("slab", "row"), "col", None),
        P(("slab", "row"), "col"),
    )
    out_specs = (
        P(("slab", "row", "col"), None),
        P(("slab", "col", "row"), None),
        P("slab", None),
        P("slab"),
    )
    return jax.shard_map(
        per_device, mesh=mesh, in_specs=in_specs, out_specs=out_specs, check_vma=False
    )
```

```python
import functools
import math

import jax
import jax.numpy as jnp
from jax import lax
from jax.experimental import pallas as pl
from jax.experimental.pallas import tpu as pltpu
from jax.sharding import PartitionSpec as P

TILE = 128
UNROLL = 16
ORDER = (
    ((0, 0), (0, 1)),
    ((1, 1), (7, 1), (1, 0), (7, 0)),
    ((2, 1), (6, 1), (2, 0), (6, 0)),
    ((3, 1), (5, 1), (3, 0), (5, 0)),
    ((4, 0), (4, 1)),
)
FIRST = (0, 2, 6, 10, 14)
LAST = 4
NY = 4
NZ = 8
F32 = jnp.float32
BF16 = jnp.bfloat16
LIMIT = pltpu.CompilerParams(vmem_limit_bytes=32 * 2**20)


def vmem():
    return pl.BlockSpec(memory_space=pltpu.VMEM)


def smem():
    return pl.BlockSpec(memory_space=pltpu.SMEM)


def shape(rows, dtype):
    return jax.ShapeDtypeStruct((rows, 256), dtype)


def call(body, name, out_shape, args, scalars=0, scratch=(), flops=0, moved=0, specs=None):
    return pl.pallas_call(
        body,
        name=name,
        out_shape=out_shape,
        in_specs=specs or [smem()] * scalars + [vmem()] * (len(args) - scalars),
        out_specs=jax.tree.map(lambda _: vmem(), out_shape),
        scratch_shapes=scratch,
        compiler_params=LIMIT,
        cost_estimate=pl.CostEstimate(flops=flops, bytes_accessed=moved, transcendentals=0),
    )(*args)


def to_core(a):
    return lax.ppermute(a, "row", [(i, i ^ 1) for i in range(2 * NY)])


def to_y(a, step):
    return lax.ppermute(a, "row", [(i, (i + 2 * step) % (2 * NY)) for i in range(2 * NY)])


def to_x(a):
    return lax.ppermute(a, "col", [(i, i ^ 1) for i in range(2 * NZ)])


def to_z(a, step):
    return lax.ppermute(a, "col", [(i, (i + 2 * step) % (2 * NZ)) for i in range(2 * NZ)])


def load_body(source, out, sem):
    copy = pltpu.make_async_copy(source, out, sem)
    copy.start()
    copy.wait()


def collect_body(*refs):
    blocks, out = refs[:-1], refs[-1]
    for k, block in enumerate(blocks):
        for half in range(2):
            out[2 * k + half] = block[half * TILE : (half + 1) * TILE]


def place(ref, total, first, dtype):
    for half in range(2):
        ref[half * TILE : (half + 1) * TILE] = total[2 * first + half].astype(dtype)


def add_tiles(group, starts, order, to_slot, product, total, dummy):
    first, last = starts[group], starts[group + 1]

    def batch(i, carry):
        slots = [first + i * UNROLL + u for u in range(UNROLL)]
        safe = [jnp.minimum(t, 191) for t in slots]
        terms = [product(order[t], t) for t in safe]
        for slot, t, term in zip(slots, safe, terms):
            place_at = jnp.where(slot < last, to_slot(t), dummy)
            total[place_at] = total[place_at] + term
        return carry

    lax.fori_loop(0, (last - first + UNROLL - 1) // UNROLL, batch, 0)


def forward_body(group, starts, order, rows, cols, vals, source, *rest):
    outs, total = rest[:-1], rest[-1]
    size = 2 * len(ORDER[group])
    total[...] = jnp.zeros_like(total)
    add_tiles(
        group,
        starts,
        order,
        lambda t: jnp.clip(rows[t] - 2 * FIRST[group], 0, size - 1),
        lambda tile, t: jnp.dot(vals[tile], source[cols[t]], preferred_element_type=F32),
        total,
        size,
    )
    if group in (0, LAST):
        kept, over = outs
        place(kept, total, 0, F32)
        place(over, total, 1, BF16)
    else:
        over, kept = outs
        for n in range(2):
            place(over.at[n], total, n, BF16)
            place(kept.at[n], total, 2 + n, F32)


def wide(ref):
    return ref[...].astype(F32)


def split_body(kept, got, low, high):
    total = (kept[...] + wide(got)).astype(BF16)
    low[...] = total[0:TILE]
    high[...] = total[TILE : 2 * TILE]


def relay_half_body(kept, over, up, down, up_out, down_out):
    top, rest = slice(0, TILE), slice(TILE, 2 * TILE)
    up_out[top] = (kept[0, top] + wide(over.at[0, top]) + wide(up)).astype(BF16)
    up_out[rest] = (kept[0, rest] + wide(over.at[0, rest])).astype(BF16)
    down_out[top] = (kept[1, top] + wide(over.at[1, top])).astype(BF16)
    down_out[rest] = (kept[1, rest] + wide(over.at[1, rest]) + wide(down)).astype(BF16)


def relay_body(kept, over, up, down, up_out, down_out):
    up_out[...] = (kept[0] + wide(over.at[0]) + wide(up)).astype(BF16)
    down_out[...] = (kept[1] + wide(over.at[1]) + wide(down)).astype(BF16)


def activate_body(own, over, up, down, weight, bias, given, hidden, grad, message):
    summed = own[...] + wide(over) + wide(up) + wide(down)
    top = summed.astype(BF16)
    rest = (summed - top.astype(F32)).astype(BF16)
    pre_act = (
        jnp.dot(top, weight[...], preferred_element_type=F32)
        + jnp.dot(rest, weight[...], preferred_element_type=F32)
        + bias[...]
    )
    gate_value = jax.nn.sigmoid(pre_act)
    hidden[...] = (pre_act * gate_value).astype(BF16)
    slope = gate_value * (1.0 + pre_act * (1.0 - gate_value))
    result = (given[...].astype(F32) * slope).astype(BF16)
    grad[...] = result
    message[0:256] = result
    message[256:512] = top


def terms_body(z, *refs):
    own, ups, downs, far_grad, far_sum, out, grads, sums = (
        refs[0],
        refs[1:4],
        refs[4:7],
        refs[7],
        refs[8],
        refs[9],
        refs[10],
        refs[11],
    )
    blocks = {0: own, 7: ups[0], 6: ups[1], 5: ups[2], 1: downs[0], 2: downs[1], 3: downs[2]}
    for dz in range(NZ):
        at = (z[0] + dz) % NZ
        if dz == 4:
            grads[at] = far_grad[...]
            sums[at] = far_sum[...]
        else:
            grads[at] = blocks[dz][0:256]
            sums[at] = blocks[dz][256:512]
    total = jnp.zeros((256, 256), F32)
    column = jnp.zeros((1, 256), F32)
    for k in range(NZ):
        total = total + lax.dot_general(
            sums[k], grads[k], (((0,), (0,)), ((), ())), preferred_element_type=F32
        )
        column = column + jnp.sum(grads[k].astype(F32), axis=0, keepdims=True)
    out[0:256] = total.astype(BF16)
    out[256:272] = jnp.broadcast_to(column.astype(BF16), (16, 256))


def backward_body(group, starts, order, rows, cols, vals, *rest):
    sizes = (1, 1) if group in (0, LAST) else (2, 1, 1)
    blocks, rest = rest[: len(sizes)], rest[len(sizes) :]
    if group:
        before, rest = rest[0], rest[1:]
    if group == LAST:
        own, kept, over, source, total = rest
    else:
        total, source = rest
    n = 0
    for block, size in zip(blocks, sizes):
        for half in range(2 * size):
            source[n] = block[half * TILE : (half + 1) * TILE]
            n += 1
    if group:
        total[...] = before[...]
    else:
        total[...] = jnp.zeros_like(total)
    add_tiles(
        group,
        starts,
        order,
        lambda t: cols[t],
        lambda tile, t: lax.dot_general(
            vals[tile],
            source[jnp.clip(rows[t] - 2 * FIRST[group], 0, n - 1)],
            (((0,), (0,)), ((), ())),
            preferred_element_type=F32,
        ),
        total,
        16,
    )
    if group == LAST:
        place(own, total, 0, F32)
        for k, dy in enumerate((1, 2, 3)):
            place(kept.at[k], total, 2 * dy, F32)
            place(over.at[k], total, 2 * dy + 1, BF16)
        place(over.at[3], total, 1, BF16)


def back_relay_body(kept, over, out_a, out_b, out_c):
    for k, out in enumerate((out_a, out_b, out_c)):
        out[...] = (kept[k] + over[k].astype(F32)).astype(BF16)


def sum_terms_body(own, a, b, c, out):
    out[...] = (wide(own) + wide(b)) + (wide(a) + wide(c))


def finish_body(scale, own, over, a, b, c, mine, other, weight, out, grad_weight, grad_bias):
    back = own[...] + over[3].astype(F32) + wide(a) + wide(b) + wide(c)
    out[...] = lax.dot_general(
        back.astype(BF16), weight[...], (((1,), (1,)), ((), ())), preferred_element_type=F32
    ).astype(BF16)
    total = mine[...] + other[...]
    grad_weight[...] = total[0:256] * scale
    grad_bias[...] = total[256:257] * scale


def per_device(feats, weight, bias, grad_out, tile_vals, tile_rows, tile_cols, tile_count):
    shard = feats.shape[0]
    scale = 1.0 / math.sqrt(shard * 2 * NY * 2 * NZ)
    row, col = lax.axis_index("row"), lax.axis_index("col")
    y, core, z, x = row // 2, row % 2, col // 2, col % 2
    owner_row, owner_col = tile_rows[0, 0] // 2, tile_cols[0, 0] // 2
    where = (owner_row // 2 - z) % NZ * 2 + (owner_row + x) % 2
    ranks = [0] * (2 * NZ)
    for rank, (dz, dx) in enumerate(sum(ORDER, ())):
        ranks[dz * 2 + dx] = rank
    rank = sum(jnp.where(where == k, r, 0) for k, r in enumerate(ranks))
    group = sum((rank >= f).astype(jnp.int32) for f in FIRST[1:])
    rows = rank * 2 + tile_rows[0, 0] % 2
    rel_y = (owner_col // 2 - y) % NY
    cols = (rel_y * 2 + (owner_col + core) % 2) * 2 + tile_cols[0, 0] % 2
    slots = jnp.arange(rows.shape[0], dtype=jnp.int32)
    live = slots < tile_count[0, 0]
    key = jnp.where(live, group, LAST + 1) * rows.shape[0] + slots
    position = jnp.sum((key[None, :] < key[:, None]).astype(jnp.int32), axis=1)
    chosen = position[None, :] == slots[:, None]
    order, rows, cols = (
        jnp.sum(jnp.where(chosen, a[None, :], 0), axis=1) for a in (slots, rows, cols)
    )
    groups = jnp.arange(8, dtype=jnp.int32)
    starts = jnp.sum((key[None, :] < groups[:, None] * rows.shape[0]).astype(jnp.int32), axis=1)
    plan = (starts, order, rows, cols)

    tiles = tile_vals[0, 0]
    vals = call(
        load_body,
        "load_tiles",
        jax.ShapeDtypeStruct(tiles.shape, BF16),
        (tiles,),
        scratch=(pltpu.SemaphoreType.DMA,),
        moved=2 * tiles.size * 2,
        specs=[pl.BlockSpec(memory_space=pltpu.HBM)],
    )
    gathered = {(0, 0): feats, (0, 1): to_core(feats)}
    steps = (1, -1, 2)
    arrived = [to_y(feats, step) for step in steps]
    arrived, vals, plan = lax.optimization_barrier((arrived, vals, plan))
    for step, block in zip(steps, arrived):
        gathered[(-step) % NY, 0] = block
        gathered[(-step) % NY, 1] = to_core(block)
    source = call(
        collect_body,
        "collect",
        jax.ShapeDtypeStruct((16, TILE, 256), BF16),
        tuple(gathered[k // 2, k % 2] for k in range(8)),
        moved=2**21,
    )
    work = 2 * 48 * TILE * TILE * 256

    one, two = shape(shard, F32), jax.ShapeDtypeStruct((2, shard, 256), F32)
    one16, two16 = shape(shard, BF16), jax.ShapeDtypeStruct((2, shard, 256), BF16)

    def forward(group, outs, source):
        return call(
            functools.partial(forward_body, group),
            f"forward_{group}",
            outs,
            (*plan, vals, source),
            scalars=4,
            scratch=(pltpu.VMEM((2 * len(ORDER[group]) + 1, TILE, 256), F32),),
            flops=0,
            moved=0,
        )

    kept4, far = forward(4, (one, one16), source)
    far, kept4, source = lax.optimization_barrier((far, kept4, source))
    far = to_x(far)
    over3, kept3 = forward(3, (two16, two), source)
    over3 = to_x(over3)
    low, high = call(
        split_body, "split", (shape(TILE, BF16), shape(TILE, BF16)), (kept4, far), moved=2**19
    )
    up, down = to_z(low, 1), to_z(high, -1)
    low, source = lax.optimization_barrier((low, source))
    over2, kept2 = forward(2, (two16, two), source)
    over2, up, down = lax.optimization_barrier((over2, up, down))
    over2 = to_x(over2)
    up, down = call(
        relay_half_body, "relay_3", (one16, one16), (kept3, over3, up, down), moved=2**20
    )
    up, down = to_z(up, 1), to_z(down, -1)
    over1, kept1 = forward(1, (two16, two), source)
    over1 = to_x(over1)
    up, down = call(relay_body, "relay_2", (one16, one16), (kept2, over2, up, down), moved=2**20)
    up, down = to_z(up, 1), to_z(down, -1)
    own, over0 = forward(0, (one, one16), source)
    over0 = to_x(over0)
    up, down = call(relay_body, "relay_1", (one16, one16), (kept1, over1, up, down), moved=2**20)
    up, down = to_z(up, 1), to_z(down, -1)
    hidden_out, grad, message = call(
        activate_body,
        "activate",
        (one16, one16, shape(2 * shard, BF16)),
        (own, over0, up, down, weight, bias[None, :], grad_out),
        flops=4 * 256**3,
        moved=2 * 2**20,
    )

    def backward(group, blocks, before, outs):
        return call(
            functools.partial(backward_body, group),
            f"backward_{group}",
            outs,
            (*plan, vals, *blocks, *before),
            scalars=4,
            scratch=(pltpu.VMEM((8, TILE, 256), BF16),)
            + ((pltpu.VMEM((17, TILE, 256), F32),) if group == LAST else ()),
            flops=0,
            moved=0,
        )

    running = jax.ShapeDtypeStruct((17, TILE, 256), F32)
    over = to_x(grad)
    up, down = to_z(message, 1), to_z(message, -1)
    up, down, over = lax.optimization_barrier((up, down, over))
    ups, downs = [up], [down]
    blocks, before = (grad, over), ()
    for group in (0, 1, 2):
        over = to_x(jnp.concatenate([downs[-1][:shard], ups[-1][:shard]]))
        if group < 2:
            up, down = to_z(ups[-1], 1), to_z(downs[-1], -1)
        else:
            up, down = to_z(ups[-1][:shard], 1), to_z(downs[-1][shard:], -1)
        total = backward(group, blocks, before, running)
        up, down, total = lax.optimization_barrier((up, down, total))
        blocks, before = (over, downs[-1], ups[-1]), (total,)
        ups.append(up)
        downs.append(down)
    far_grad, far_sum = ups.pop(), downs.pop()
    far_over = to_x(far_grad)
    total = backward(3, blocks, before, running)
    total, far_sum = lax.optimization_barrier((total, far_sum))
    terms = call(
        terms_body,
        "weight_terms",
        shape(272, BF16),
        (z[None], message, *ups, *downs, far_grad, far_sum),
        scalars=1,
        scratch=(pltpu.VMEM((NZ, 256, 256), BF16), pltpu.VMEM((NZ, 256, 256), BF16)),
        flops=2 * 2048 * 256 * 256,
        moved=0,
    )
    moved_terms = [to_y(terms, s) for s in (1, 2, 3)]
    terms = call(
        sum_terms_body, "sum_terms", shape(272, F32), (terms, *moved_terms), moved=2**20
    )
    own, kept, over = backward(
        4,
        (far_grad, far_over),
        (total,),
        (
            one,
            jax.ShapeDtypeStruct((3, shard, 256), F32),
            jax.ShapeDtypeStruct((4, shard, 256), BF16),
        ),
    )
    over = to_core(over)
    across = to_x(terms)
    sends = call(
        back_relay_body, "back_relay", (one16, one16, one16), (kept, over), moved=2 * 2**20
    )
    got = [to_y(a, s) for a, s in zip(sends, (1, 2, 3))]
    across, _ = lax.optimization_barrier((across, sends[0]))
    terms = terms + across
    other = to_core(terms)
    grad_feats, grad_weight, grad_bias = call(
        functools.partial(finish_body, scale),
        "finish",
        (one16, shape(256, F32), shape(1, F32)),
        (own, over, *got, terms, other, weight),
        flops=2 * 256**3,
        moved=2 * 2**20,
    )
    return (hidden_out, grad_feats, grad_weight, grad_bias.reshape(256))


def solution(mesh):
    in_specs = (
        P(("slab", "col", "row"), None),
        P(),
        P(),
        P(("slab", "row", "col"), None),
        P(("slab", "row"), "col", None, None, None),
        P(("slab", "row"), "col", None),
        P(("slab", "row"), "col", None),
        P(("slab", "row"), "col"),
    )
    out_specs = (
        P(("slab", "row", "col"), None),
        P(("slab", "col", "row"), None),
        P("slab", None),
        P("slab"),
    )
    return jax.shard_map(
        per_device, mesh=mesh, in_specs=in_specs, out_specs=out_specs, check_vma=False
    )
```

```python
import functools
import math

import jax
import jax.numpy as jnp
from jax import lax
from jax.experimental import pallas as pl
from jax.experimental.pallas import tpu as pltpu
from jax.sharding import PartitionSpec as P

TILE = 128
UNROLL = 16
ORDER = (
    ((0, 0), (1, 0)),
    ((7, 0), (6, 0), (0, 1), (1, 1)),
    ((2, 0), (3, 0), (7, 1), (6, 1)),
    ((5, 0), (4, 0), (2, 1), (3, 1)),
    ((5, 1), (4, 1)),
)
FIRST = (0, 2, 6, 10, 14)
LAST = 4
NY = 4
NZ = 8
F32 = jnp.float32
BF16 = jnp.bfloat16
LIMIT = pltpu.CompilerParams(vmem_limit_bytes=32 * 2**20)


def vmem():
    return pl.BlockSpec(memory_space=pltpu.VMEM)


def smem():
    return pl.BlockSpec(memory_space=pltpu.SMEM)


def shape(rows, dtype):
    return jax.ShapeDtypeStruct((rows, 256), dtype)


def call(body, name, out_shape, args, scalars=0, scratch=(), flops=0, moved=0, specs=None):
    return pl.pallas_call(
        body,
        name=name,
        out_shape=out_shape,
        in_specs=specs or [smem()] * scalars + [vmem()] * (len(args) - scalars),
        out_specs=jax.tree.map(lambda _: vmem(), out_shape),
        scratch_shapes=scratch,
        compiler_params=LIMIT,
        cost_estimate=pl.CostEstimate(flops=flops, bytes_accessed=moved, transcendentals=0),
    )(*args)


def to_core(a):
    return lax.ppermute(a, "row", [(i, i ^ 1) for i in range(2 * NY)])


def to_y(a, step):
    return lax.ppermute(a, "row", [(i, (i + 2 * step) % (2 * NY)) for i in range(2 * NY)])


def to_x(a):
    return lax.ppermute(a, "col", [(i, i ^ 1) for i in range(2 * NZ)])


def swap_z(a, side):
    pairs = []
    for row in range(2 * NY):
        for col in range(2 * NZ):
            z, x = divmod(col, 2)
            step = side if (z + row) % 2 == 0 else -side
            pairs.append((row * 2 * NZ + col, row * 2 * NZ + (z + step) % NZ * 2 + x))
    return lax.ppermute(a, ("row", "col"), pairs)


def flip_z(a, bit):
    return lax.ppermute(a, "col", [(i, i ^ (2 * bit)) for i in range(2 * NZ)])


def load_body(source, out, sem):
    copy = pltpu.make_async_copy(source, out, sem)
    copy.start()
    copy.wait()


def collect_body(*refs):
    blocks, out = refs[:-1], refs[-1]
    for k, block in enumerate(blocks):
        for half in range(2):
            out[2 * k + half] = block[half * TILE : (half + 1) * TILE]


def place(ref, total, first, dtype):
    for half in range(2):
        ref[half * TILE : (half + 1) * TILE] = total[2 * first + half].astype(dtype)


def add_tiles(group, starts, order, to_slot, product, total, dummy):
    first, last = starts[group], starts[group + 1]

    def batch(i, carry):
        slots = [first + i * UNROLL + u for u in range(UNROLL)]
        safe = [jnp.minimum(t, 191) for t in slots]
        terms = [product(order[t], t) for t in safe]
        for slot, t, term in zip(slots, safe, terms):
            place_at = jnp.where(slot < last, to_slot(t), dummy)
            total[place_at] = total[place_at] + term
        return carry

    lax.fori_loop(0, (last - first + UNROLL - 1) // UNROLL, batch, 0)


def forward_body(group, starts, order, rows, cols, vals, source, *rest):
    outs, total = rest[:-1], rest[-1]
    size = 2 * len(ORDER[group])
    total[...] = jnp.zeros_like(total)
    add_tiles(
        group,
        starts,
        order,
        lambda t: jnp.clip(rows[t] - 2 * FIRST[group], 0, size - 1),
        lambda tile, t: jnp.dot(vals[tile], source[cols[t]], preferred_element_type=F32),
        total,
        size,
    )
    outs = list(outs)
    if group < LAST:
        kept = outs.pop(0)
        for n in range(2):
            place(kept.at[n], total, n, F32)
    if group:
        over = outs.pop(0)
        for n in range(2):
            place(over.at[n], total, size // 2 - 2 + n, BF16)


def wide(ref):
    return ref[...].astype(F32)


def relay_first_body(kept, over, out):
    out[...] = (kept[...] + wide(over)).astype(BF16)


def relay_body(kept, over, got, out):
    out[...] = (kept[...] + wide(over) + wide(got)).astype(BF16)


def relay_last_body(kept, over, got, own, out):
    own[...] = kept[0] + wide(over.at[0]) + wide(got.at[0])
    out[...] = (kept[1] + wide(over.at[1]) + wide(got.at[1])).astype(BF16)


def activate_body(own, got, weight, bias, given, hidden, grad, high, low):
    summed = own[...] + wide(got)
    top = summed.astype(BF16)
    rest = (summed - top.astype(F32)).astype(BF16)
    high[...] = top
    low[...] = rest
    pre_act = (
        jnp.dot(top, weight[...], preferred_element_type=F32)
        + jnp.dot(rest, weight[...], preferred_element_type=F32)
        + bias[...]
    )
    gate_value = jax.nn.sigmoid(pre_act)
    hidden[...] = (pre_act * gate_value).astype(BF16)
    slope = gate_value * (1.0 + pre_act * (1.0 - gate_value))
    grad[...] = (given[...].astype(F32) * slope).astype(BF16)


def terms_body(core, high, low, grad, kept, sent, whole):
    g = grad[...]
    dims = (((0,), (0,)), ((), ()))
    whole[...] = lax.dot_general(high[...], g, dims, preferred_element_type=F32) + lax.dot_general(
        low[...], g, dims, preferred_element_type=F32
    )
    column = jnp.sum(g.astype(F32), axis=0, keepdims=True)
    for ref, half in ((kept, core[0]), (sent, 1 - core[0])):
        ref[0:128] = whole[pl.ds(pl.multiple_of(half * 128, 128), 128)]
        ref[128:136] = jnp.broadcast_to(column, (8, 256))


def backward_body(group, starts, order, rows, cols, vals, *rest):
    count = 1 if group in (0, LAST) else 2
    blocks, rest = rest[:count], rest[count:]
    if group:
        before, rest = rest[0], rest[1:]
    if group == LAST:
        own, kept, over, source, total = rest
    else:
        total, source = rest
    n = 0
    for block in blocks:
        for half in range(4):
            source[n] = block[half // 2, half % 2 * TILE : (half % 2 + 1) * TILE]
            n += 1
    if group:
        total[...] = before[...]
    else:
        total[...] = jnp.zeros_like(total)
    add_tiles(
        group,
        starts,
        order,
        lambda t: cols[t],
        lambda tile, t: lax.dot_general(
            vals[tile],
            source[jnp.clip(rows[t] - 2 * FIRST[group], 0, n - 1)],
            (((0,), (0,)), ((), ())),
            preferred_element_type=F32,
        ),
        total,
        16,
    )
    if group == LAST:
        place(own, total, 0, F32)
        for k, dy in enumerate((1, 2, 3)):
            place(kept.at[k], total, 2 * dy, F32)
            place(over.at[k], total, 2 * dy + 1, BF16)
        place(over.at[3], total, 1, BF16)


def back_relay_body(kept, over, terms, out_a, out_b, out_c, mine):
    mine[0:128] = terms[0:128].astype(BF16)
    mine[128:144] = jnp.broadcast_to(terms[128:129], (16, 256)).astype(BF16)
    for k, out in enumerate((out_a, out_b, out_c)):
        out[0:256] = (kept[k] + over[k].astype(F32)).astype(BF16)
        out[256:400] = mine[...]


def sum_terms_body(scale, own, a, b, c, out):
    total = (wide(own) + b[256:400].astype(F32)) + (
        a[256:400].astype(F32) + c[256:400].astype(F32)
    )
    out[...] = total[0:136] * scale


def finish_body(own, over, a, b, c, weight, out):
    back = own[...] + over[3].astype(F32)
    for ref in (a, b, c):
        back = back + ref[0:256].astype(F32)
    out[...] = lax.dot_general(
        back.astype(BF16), weight[...], (((1,), (1,)), ((), ())), preferred_element_type=F32
    ).astype(BF16)


def assemble_body(core, mine, other, weight, bias):
    for ref, half in ((mine, core[0]), (other, 1 - core[0])):
        weight[pl.ds(pl.multiple_of(half * 128, 128), 128)] = ref[0:128]
    bias[...] = mine[128:129]


def per_device(feats, weight, bias, grad_out, tile_vals, tile_rows, tile_cols, tile_count):
    shard = feats.shape[0]
    scale = 1.0 / math.sqrt(shard * 2 * NY * 2 * NZ)
    row, col = lax.axis_index("row"), lax.axis_index("col")
    y, core, z, x = row // 2, row % 2, col // 2, col % 2
    owner_row, owner_col = tile_rows[0, 0] // 2, tile_cols[0, 0] // 2
    toward = 1 - 2 * ((z + core) % 2)
    where = (owner_row // 2 - z) * toward % NZ * 2 + (owner_row + x) % 2
    ranks = [0] * (2 * NZ)
    for rank, (dz, dx) in enumerate(sum(ORDER, ())):
        ranks[dz * 2 + dx] = rank
    rank = sum(jnp.where(where == k, r, 0) for k, r in enumerate(ranks))
    group = sum((rank >= f).astype(jnp.int32) for f in FIRST[1:])
    rows = rank * 2 + tile_rows[0, 0] % 2
    rel_y = (owner_col // 2 - y) % NY
    cols = (rel_y * 2 + (owner_col + core) % 2) * 2 + tile_cols[0, 0] % 2
    slots = jnp.arange(rows.shape[0], dtype=jnp.int32)
    live = slots < tile_count[0, 0]
    key = jnp.where(live, group, LAST + 1) * rows.shape[0] + slots
    position = jnp.sum((key[None, :] < key[:, None]).astype(jnp.int32), axis=1)
    chosen = position[None, :] == slots[:, None]
    order, rows, cols = (
        jnp.sum(jnp.where(chosen, a[None, :], 0), axis=1) for a in (slots, rows, cols)
    )
    groups = jnp.arange(8, dtype=jnp.int32)
    starts = jnp.sum((key[None, :] < groups[:, None] * rows.shape[0]).astype(jnp.int32), axis=1)
    plan = (starts, order, rows, cols)

    tiles = tile_vals[0, 0]
    vals = call(
        load_body,
        "load_tiles",
        jax.ShapeDtypeStruct(tiles.shape, BF16),
        (tiles,),
        scratch=(pltpu.SemaphoreType.DMA,),
        moved=2 * tiles.size * 2,
        specs=[pl.BlockSpec(memory_space=pltpu.HBM)],
    )
    gathered = {(0, 0): feats, (0, 1): to_core(feats)}
    steps = (1, -1, 2)
    arrived = [to_y(feats, step) for step in steps]
    arrived, vals, plan = lax.optimization_barrier((arrived, vals, plan))
    for step, block in zip(steps, arrived):
        gathered[(-step) % NY, 0] = block
        gathered[(-step) % NY, 1] = to_core(block)
    source = call(
        collect_body,
        "collect",
        jax.ShapeDtypeStruct((16, TILE, 256), BF16),
        tuple(gathered[k // 2, k % 2] for k in range(8)),
        moved=2**21,
    )
    work = 2 * 48 * TILE * TILE * 256

    one, two = shape(shard, F32), jax.ShapeDtypeStruct((2, shard, 256), F32)
    one16, two16 = shape(shard, BF16), jax.ShapeDtypeStruct((2, shard, 256), BF16)
    half = shape(136, F32)

    def forward(group, outs, source):
        return call(
            functools.partial(forward_body, group),
            f"forward_{group}",
            outs,
            (*plan, vals, source),
            scalars=4,
            scratch=(pltpu.VMEM((2 * len(ORDER[group]) + 1, TILE, 256), F32),),
            flops=0,
            moved=0,
        )

    def relay(body, name, outs, *args):
        return call(body, name, outs, args, moved=2**20)

    (over_a,) = forward(4, (two16,), source)
    over_a, source = lax.optimization_barrier((over_a, source))
    over_a = to_x(over_a)
    kept_a, over_b = forward(3, (two, two16), source)
    over_b = to_x(over_b)
    moving = relay(relay_first_body, "relay_first", two16, kept_a, over_a)
    moving, source = lax.optimization_barrier((moving, source))
    moving = swap_z(moving, -1)
    kept_b, over_c = forward(2, (two, two16), source)
    over_c = to_x(over_c)
    moving = relay(relay_body, "relay_b", two16, kept_b, over_b, moving)
    moving, source = lax.optimization_barrier((moving, source))
    moving = swap_z(moving, 1)
    kept_c, over_d = forward(1, (two, two16), source)
    over_d = to_x(over_d)
    moving = relay(relay_body, "relay_c", two16, kept_c, over_c, moving)
    moving, source = lax.optimization_barrier((moving, source))
    moving = swap_z(moving, -1)
    (kept_d,) = forward(0, (two,), source)
    own, moving = relay(relay_last_body, "relay_last", (one, one16), kept_d, over_d, moving)
    moving = swap_z(moving, 1)
    hidden_out, grad, high, low = call(
        activate_body,
        "activate",
        (one16, one16, one16, one16),
        (own, moving, weight, bias[None, :], grad_out),
        flops=4 * 256**3,
        moved=2 * 2**20,
    )

    def backward(group, blocks, before, outs):
        return call(
            functools.partial(backward_body, group),
            f"backward_{group}",
            outs,
            (*plan, vals, *blocks, *before),
            scalars=4,
            scratch=(pltpu.VMEM((8, TILE, 256), BF16),)
            + ((pltpu.VMEM((17, TILE, 256), F32),) if group == LAST else ()),
            flops=0,
            moved=0,
        )

    running = jax.ShapeDtypeStruct((17, TILE, 256), F32)
    barrier = lax.optimization_barrier
    first = swap_z(grad, 1)
    kept, sent = call(
        terms_body,
        "weight_terms",
        (half, half),
        (core[None], high, low, grad),
        scalars=1,
        scratch=(pltpu.VMEM((256, 256), F32),),
        flops=4 * 256**3,
        moved=2**20,
    )
    terms = kept + to_core(sent)
    terms, _ = barrier((terms, first))
    pair_d = jnp.stack([grad, first])
    pair_c = swap_z(pair_d, -1)
    over_d = to_x(pair_d)
    terms = terms + to_x(terms)
    total = backward(0, (pair_d,), (), running)
    pair_c, total, terms = barrier((pair_c, total, terms))
    pair_b = swap_z(pair_c, 1)
    over_c = to_x(pair_c)
    terms = terms + flip_z(terms, 1)
    total = backward(1, (pair_c, over_d), (total,), running)
    pair_b, total, terms = barrier((pair_b, total, terms))
    pair_a = swap_z(pair_b, -1)
    over_b = to_x(pair_b)
    terms = terms + flip_z(terms, 2)
    total = backward(2, (pair_b, over_c), (total,), running)
    pair_a, total, terms = barrier((pair_a, total, terms))
    over_a = to_x(pair_a)
    terms = terms + flip_z(terms, 4)
    total = backward(3, (pair_a, over_b), (total,), running)
    over_a, total, terms = barrier((over_a, total, terms))
    own, kept, over = backward(
        4,
        (over_a,),
        (total,),
        (
            one,
            jax.ShapeDtypeStruct((3, shard, 256), F32),
            jax.ShapeDtypeStruct((4, shard, 256), BF16),
        ),
    )
    over = to_core(over)
    *sends, mine = call(
        back_relay_body,
        "back_relay",
        (*[shape(400, BF16)] * 3, shape(144, BF16)),
        (kept, over, terms),
        moved=2 * 2**20,
    )
    got = [to_y(a, s) for a, s in zip(sends, (1, 2, 3))]
    mine = call(
        functools.partial(sum_terms_body, scale), "sum_terms", half, (mine, *got), moved=2**19
    )
    other = to_core(mine)
    grad_feats = call(
        finish_body,
        "finish",
        one16,
        (own, over, *got, weight),
        flops=2 * 256**3,
        moved=2 * 2**20,
    )
    grad_weight, grad_bias = call(
        assemble_body,
        "assemble",
        (shape(256, F32), shape(1, F32)),
        (core[None], mine, other),
        scalars=1,
        moved=2**19,
    )
    return (hidden_out, grad_feats, grad_weight, grad_bias.reshape(256))


def solution(mesh):
    in_specs = (
        P(("slab", "col", "row"), None),
        P(),
        P(),
        P(("slab", "row", "col"), None),
        P(("slab", "row"), "col", None, None, None),
        P(("slab", "row"), "col", None),
        P(("slab", "row"), "col", None),
        P(("slab", "row"), "col"),
    )
    out_specs = (
        P(("slab", "row", "col"), None),
        P(("slab", "col", "row"), None),
        P("slab", None),
        P("slab"),
    )
    return jax.shard_map(
        per_device, mesh=mesh, in_specs=in_specs, out_specs=out_specs, check_vma=False
    )
```

```python
import functools
import math

import jax
import jax.numpy as jnp
from jax import lax
from jax.experimental import pallas as pl
from jax.experimental.pallas import tpu as pltpu
from jax.sharding import PartitionSpec as P

TILE = 128
UNROLL = 16
ORDER = (
    ((0, 0), (1, 0)),
    ((7, 0), (6, 0), (7, 1), (6, 1), (0, 1), (1, 1)),
    ((2, 0), (3, 0), (2, 1), (3, 1)),
    ((5, 0), (4, 0), (5, 1), (4, 1)),
)
FIRST = (0, 2, 8, 12)
LAST = 3
NY = 4
NZ = 8
F32 = jnp.float32
BF16 = jnp.bfloat16
LIMIT = pltpu.CompilerParams(vmem_limit_bytes=32 * 2**20)


def vmem():
    return pl.BlockSpec(memory_space=pltpu.VMEM)


def smem():
    return pl.BlockSpec(memory_space=pltpu.SMEM)


def shape(rows, dtype):
    return jax.ShapeDtypeStruct((rows, 256), dtype)


def call(body, name, out_shape, args, scalars=0, scratch=(), flops=0, moved=0, specs=None):
    return pl.pallas_call(
        body,
        name=name,
        out_shape=out_shape,
        in_specs=specs or [smem()] * scalars + [vmem()] * (len(args) - scalars),
        out_specs=jax.tree.map(lambda _: vmem(), out_shape),
        scratch_shapes=scratch,
        compiler_params=LIMIT,
        cost_estimate=pl.CostEstimate(flops=flops, bytes_accessed=moved, transcendentals=0),
    )(*args)


def to_core(a):
    return lax.ppermute(a, "row", [(i, i ^ 1) for i in range(2 * NY)])


def to_y(a, step):
    return lax.ppermute(a, "row", [(i, (i + 2 * step) % (2 * NY)) for i in range(2 * NY)])


def to_x(a):
    return lax.ppermute(a, "col", [(i, i ^ 1) for i in range(2 * NZ)])


def swap_z(a, side, across=0):
    pairs = []
    for row in range(2 * NY):
        for col in range(2 * NZ):
            z, x = divmod(col, 2)
            step = side if (z + row) % 2 == 0 else -side
            to = (z + step) % NZ * 2 + (x + across) % 2
            pairs.append((row * 2 * NZ + col, row * 2 * NZ + to))
    return lax.ppermute(a, ("row", "col"), pairs)


def flip_z(a, bit):
    return lax.ppermute(a, "col", [(i, i ^ (2 * bit)) for i in range(2 * NZ)])


def load_body(source, out, sem):
    copy = pltpu.make_async_copy(source, out, sem)
    copy.start()
    copy.wait()


def collect_body(*refs):
    blocks, out = refs[:-1], refs[-1]
    for k, block in enumerate(blocks):
        for half in range(2):
            out[2 * k + half] = block[half * TILE : (half + 1) * TILE]


def place(ref, total, first, dtype):
    for half in range(2):
        ref[half * TILE : (half + 1) * TILE] = total[2 * first + half].astype(dtype)


def add_tiles(group, starts, order, to_slot, product, total, dummy):
    first, last = starts[group], starts[group + 1]

    def batch(i, carry):
        slots = [first + i * UNROLL + u for u in range(UNROLL)]
        safe = [jnp.minimum(t, 191) for t in slots]
        terms = [product(order[t], t) for t in safe]
        for slot, t, term in zip(slots, safe, terms):
            place_at = jnp.where(slot < last, to_slot(t), dummy)
            total[place_at] = total[place_at] + term
        return carry

    lax.fori_loop(0, (last - first + UNROLL - 1) // UNROLL, batch, 0)


def forward_body(group, starts, order, rows, cols, vals, source, *rest):
    outs, total = rest[:-1], rest[-1]
    size = 2 * len(ORDER[group])
    total[...] = jnp.zeros_like(total)
    add_tiles(
        group,
        starts,
        order,
        lambda t: jnp.clip(rows[t] - 2 * FIRST[group], 0, size - 1),
        lambda tile, t: jnp.dot(vals[tile], source[cols[t]], preferred_element_type=F32),
        total,
        size,
    )
    for k, out in enumerate(outs):
        for n in range(2):
            place(out.at[n], total, 2 * k + n, F32 if k == 0 and group < LAST else BF16)


def wide(ref):
    return ref[...].astype(F32)


def relay_body(kept, got, over, out):
    out[...] = (kept[...] + wide(got) + wide(over)).astype(BF16)


def relay_last_body(kept, got, over, near, own, out):
    own[...] = kept[0] + wide(got.at[0]) + wide(over.at[0]) + wide(near.at[0])
    out[...] = (kept[1] + wide(got.at[1]) + wide(over.at[1]) + wide(near.at[1])).astype(BF16)


def activate_body(own, got, weight, bias, given, hidden, grad, high, low):
    summed = own[...] + wide(got)
    top = summed.astype(BF16)
    rest = (summed - top.astype(F32)).astype(BF16)
    high[...] = top
    low[...] = rest
    pre_act = (
        jnp.dot(top, weight[...], preferred_element_type=F32)
        + jnp.dot(rest, weight[...], preferred_element_type=F32)
        + bias[...]
    )
    gate_value = jax.nn.sigmoid(pre_act)
    hidden[...] = (pre_act * gate_value).astype(BF16)
    slope = gate_value * (1.0 + pre_act * (1.0 - gate_value))
    grad[...] = (given[...].astype(F32) * slope).astype(BF16)


def terms_body(core, high, low, grad, kept, sent, whole):
    g = grad[...]
    dims = (((0,), (0,)), ((), ()))
    whole[...] = lax.dot_general(high[...], g, dims, preferred_element_type=F32) + lax.dot_general(
        low[...], g, dims, preferred_element_type=F32
    )
    column = jnp.sum(g.astype(F32), axis=0, keepdims=True)
    for ref, half in ((kept, core[0]), (sent, 1 - core[0])):
        ref[0:128] = whole[pl.ds(pl.multiple_of(half * 128, 128), 128)].astype(BF16)
        ref[128:144] = jnp.broadcast_to(column, (16, 256)).astype(BF16)


def add_terms_body(mine, other, out):
    out[...] = (wide(mine) + wide(other)).astype(BF16)


def backward_body(group, starts, order, rows, cols, vals, *rest):
    count = (1, 3, 2, 2)[group]
    blocks, rest = rest[:count], rest[count:]
    if group:
        before, rest = rest[0], rest[1:]
    if group == LAST:
        own, kept, over, source, total = rest
    else:
        total, source = rest
    n = 0
    for block in blocks:
        for half in range(4):
            source[n] = block[half // 2, half % 2 * TILE : (half % 2 + 1) * TILE]
            n += 1
    if group:
        total[...] = before[...]
    else:
        total[...] = jnp.zeros_like(total)
    add_tiles(
        group,
        starts,
        order,
        lambda t: cols[t],
        lambda tile, t: lax.dot_general(
            vals[tile],
            source[jnp.clip(rows[t] - 2 * FIRST[group], 0, n - 1)],
            (((0,), (0,)), ((), ())),
            preferred_element_type=F32,
        ),
        total,
        16,
    )
    if group == LAST:
        place(own, total, 0, F32)
        for k, dy in enumerate((1, 2, 3)):
            place(kept.at[k], total, 2 * dy, F32)
            place(over.at[k], total, 2 * dy + 1, BF16)
        place(over.at[3], total, 1, BF16)


def back_relay_body(kept, over, terms, out_a, out_b, out_c):
    for k, out in enumerate((out_a, out_b, out_c)):
        out[0:256] = (kept[k] + over[k].astype(F32)).astype(BF16)
        out[256:400] = terms[...]


def sum_terms_body(scale, own, a, b, c, out):
    total = (wide(own) + b[256:400].astype(F32)) + (
        a[256:400].astype(F32) + c[256:400].astype(F32)
    )
    out[...] = total[0:136] * scale


def finish_body(own, over, a, b, c, weight, out):
    back = own[...] + over[3].astype(F32)
    for ref in (a, b, c):
        back = back + ref[0:256].astype(F32)
    out[...] = lax.dot_general(
        back.astype(BF16), weight[...], (((1,), (1,)), ((), ())), preferred_element_type=F32
    ).astype(BF16)


def assemble_body(core, mine, other, weight, bias):
    for ref, half in ((mine, core[0]), (other, 1 - core[0])):
        weight[pl.ds(pl.multiple_of(half * 128, 128), 128)] = ref[0:128]
    bias[...] = mine[128:129]


def per_device(feats, weight, bias, grad_out, tile_vals, tile_rows, tile_cols, tile_count):
    shard = feats.shape[0]
    scale = 1.0 / math.sqrt(shard * 2 * NY * 2 * NZ)
    row, col = lax.axis_index("row"), lax.axis_index("col")
    y, core, z, x = row // 2, row % 2, col // 2, col % 2
    owner_row, owner_col = tile_rows[0, 0] // 2, tile_cols[0, 0] // 2
    toward = 1 - 2 * ((z + core) % 2)
    where = (owner_row // 2 - z) * toward % NZ * 2 + (owner_row + x) % 2
    ranks = [0] * (2 * NZ)
    for rank, (dz, dx) in enumerate(sum(ORDER, ())):
        ranks[dz * 2 + dx] = rank
    rank = sum(jnp.where(where == k, r, 0) for k, r in enumerate(ranks))
    group = sum((rank >= f).astype(jnp.int32) for f in FIRST[1:])
    rows = rank * 2 + tile_rows[0, 0] % 2
    rel_y = (owner_col // 2 - y) % NY
    cols = (rel_y * 2 + (owner_col + core) % 2) * 2 + tile_cols[0, 0] % 2
    slots = jnp.arange(rows.shape[0], dtype=jnp.int32)
    live = slots < tile_count[0, 0]
    key = jnp.where(live, group, LAST + 1) * rows.shape[0] + slots
    position = jnp.sum((key[None, :] < key[:, None]).astype(jnp.int32), axis=1)
    chosen = position[None, :] == slots[:, None]
    order, rows, cols = (
        jnp.sum(jnp.where(chosen, a[None, :], 0), axis=1) for a in (slots, rows, cols)
    )
    groups = jnp.arange(8, dtype=jnp.int32)
    starts = jnp.sum((key[None, :] < groups[:, None] * rows.shape[0]).astype(jnp.int32), axis=1)
    plan = (starts, order, rows, cols)

    tiles = tile_vals[0, 0]
    vals = call(
        load_body,
        "load_tiles",
        jax.ShapeDtypeStruct(tiles.shape, BF16),
        (tiles,),
        scratch=(pltpu.SemaphoreType.DMA,),
        moved=2 * tiles.size * 2,
        specs=[pl.BlockSpec(memory_space=pltpu.HBM)],
    )
    gathered = {(0, 0): feats, (0, 1): to_core(feats)}
    steps = (1, -1, 2)
    arrived = [to_y(feats, step) for step in steps]
    arrived, vals, plan = lax.optimization_barrier((arrived, vals, plan))
    for step, block in zip(steps, arrived):
        gathered[(-step) % NY, 0] = block
        gathered[(-step) % NY, 1] = to_core(block)
    source = call(
        collect_body,
        "collect",
        jax.ShapeDtypeStruct((16, TILE, 256), BF16),
        tuple(gathered[k // 2, k % 2] for k in range(8)),
        moved=2**21,
    )
    work = 2 * 48 * TILE * TILE * 256

    one, two = shape(shard, F32), jax.ShapeDtypeStruct((2, shard, 256), F32)
    one16, two16 = shape(shard, BF16), jax.ShapeDtypeStruct((2, shard, 256), BF16)
    half = shape(144, BF16)

    def forward(group, outs, source):
        return call(
            functools.partial(forward_body, group),
            f"forward_{group}",
            outs,
            (*plan, vals, source),
            scalars=4,
            scratch=(pltpu.VMEM((2 * len(ORDER[group]) + 1, TILE, 256), F32),),
            flops=0,
            moved=0,
        )

    def relay(body, name, outs, *args):
        return call(body, name, outs, args, moved=2**20)

    barrier = lax.optimization_barrier
    moving, over = forward(3, (two16, two16), source)
    moving, over, source = barrier((moving, over, source))
    moving, over = swap_z(moving, -1), swap_z(over, -1, 1)
    kept, next_over = forward(2, (two, two16), source)
    next_over = swap_z(next_over, 1, 1)
    moving = relay(relay_body, "relay_2", two16, kept, moving, over)
    moving, source = barrier((moving, source))
    moving, over = swap_z(moving, 1), next_over
    kept, next_over, near = forward(1, (two, two16, two16), source)
    next_over, near = swap_z(next_over, -1, 1), to_x(near)
    moving = relay(relay_body, "relay_1", two16, kept, moving, over)
    moving, source = barrier((moving, source))
    moving, over = swap_z(moving, -1), next_over
    (kept,) = forward(0, (two,), source)
    own, moving = relay(relay_last_body, "relay_0", (one, one16), kept, moving, over, near)
    moving = swap_z(moving, 1)
    hidden_out, grad, high, low = call(
        activate_body,
        "activate",
        (one16, one16, one16, one16),
        (own, moving, weight, bias[None, :], grad_out),
        flops=4 * 256**3,
        moved=2 * 2**20,
    )

    def backward(group, blocks, before, outs):
        return call(
            functools.partial(backward_body, group),
            f"backward_{group}",
            outs,
            (*plan, vals, *blocks, *before),
            scalars=4,
            scratch=(pltpu.VMEM((2 * len(ORDER[group]), TILE, 256), BF16),)
            + ((pltpu.VMEM((17, TILE, 256), F32),) if group == LAST else ()),
            flops=0,
            moved=0,
        )

    running = jax.ShapeDtypeStruct((17, TILE, 256), F32)
    last = (
        one,
        jax.ShapeDtypeStruct((3, shard, 256), F32),
        jax.ShapeDtypeStruct((4, shard, 256), BF16),
    )
    def add_terms(mine, other):
        return call(add_terms_body, "add_terms", half, (mine, other), moved=2**18)

    first = swap_z(grad, 1)
    terms, sent = call(
        terms_body,
        "weight_terms",
        (half, half),
        (core[None], high, low, grad),
        scalars=1,
        scratch=(pltpu.VMEM((256, 256), F32),),
        flops=4 * 256**3,
        moved=2**20,
    )
    terms = add_terms(terms, to_core(sent))
    terms, first = barrier((terms, first))
    pair_d = jnp.stack([grad, first])
    pair, over, near = swap_z(pair_d, -1), swap_z(pair_d, -1, 1), to_x(pair_d)
    moved_terms = to_x(terms)
    total = backward(0, (pair_d,), (), running)
    pair, over, total, moved_terms = barrier((pair, over, total, moved_terms))
    blocks = (pair, over, near)
    for group, way, bit in ((1, 1, 1), (2, -1, 2)):
        next_pair, over = swap_z(pair, way), swap_z(pair, way, 1)
        terms = add_terms(terms, moved_terms)
        terms, blocks, total = barrier((terms, blocks, total))
        moved_terms = flip_z(terms, bit)
        total = backward(group, blocks, (total,), running)
        pair, over, total, moved_terms = barrier((next_pair, over, total, moved_terms))
        blocks = (pair, over)
    terms = add_terms(terms, moved_terms)
    terms, blocks, total = barrier((terms, blocks, total))
    moved_terms = flip_z(terms, 4)
    own, kept, over = backward(LAST, blocks, (total,), last)
    terms = add_terms(terms, moved_terms)
    over = to_core(over)
    sends = call(
        back_relay_body,
        "back_relay",
        (shape(400, BF16),) * 3,
        (kept, over, terms),
        moved=2 * 2**20,
    )
    got = [to_y(a, s) for a, s in zip(sends, (1, 2, 3))]
    mine = call(
        functools.partial(sum_terms_body, scale),
        "sum_terms",
        shape(136, F32),
        (terms, *got),
        moved=2**19,
    )
    other = to_core(mine)
    grad_feats = call(
        finish_body,
        "finish",
        one16,
        (own, over, *got, weight),
        flops=2 * 256**3,
        moved=2 * 2**20,
    )
    grad_weight, grad_bias = call(
        assemble_body,
        "assemble",
        (shape(256, F32), shape(1, F32)),
        (core[None], mine, other),
        scalars=1,
        moved=2**19,
    )
    return (hidden_out, grad_feats, grad_weight, grad_bias.reshape(256))


def solution(mesh):
    in_specs = (
        P(("slab", "col", "row"), None),
        P(),
        P(),
        P(("slab", "row", "col"), None),
        P(("slab", "row"), "col", None, None, None),
        P(("slab", "row"), "col", None),
        P(("slab", "row"), "col", None),
        P(("slab", "row"), "col"),
    )
    out_specs = (
        P(("slab", "row", "col"), None),
        P(("slab", "col", "row"), None),
        P("slab", None),
        P("slab"),
    )
    return jax.shard_map(
        per_device, mesh=mesh, in_specs=in_specs, out_specs=out_specs, check_vma=False
    )
```

```python
import functools
import math

import jax
import jax.numpy as jnp
from jax import lax
from jax.experimental import pallas as pl
from jax.experimental.pallas import tpu as pltpu
from jax.sharding import PartitionSpec as P

TILE = 128
UNROLL = 16
ORDER = (
    ((0, 0), (1, 0)),
    ((7, 0), (6, 0)),
    ((0, 1), (1, 1)),
    ((2, 0), (3, 0)),
    ((7, 1), (6, 1)),
    ((2, 1), (3, 1)),
    ((5, 0), (4, 0)),
    ((5, 1), (4, 1)),
)
NY = 4
NZ = 8
F32 = jnp.float32
BF16 = jnp.bfloat16
LIMIT = pltpu.CompilerParams(vmem_limit_bytes=32 * 2**20)


def vmem():
    return pl.BlockSpec(memory_space=pltpu.VMEM)


def smem():
    return pl.BlockSpec(memory_space=pltpu.SMEM)


def shape(rows, dtype):
    return jax.ShapeDtypeStruct((rows, 256), dtype)


def call(body, name, out_shape, args, scalars=0, scratch=(), flops=0, moved=0, specs=None):
    return pl.pallas_call(
        body,
        name=name,
        out_shape=out_shape,
        in_specs=specs or [smem()] * scalars + [vmem()] * (len(args) - scalars),
        out_specs=jax.tree.map(lambda _: vmem(), out_shape),
        scratch_shapes=scratch,
        compiler_params=LIMIT,
        cost_estimate=pl.CostEstimate(flops=flops, bytes_accessed=moved, transcendentals=0),
    )(*args)


def to_core(a):
    return lax.ppermute(a, "row", [(i, i ^ 1) for i in range(2 * NY)])


def to_y(a, step):
    return lax.ppermute(a, "row", [(i, (i + 2 * step) % (2 * NY)) for i in range(2 * NY)])


def to_x(a):
    return lax.ppermute(a, "col", [(i, i ^ 1) for i in range(2 * NZ)])


def swap_z(a, side, across=0):
    pairs = []
    for row in range(2 * NY):
        for col in range(2 * NZ):
            z, x = divmod(col, 2)
            step = side if (z + row) % 2 == 0 else -side
            to = (z + step) % NZ * 2 + (x + across) % 2
            pairs.append((row * 2 * NZ + col, row * 2 * NZ + to))
    return lax.ppermute(a, ("row", "col"), pairs)


def load_body(source, out, sem):
    copy = pltpu.make_async_copy(source, out, sem)
    copy.start()
    copy.wait()


def collect_body(*refs):
    blocks, out = refs[:-1], refs[-1]
    for k, block in enumerate(blocks):
        for half in range(2):
            out[2 * k + half] = block[half * TILE : (half + 1) * TILE]


def place(ref, total, first, dtype):
    for half in range(2):
        ref[half * TILE : (half + 1) * TILE] = total[2 * first + half].astype(dtype)


def add_tiles(begin, end, starts, order, to_slot, product, total, dummy):
    first, last = starts[begin], starts[end]

    def batch(i, carry):
        slots = [first + i * UNROLL + u for u in range(UNROLL)]
        safe = [jnp.minimum(t, 191) for t in slots]
        terms = [product(order[t], t) for t in safe]
        for slot, t, term in zip(slots, safe, terms):
            place_at = jnp.where(slot < last, to_slot(t), dummy)
            total[place_at] = total[place_at] + term
        return carry

    lax.fori_loop(0, (last - first + UNROLL - 1) // UNROLL, batch, 0)


def forward_body(begin, end, starts, order, rows, cols, vals, source, *rest):
    outs, total = rest[:-1], rest[-1]
    size = 4 * (end - begin)
    total[...] = jnp.zeros_like(total)
    add_tiles(
        begin,
        end,
        starts,
        order,
        lambda t: jnp.clip(rows[t] - 4 * begin, 0, size - 1),
        lambda tile, t: jnp.dot(vals[tile], source[cols[t]], preferred_element_type=F32),
        total,
        size,
    )
    for k, out in enumerate(outs):
        for n in range(2):
            place(out.at[n], total, 2 * k + n, out.dtype)


def wide(ref):
    return ref[...].astype(F32)


def relay_body(kept, *rest):
    total = kept[...]
    for ref in rest[:-1]:
        total = total + wide(ref)
    rest[-1][...] = total.astype(BF16)


def relay_last_body(kept, over, got, own, out):
    own[...] = kept[0] + wide(over.at[0]) + wide(got.at[0])
    out[...] = (kept[1] + wide(over.at[1]) + wide(got.at[1])).astype(BF16)


def activate_body(own, got, weight, bias, given, hidden, grad, high, low):
    summed = own[...] + wide(got)
    top = summed.astype(BF16)
    rest = (summed - top.astype(F32)).astype(BF16)
    high[...] = top
    low[...] = rest
    pre_act = (
        jnp.dot(top, weight[...], preferred_element_type=F32)
        + jnp.dot(rest, weight[...], preferred_element_type=F32)
        + bias[...]
    )
    gate_value = jax.nn.sigmoid(pre_act)
    hidden[...] = (pre_act * gate_value).astype(BF16)
    slope = gate_value * (1.0 + pre_act * (1.0 - gate_value))
    grad[...] = (given[...].astype(F32) * slope).astype(BF16)


def terms_body(core, high, low, grad, kept, sent, whole):
    g = grad[...]
    dims = (((0,), (0,)), ((), ()))
    whole[...] = lax.dot_general(high[...], g, dims, preferred_element_type=F32) + lax.dot_general(
        low[...], g, dims, preferred_element_type=F32
    )
    column = jnp.sum(g.astype(F32), axis=0, keepdims=True)
    for ref, half in ((kept, core[0]), (sent, 1 - core[0])):
        ref[0:128] = whole[pl.ds(pl.multiple_of(half * 128, 128), 128)].astype(BF16)
        ref[128:144] = jnp.broadcast_to(column, (16, 256)).astype(BF16)


def add_rows(a, b):
    return (a.astype(F32) + b.astype(F32)).astype(BF16)


def pack_own_body(grad, mine, other, out):
    out[0:256] = grad[...]
    out[256:400] = add_rows(mine[...], other[...])


def pack_pair_body(own, got, out):
    out[0:256] = own[0:256]
    out[256:512] = got[0:256]
    out[512:656] = add_rows(own[256:400], got[256:400])


def pack_far_body(before, got, out):
    out[0:512] = got[0:512]
    out[512:656] = add_rows(before[512:656], got[512:656])


def backward_body(begin, end, starts, order, rows, cols, vals, *rest):
    blocks, rest = rest[: end - begin], rest[end - begin :]
    if begin:
        before, rest = rest[0], rest[1:]
    if end == len(ORDER):
        own, kept, over, source, total = rest
    else:
        total, source = rest
    n = 0
    for block in blocks:
        for k in range(4):
            source[n] = block[k * TILE : (k + 1) * TILE]
            n += 1
    if begin:
        total[...] = before[...]
    else:
        total[...] = jnp.zeros_like(total)
    add_tiles(
        begin,
        end,
        starts,
        order,
        lambda t: cols[t],
        lambda tile, t: lax.dot_general(
            vals[tile],
            source[jnp.clip(rows[t] - 4 * begin, 0, n - 1)],
            (((0,), (0,)), ((), ())),
            preferred_element_type=F32,
        ),
        total,
        16,
    )
    if end == len(ORDER):
        place(own, total, 0, F32)
        for k, dy in enumerate((1, 2, 3)):
            place(kept.at[k], total, 2 * dy, F32)
            place(over.at[k], total, 2 * dy + 1, BF16)
        place(over.at[3], total, 1, BF16)


def back_relay_body(kept, over, pair, last, far, side, near, out_a, out_b, out_c, terms):
    sums = slice(512, 656)
    plane = add_rows(pair[sums], last[sums]).astype(F32) + far[sums].astype(F32)
    other = side[sums].astype(F32) + near[sums].astype(F32)
    terms[...] = (plane + other).astype(BF16)
    for k, out in enumerate((out_a, out_b, out_c)):
        out[0:256] = (kept[k] + over[k].astype(F32)).astype(BF16)
        out[256:400] = terms[...]


def sum_terms_body(scale, own, a, b, c, out):
    total = (wide(own) + b[256:400].astype(F32)) + (
        a[256:400].astype(F32) + c[256:400].astype(F32)
    )
    out[...] = total[0:136] * scale


def finish_body(own, over, a, b, c, weight, out):
    back = own[...] + over[3].astype(F32)
    for ref in (a, b, c):
        back = back + ref[0:256].astype(F32)
    out[...] = lax.dot_general(
        back.astype(BF16), weight[...], (((1,), (1,)), ((), ())), preferred_element_type=F32
    ).astype(BF16)


def assemble_body(core, mine, other, weight, bias):
    for ref, half in ((mine, core[0]), (other, 1 - core[0])):
        weight[pl.ds(pl.multiple_of(half * 128, 128), 128)] = ref[0:128]
    bias[...] = mine[128:129]


def per_device(feats, weight, bias, grad_out, tile_vals, tile_rows, tile_cols, tile_count):
    shard = feats.shape[0]
    scale = 1.0 / math.sqrt(shard * 2 * NY * 2 * NZ)
    row, col = lax.axis_index("row"), lax.axis_index("col")
    y, core, z, x = row // 2, row % 2, col // 2, col % 2
    owner_row, owner_col = tile_rows[0, 0] // 2, tile_cols[0, 0] // 2
    toward = 1 - 2 * ((z + core) % 2)
    where = (owner_row // 2 - z) * toward % NZ * 2 + (owner_row + x) % 2
    ranks = [0] * (2 * NZ)
    for rank, (dz, dx) in enumerate(sum(ORDER, ())):
        ranks[dz * 2 + dx] = rank
    rank = sum(jnp.where(where == k, r, 0) for k, r in enumerate(ranks))
    rows = rank * 2 + tile_rows[0, 0] % 2
    rel_y = (owner_col // 2 - y) % NY
    cols = (rel_y * 2 + (owner_col + core) % 2) * 2 + tile_cols[0, 0] % 2
    slots = jnp.arange(rows.shape[0], dtype=jnp.int32)
    live = slots < tile_count[0, 0]
    key = jnp.where(live, rank // 2, len(ORDER)) * rows.shape[0] + slots
    position = jnp.sum((key[None, :] < key[:, None]).astype(jnp.int32), axis=1)
    chosen = position[None, :] == slots[:, None]
    order, rows, cols = (
        jnp.sum(jnp.where(chosen, a[None, :], 0), axis=1) for a in (slots, rows, cols)
    )
    groups = jnp.arange(16, dtype=jnp.int32)
    starts = jnp.sum((key[None, :] < groups[:, None] * rows.shape[0]).astype(jnp.int32), axis=1)
    plan = (starts, order, rows, cols)

    tiles = tile_vals[0, 0]
    vals = call(
        load_body,
        "load_tiles",
        jax.ShapeDtypeStruct(tiles.shape, BF16),
        (tiles,),
        scratch=(pltpu.SemaphoreType.DMA,),
        moved=2 * tiles.size * 2,
        specs=[pl.BlockSpec(memory_space=pltpu.HBM)],
    )
    gathered = {(0, 0): feats, (0, 1): to_core(feats)}
    steps = (1, -1, 2)
    arrived = [to_y(feats, step) for step in steps]
    arrived, vals, plan = lax.optimization_barrier((arrived, vals, plan))
    for step, block in zip(steps, arrived):
        gathered[(-step) % NY, 0] = block
        gathered[(-step) % NY, 1] = to_core(block)
    source = call(
        collect_body,
        "collect",
        jax.ShapeDtypeStruct((16, TILE, 256), BF16),
        tuple(gathered[k // 2, k % 2] for k in range(8)),
        moved=2**21,
    )

    one, two = shape(shard, F32), jax.ShapeDtypeStruct((2, shard, 256), F32)
    one16, two16 = shape(shard, BF16), jax.ShapeDtypeStruct((2, shard, 256), BF16)
    half = shape(144, BF16)

    def forward(begin, end, outs, source):
        return call(
            functools.partial(forward_body, begin, end),
            f"forward_{begin}",
            outs,
            (*plan, vals, source),
            scalars=4,
            scratch=(pltpu.VMEM((4 * (end - begin) + 1, TILE, 256), F32),),
        )

    def relay(body, name, outs, *args):
        return call(body, name, outs, args, moved=2**20)

    barrier = lax.optimization_barrier
    moving, far = forward(6, 8, (two16, two16), source)
    moving, far, source = barrier((moving, far, source))
    far, moving = swap_z(far, -1, 1), swap_z(moving, -1)
    kept_b, over_c, over_b = forward(3, 6, (two, two16, two16), source)
    over_b, over_c = to_x(over_b), to_x(over_c)
    moving = relay(relay_body, "relay_b", two16, kept_b, moving, far, over_b)
    moving, source = barrier((moving, source))
    moving = swap_z(moving, 1)
    kept_c, over_d = forward(1, 3, (two, two16), source)
    over_d = to_x(over_d)
    moving = relay(relay_body, "relay_c", two16, kept_c, moving, over_c)
    moving, source = barrier((moving, source))
    moving = swap_z(moving, -1)
    (kept_d,) = forward(0, 1, (two,), source)
    own, moving = relay(relay_last_body, "relay_last", (one, one16), kept_d, over_d, moving)
    moving = swap_z(moving, 1)
    hidden_out, grad, high, low = call(
        activate_body,
        "activate",
        (one16, one16, one16, one16),
        (own, moving, weight, bias[None, :], grad_out),
        flops=4 * 256**3,
        moved=2 * 2**20,
    )

    def backward(begin, blocks, before, outs):
        end = begin + len(blocks)
        return call(
            functools.partial(backward_body, begin, end),
            f"backward_{begin}",
            outs,
            (*plan, vals, *blocks, *before),
            scalars=4,
            scratch=(pltpu.VMEM((4 * len(blocks), TILE, 256), BF16),)
            + ((pltpu.VMEM((17, TILE, 256), F32),) if end == len(ORDER) else ()),
        )

    running = jax.ShapeDtypeStruct((17, TILE, 256), F32)
    terms, sent = call(
        terms_body,
        "weight_terms",
        (half, half),
        (core[None], high, low, grad),
        scalars=1,
        scratch=(pltpu.VMEM((256, 256), F32),),
        flops=4 * 256**3,
        moved=2**20,
    )
    message = shape(656, BF16)
    own_grad = call(
        pack_own_body, "pack_own", shape(400, BF16), (grad, terms, to_core(sent)), moved=2**19
    )
    first = swap_z(own_grad, 1)
    pair_d = call(pack_pair_body, "pack_pair", message, (own_grad, first), moved=2**20)
    pair_c, over_d = swap_z(pair_d, -1), to_x(pair_d[:512])
    total = backward(0, (pair_d,), (), running)
    pair_c, over_d, total = barrier((pair_c, over_d, total))
    pair_b, over_c = swap_z(pair_c, 1), to_x(pair_c[:512])
    total = backward(1, (pair_c, over_d), (total,), running)
    pair_b, over_c, total = barrier((pair_b, over_c, total))
    far = call(pack_far_body, "pack_far", message, (pair_c, pair_b), moved=2**20)
    pair_b, far = barrier((pair_b, far))
    side, pair_a, near = swap_z(far, -1, 1), swap_z(pair_b, -1), to_x(far)
    total = backward(3, (pair_b, over_c), (total,), running)
    pair_a, near, total = barrier((pair_a, near, total))
    total = backward(5, (near, pair_a), (total,), running)
    side, total = barrier((side, total))
    own, kept, over = backward(
        7,
        (side,),
        (total,),
        (
            one,
            jax.ShapeDtypeStruct((3, shard, 256), F32),
            jax.ShapeDtypeStruct((4, shard, 256), BF16),
        ),
    )
    over = to_core(over)
    *sends, terms = call(
        back_relay_body,
        "back_relay",
        (*[shape(400, BF16)] * 3, half),
        (kept, over, pair_d, pair_a, far, side, near),
        moved=2 * 2**20,
    )
    got = [to_y(a, s) for a, s in zip(sends, (1, 2, 3))]
    mine = call(
        functools.partial(sum_terms_body, scale),
        "sum_terms",
        shape(136, F32),
        (terms, *got),
        moved=2**19,
    )
    other = to_core(mine)
    grad_feats = call(
        finish_body,
        "finish",
        one16,
        (own, over, *got, weight),
        flops=2 * 256**3,
        moved=2 * 2**20,
    )
    grad_weight, grad_bias = call(
        assemble_body,
        "assemble",
        (shape(256, F32), shape(1, F32)),
        (core[None], mine, other),
        scalars=1,
        moved=2**19,
    )
    return (hidden_out, grad_feats, grad_weight, grad_bias.reshape(256))


def solution(mesh):
    in_specs = (
        P(("slab", "col", "row"), None),
        P(),
        P(),
        P(("slab", "row", "col"), None),
        P(("slab", "row"), "col", None, None, None),
        P(("slab", "row"), "col", None),
        P(("slab", "row"), "col", None),
        P(("slab", "row"), "col"),
    )
    out_specs = (
        P(("slab", "row", "col"), None),
        P(("slab", "col", "row"), None),
        P("slab", None),
        P("slab"),
    )
    return jax.shard_map(
        per_device, mesh=mesh, in_specs=in_specs, out_specs=out_specs, check_vma=False
    )
```

```python
import functools
import math

import jax
import jax.numpy as jnp
from jax import lax
from jax.experimental import pallas as pl
from jax.experimental.pallas import tpu as pltpu
from jax.sharding import PartitionSpec as P

TILE = 128
UNROLL = 16
ORDER = (
    ((0, 0), (1, 0)),
    ((7, 0), (6, 0)),
    ((0, 1), (1, 1)),
    ((2, 0), (3, 0)),
    ((2, 1), (3, 1)),
    ((7, 1), (6, 1)),
    ((5, 0), (4, 0)),
    ((5, 1), (4, 1)),
)
NY = 4
NZ = 8
F32 = jnp.float32
BF16 = jnp.bfloat16
LIMIT = pltpu.CompilerParams(vmem_limit_bytes=32 * 2**20)


def vmem():
    return pl.BlockSpec(memory_space=pltpu.VMEM)


def smem():
    return pl.BlockSpec(memory_space=pltpu.SMEM)


def shape(rows, dtype):
    return jax.ShapeDtypeStruct((rows, 256), dtype)


def call(body, name, out_shape, args, scalars=0, scratch=(), flops=0, moved=0, specs=None):
    return pl.pallas_call(
        body,
        name=name,
        out_shape=out_shape,
        in_specs=specs or [smem()] * scalars + [vmem()] * (len(args) - scalars),
        out_specs=jax.tree.map(lambda _: vmem(), out_shape),
        scratch_shapes=scratch,
        compiler_params=LIMIT,
        cost_estimate=pl.CostEstimate(flops=flops, bytes_accessed=moved, transcendentals=0),
    )(*args)


def to_core(a):
    return lax.ppermute(a, "row", [(i, i ^ 1) for i in range(2 * NY)])


def to_y(a, step):
    return lax.ppermute(a, "row", [(i, (i + 2 * step) % (2 * NY)) for i in range(2 * NY)])


def to_x(a):
    return lax.ppermute(a, "col", [(i, i ^ 1) for i in range(2 * NZ)])


def swap_z(a, side, across=0):
    pairs = []
    for row in range(2 * NY):
        for col in range(2 * NZ):
            z, x = divmod(col, 2)
            step = side if (z + row) % 2 == 0 else -side
            to = (z + step) % NZ * 2 + (x + across) % 2
            pairs.append((row * 2 * NZ + col, row * 2 * NZ + to))
    return lax.ppermute(a, ("row", "col"), pairs)


def load_body(source, out, sem):
    copy = pltpu.make_async_copy(source, out, sem)
    copy.start()
    copy.wait()


def collect_body(*refs):
    blocks, out = refs[:-1], refs[-1]
    for k, block in enumerate(blocks):
        for half in range(2):
            out[2 * k + half] = block[half * TILE : (half + 1) * TILE]


def place(ref, total, first, dtype):
    for half in range(2):
        ref[half * TILE : (half + 1) * TILE] = total[2 * first + half].astype(dtype)


def add_tiles(begin, end, starts, order, to_slot, product, total, dummy):
    first, last = starts[begin], starts[end]

    def batch(i, carry):
        slots = [first + i * UNROLL + u for u in range(UNROLL)]
        safe = [jnp.minimum(t, 191) for t in slots]
        terms = [product(order[t], t) for t in safe]
        for slot, t, term in zip(slots, safe, terms):
            place_at = jnp.where(slot < last, to_slot(t), dummy)
            total[place_at] = total[place_at] + term
        return carry

    lax.fori_loop(0, (last - first + UNROLL - 1) // UNROLL, batch, 0)


def forward_body(begin, end, starts, order, rows, cols, vals, source, *rest):
    outs, total = rest[:-1], rest[-1]
    size = 4 * (end - begin)
    total[...] = jnp.zeros_like(total)
    add_tiles(
        begin,
        end,
        starts,
        order,
        lambda t: jnp.clip(rows[t] - 4 * begin, 0, size - 1),
        lambda tile, t: jnp.dot(vals[tile], source[cols[t]], preferred_element_type=F32),
        total,
        size,
    )
    first = 0
    for out in outs:
        for n in range(out.shape[0]):
            place(out.at[n], total, first + n, out.dtype)
        first += out.shape[0]


def wide(ref):
    return ref[...].astype(F32)


def relay_first_body(kept, side, got, out, out_side):
    out[...] = (kept[...] + wide(got.at[0:2])).astype(BF16)
    out_side[...] = (side[...] + wide(got.at[2:4])).astype(BF16)


def relay_body(kept, *rest):
    total = kept[...]
    for ref in rest[:-1]:
        total = total + wide(ref)
    rest[-1][...] = total.astype(BF16)


def relay_last_body(kept, over, got, own, out):
    own[...] = kept[0] + wide(over.at[0]) + wide(got.at[0])
    out[...] = (kept[1] + wide(over.at[1]) + wide(got.at[1])).astype(BF16)


def activate_body(own, got, weight, bias, given, hidden, grad, high, low):
    summed = own[...] + wide(got)
    top = summed.astype(BF16)
    rest = (summed - top.astype(F32)).astype(BF16)
    high[...] = top
    low[...] = rest
    pre_act = (
        jnp.dot(top, weight[...], preferred_element_type=F32)
        + jnp.dot(rest, weight[...], preferred_element_type=F32)
        + bias[...]
    )
    gate_value = jax.nn.sigmoid(pre_act)
    hidden[...] = (pre_act * gate_value).astype(BF16)
    slope = gate_value * (1.0 + pre_act * (1.0 - gate_value))
    grad[...] = (given[...].astype(F32) * slope).astype(BF16)


def terms_body(core, high, low, grad, kept, sent, whole):
    g = grad[...]
    dims = (((0,), (0,)), ((), ()))
    whole[...] = lax.dot_general(high[...], g, dims, preferred_element_type=F32) + lax.dot_general(
        low[...], g, dims, preferred_element_type=F32
    )
    column = jnp.sum(g.astype(F32), axis=0, keepdims=True)
    for ref, half in ((kept, core[0]), (sent, 1 - core[0])):
        ref[0:128] = whole[pl.ds(pl.multiple_of(half * 128, 128), 128)].astype(BF16)
        ref[128:144] = jnp.broadcast_to(column, (16, 256)).astype(BF16)


def add_rows(a, b):
    return (a.astype(F32) + b.astype(F32)).astype(BF16)


def pack_own_body(grad, mine, other, out):
    out[0:256] = grad[...]
    out[256:400] = add_rows(mine[...], other[...])


def pack_pair_body(own, got, out):
    out[0:256] = own[0:256]
    out[256:512] = got[0:256]
    out[512:656] = add_rows(own[256:400], got[256:400])


def backward_body(begin, end, starts, order, rows, cols, vals, *rest):
    blocks, rest = rest[: end - begin], rest[end - begin :]
    if begin:
        before, rest = rest[0], rest[1:]
    if end == len(ORDER):
        own, kept, over, source, total = rest
    else:
        total, source = rest
    n = 0
    for block in blocks:
        for k in range(4):
            source[n] = block[k * TILE : (k + 1) * TILE]
            n += 1
    if begin:
        total[...] = before[...]
    else:
        total[...] = jnp.zeros_like(total)
    add_tiles(
        begin,
        end,
        starts,
        order,
        lambda t: cols[t],
        lambda tile, t: lax.dot_general(
            vals[tile],
            source[jnp.clip(rows[t] - 4 * begin, 0, n - 1)],
            (((0,), (0,)), ((), ())),
            preferred_element_type=F32,
        ),
        total,
        16,
    )
    if end == len(ORDER):
        place(own, total, 0, F32)
        for k, dy in enumerate((1, 2, 3)):
            place(kept.at[k], total, 2 * dy, F32)
            place(over.at[k], total, 2 * dy + 1, BF16)
        place(over.at[3], total, 1, BF16)


def back_relay_body(kept, over, pd, pa, pc, pb, sd, sa, sc, sb, out_a, out_b, out_c, terms):
    sums = slice(512, 656)
    plane = add_rows(pd[sums], pa[sums]).astype(F32) + add_rows(pc[sums], pb[sums]).astype(F32)
    other = add_rows(sd[sums], sa[sums]).astype(F32) + add_rows(sc[sums], sb[sums]).astype(F32)
    terms[...] = (plane + other).astype(BF16)
    for k, out in enumerate((out_a, out_b, out_c)):
        out[0:256] = (kept[k] + over[k].astype(F32)).astype(BF16)
        out[256:400] = terms[...]


def sum_terms_body(scale, own, a, b, c, out):
    total = (wide(own) + b[256:400].astype(F32)) + (
        a[256:400].astype(F32) + c[256:400].astype(F32)
    )
    out[...] = total[0:136] * scale


def finish_body(own, over, a, b, c, weight, out):
    back = own[...] + over[3].astype(F32)
    for ref in (a, b, c):
        back = back + ref[0:256].astype(F32)
    out[...] = lax.dot_general(
        back.astype(BF16), weight[...], (((1,), (1,)), ((), ())), preferred_element_type=F32
    ).astype(BF16)


def assemble_body(core, mine, other, weight, bias):
    for ref, half in ((mine, core[0]), (other, 1 - core[0])):
        weight[pl.ds(pl.multiple_of(half * 128, 128), 128)] = ref[0:128]
    bias[...] = mine[128:129]


def per_device(feats, weight, bias, grad_out, tile_vals, tile_rows, tile_cols, tile_count):
    shard = feats.shape[0]
    scale = 1.0 / math.sqrt(shard * 2 * NY * 2 * NZ)
    row, col = lax.axis_index("row"), lax.axis_index("col")
    y, core, z, x = row // 2, row % 2, col // 2, col % 2
    owner_row, owner_col = tile_rows[0, 0] // 2, tile_cols[0, 0] // 2
    toward = 1 - 2 * ((z + core) % 2)
    where = (owner_row // 2 - z) * toward % NZ * 2 + (owner_row + x) % 2
    ranks = [0] * (2 * NZ)
    for rank, (dz, dx) in enumerate(sum(ORDER, ())):
        ranks[dz * 2 + dx] = rank
    rank = sum(jnp.where(where == k, r, 0) for k, r in enumerate(ranks))
    rows = rank * 2 + tile_rows[0, 0] % 2
    rel_y = (owner_col // 2 - y) % NY
    cols = (rel_y * 2 + (owner_col + core) % 2) * 2 + tile_cols[0, 0] % 2
    slots = jnp.arange(rows.shape[0], dtype=jnp.int32)
    live = slots < tile_count[0, 0]
    key = jnp.where(live, rank // 2, len(ORDER)) * rows.shape[0] + slots
    position = jnp.sum((key[None, :] < key[:, None]).astype(jnp.int32), axis=1)
    chosen = position[None, :] == slots[:, None]
    order, rows, cols = (
        jnp.sum(jnp.where(chosen, a[None, :], 0), axis=1) for a in (slots, rows, cols)
    )
    groups = jnp.arange(16, dtype=jnp.int32)
    starts = jnp.sum((key[None, :] < groups[:, None] * rows.shape[0]).astype(jnp.int32), axis=1)
    plan = (starts, order, rows, cols)

    tiles = tile_vals[0, 0]
    vals = call(
        load_body,
        "load_tiles",
        jax.ShapeDtypeStruct(tiles.shape, BF16),
        (tiles,),
        scratch=(pltpu.SemaphoreType.DMA,),
        moved=2 * tiles.size * 2,
        specs=[pl.BlockSpec(memory_space=pltpu.HBM)],
    )
    gathered = {(0, 0): feats, (0, 1): to_core(feats)}
    steps = (1, -1, 2)
    arrived = [to_y(feats, step) for step in steps]
    arrived, vals, plan = lax.optimization_barrier((arrived, vals, plan))
    for step, block in zip(steps, arrived):
        gathered[(-step) % NY, 0] = block
        gathered[(-step) % NY, 1] = to_core(block)
    source = call(
        collect_body,
        "collect",
        jax.ShapeDtypeStruct((16, TILE, 256), BF16),
        tuple(gathered[k // 2, k % 2] for k in range(8)),
        moved=2**21,
    )

    one, two = shape(shard, F32), jax.ShapeDtypeStruct((2, shard, 256), F32)
    one16, two16 = shape(shard, BF16), jax.ShapeDtypeStruct((2, shard, 256), BF16)
    half = shape(144, BF16)

    def forward(begin, end, outs, source):
        return call(
            functools.partial(forward_body, begin, end),
            f"forward_{begin}",
            outs,
            (*plan, vals, source),
            scalars=4,
            scratch=(pltpu.VMEM((4 * (end - begin) + 1, TILE, 256), F32),),
        )

    def relay(body, name, outs, *args):
        return call(body, name, outs, args, moved=2**20)

    barrier = lax.optimization_barrier
    (moving,) = forward(6, 8, (jax.ShapeDtypeStruct((4, shard, 256), BF16),), source)
    moving, source = barrier((moving, source))
    moving = swap_z(moving, -1)
    kept_b, side_b, side_c = forward(3, 6, (two, two, two16), source)
    side_c = swap_z(side_c, -1)
    moving, side = relay(relay_first_body, "relay_b", (two16, two16), kept_b, side_b, moving)
    moving, side, source = barrier((moving, side, source))
    side, moving = swap_z(side, 1, 1), swap_z(moving, 1)
    kept_c, side_d = forward(1, 3, (two, two), source)
    side_d = relay(relay_body, "relay_side", two16, side_d, side_c)
    side_d = to_x(side_d)
    moving = relay(relay_body, "relay_c", two16, kept_c, moving, side)
    moving, source = barrier((moving, source))
    moving = swap_z(moving, -1)
    (kept_d,) = forward(0, 1, (two,), source)
    own, moving = relay(relay_last_body, "relay_last", (one, one16), kept_d, side_d, moving)
    moving = swap_z(moving, 1)
    hidden_out, grad, high, low = call(
        activate_body,
        "activate",
        (one16, one16, one16, one16),
        (own, moving, weight, bias[None, :], grad_out),
        flops=4 * 256**3,
        moved=2 * 2**20,
    )

    def backward(begin, blocks, before, outs):
        end = begin + len(blocks)
        return call(
            functools.partial(backward_body, begin, end),
            f"backward_{begin}",
            outs,
            (*plan, vals, *blocks, *before),
            scalars=4,
            scratch=(pltpu.VMEM((4 * len(blocks), TILE, 256), BF16),)
            + ((pltpu.VMEM((17, TILE, 256), F32),) if end == len(ORDER) else ()),
        )

    running = jax.ShapeDtypeStruct((17, TILE, 256), F32)
    terms, sent = call(
        terms_body,
        "weight_terms",
        (half, half),
        (core[None], high, low, grad),
        scalars=1,
        scratch=(pltpu.VMEM((256, 256), F32),),
        flops=4 * 256**3,
        moved=2**20,
    )
    message = shape(656, BF16)
    own_grad = call(
        pack_own_body, "pack_own", shape(400, BF16), (grad, terms, to_core(sent)), moved=2**19
    )
    first = swap_z(own_grad, 1)
    pair_d = call(pack_pair_body, "pack_pair", message, (own_grad, first), moved=2**20)
    pair_c, side_d = swap_z(pair_d, -1), to_x(pair_d)
    total = backward(0, (pair_d,), (), running)
    pair_c, side_d, total = barrier((pair_c, side_d, total))
    side_b, pair_b, side_c = swap_z(pair_c, 1, 1), swap_z(pair_c, 1), swap_z(side_d, -1)
    total = backward(1, (pair_c, side_d), (total,), running)
    pair_b, side_b, total = barrier((pair_b, side_b, total))
    pair_a, side_a = swap_z(pair_b, -1), swap_z(side_b, -1)
    total = backward(3, (pair_b, side_b), (total,), running)
    pair_a, side_c, total = barrier((pair_a, side_c, total))
    total = backward(5, (side_c, pair_a), (total,), running)
    side_a, total = barrier((side_a, total))
    own, kept, over = backward(
        7,
        (side_a,),
        (total,),
        (
            one,
            jax.ShapeDtypeStruct((3, shard, 256), F32),
            jax.ShapeDtypeStruct((4, shard, 256), BF16),
        ),
    )
    over = to_core(over)
    *sends, terms = call(
        back_relay_body,
        "back_relay",
        (*[shape(400, BF16)] * 3, half),
        (kept, over, pair_d, pair_a, pair_c, pair_b, side_d, side_a, side_c, side_b),
        moved=2 * 2**20,
    )
    got = [to_y(a, s) for a, s in zip(sends, (1, 2, 3))]
    mine = call(
        functools.partial(sum_terms_body, scale),
        "sum_terms",
        shape(136, F32),
        (terms, *got),
        moved=2**19,
    )
    other = to_core(mine)
    grad_feats = call(
        finish_body,
        "finish",
        one16,
        (own, over, *got, weight),
        flops=2 * 256**3,
        moved=2 * 2**20,
    )
    grad_weight, grad_bias = call(
        assemble_body,
        "assemble",
        (shape(256, F32), shape(1, F32)),
        (core[None], mine, other),
        scalars=1,
        moved=2**19,
    )
    return (hidden_out, grad_feats, grad_weight, grad_bias.reshape(256))


def solution(mesh):
    in_specs = (
        P(("slab", "col", "row"), None),
        P(),
        P(),
        P(("slab", "row", "col"), None),
        P(("slab", "row"), "col", None, None, None),
        P(("slab", "row"), "col", None),
        P(("slab", "row"), "col", None),
        P(("slab", "row"), "col"),
    )
    out_specs = (
        P(("slab", "row", "col"), None),
        P(("slab", "col", "row"), None),
        P("slab", None),
        P("slab"),
    )
    return jax.shard_map(
        per_device, mesh=mesh, in_specs=in_specs, out_specs=out_specs, check_vma=False
    )
```

```python
import functools
import math

import jax
import jax.numpy as jnp
from jax import lax
from jax.experimental import pallas as pl
from jax.experimental.pallas import tpu as pltpu
from jax.sharding import PartitionSpec as P

TILE = 128
UNROLL = 16
ORDER = (
    ((0, 0), (1, 0)),
    ((7, 0), (6, 0)),
    ((0, 1), (1, 1)),
    ((2, 0), (3, 0)),
    ((7, 1), (6, 1)),
    ((2, 1), (3, 1)),
    ((5, 0), (4, 0)),
    ((5, 1), (4, 1)),
)
NY = 4
NZ = 8
F32 = jnp.float32
BF16 = jnp.bfloat16
LIMIT = pltpu.CompilerParams(vmem_limit_bytes=32 * 2**20)


def vmem():
    return pl.BlockSpec(memory_space=pltpu.VMEM)


def smem():
    return pl.BlockSpec(memory_space=pltpu.SMEM)


def shape(rows, dtype):
    return jax.ShapeDtypeStruct((rows, 256), dtype)


def call(body, name, out_shape, args, scalars=0, scratch=(), flops=0, moved=0, specs=None):
    return pl.pallas_call(
        body,
        name=name,
        out_shape=out_shape,
        in_specs=specs or [smem()] * scalars + [vmem()] * (len(args) - scalars),
        out_specs=jax.tree.map(lambda _: vmem(), out_shape),
        scratch_shapes=scratch,
        compiler_params=LIMIT,
        cost_estimate=pl.CostEstimate(flops=flops, bytes_accessed=moved, transcendentals=0),
    )(*args)


def to_core(a):
    return lax.ppermute(a, "row", [(i, i ^ 1) for i in range(2 * NY)])


def to_y(a, step):
    return lax.ppermute(a, "row", [(i, (i + 2 * step) % (2 * NY)) for i in range(2 * NY)])


def to_x(a):
    return lax.ppermute(a, "col", [(i, i ^ 1) for i in range(2 * NZ)])


def swap_z(a, side, across=0):
    pairs = []
    for row in range(2 * NY):
        for col in range(2 * NZ):
            z, x = divmod(col, 2)
            step = side if (z + row) % 2 == 0 else -side
            to = (z + step) % NZ * 2 + (x + across) % 2
            pairs.append((row * 2 * NZ + col, row * 2 * NZ + to))
    return lax.ppermute(a, ("row", "col"), pairs)


def load_body(source, out, sem):
    copy = pltpu.make_async_copy(source, out, sem)
    copy.start()
    copy.wait()


def collect_body(*refs):
    blocks, out = refs[:-1], refs[-1]
    for k, block in enumerate(blocks):
        for half in range(2):
            out[2 * k + half] = block[half * TILE : (half + 1) * TILE]


def place(ref, total, first, dtype):
    for half in range(2):
        ref[half * TILE : (half + 1) * TILE] = total[2 * first + half].astype(dtype)


def add_tiles(begin, end, starts, order, to_slot, product, total, dummy):
    first, last = starts[begin], starts[end]

    def batch(i, carry):
        slots = [first + i * UNROLL + u for u in range(UNROLL)]
        safe = [jnp.minimum(t, 191) for t in slots]
        terms = [product(order[t], t) for t in safe]
        for slot, t, term in zip(slots, safe, terms):
            place_at = jnp.where(slot < last, to_slot(t), dummy)
            total[place_at] = total[place_at] + term
        return carry

    lax.fori_loop(0, (last - first + UNROLL - 1) // UNROLL, batch, 0)


def forward_body(begin, end, starts, order, rows, cols, vals, source, *rest):
    outs, total = rest[:-1], rest[-1]
    size = 4 * (end - begin)
    total[...] = jnp.zeros_like(total)
    add_tiles(
        begin,
        end,
        starts,
        order,
        lambda t: jnp.clip(rows[t] - 4 * begin, 0, size - 1),
        lambda tile, t: jnp.dot(vals[tile], source[cols[t]], preferred_element_type=F32),
        total,
        size,
    )
    first = 0
    for out in outs:
        for n in range(out.shape[0]):
            place(out.at[n], total, first + n, out.dtype)
        first += out.shape[0]


def wide(ref):
    return ref[...].astype(F32)


def relay_first_body(kept, side, got, out, out_side):
    out[...] = (kept[...] + wide(got.at[0:2])).astype(BF16)
    out_side[...] = (side[...] + wide(got.at[2:4])).astype(BF16)


def relay_body(kept, *rest):
    total = kept[...]
    for ref in rest[:-1]:
        total = total + wide(ref)
    rest[-1][...] = total.astype(BF16)


def relay_last_body(kept, got, own, out):
    own[...] = kept[0] + wide(got.at[0])
    out[...] = (kept[1] + wide(got.at[1])).astype(BF16)


def activate_body(own, got, near, side, weight, bias, given, hidden, grad, high, low):
    summed = own[...] + wide(got) + wide(near) + wide(side)
    top = summed.astype(BF16)
    rest = (summed - top.astype(F32)).astype(BF16)
    high[...] = top
    low[...] = rest
    pre_act = (
        jnp.dot(top, weight[...], preferred_element_type=F32)
        + jnp.dot(rest, weight[...], preferred_element_type=F32)
        + bias[...]
    )
    gate_value = jax.nn.sigmoid(pre_act)
    hidden[...] = (pre_act * gate_value).astype(BF16)
    slope = gate_value * (1.0 + pre_act * (1.0 - gate_value))
    grad[...] = (given[...].astype(F32) * slope).astype(BF16)


def terms_body(core, high, low, grad, kept, sent, whole):
    g = grad[...]
    dims = (((0,), (0,)), ((), ()))
    whole[...] = lax.dot_general(high[...], g, dims, preferred_element_type=F32) + lax.dot_general(
        low[...], g, dims, preferred_element_type=F32
    )
    column = jnp.sum(g.astype(F32), axis=0, keepdims=True)
    for ref, half in ((kept, core[0]), (sent, 1 - core[0])):
        ref[0:128] = whole[pl.ds(pl.multiple_of(half * 128, 128), 128)].astype(BF16)
        ref[128:144] = jnp.broadcast_to(column, (16, 256)).astype(BF16)


def add_rows(a, b):
    return (a.astype(F32) + b.astype(F32)).astype(BF16)


def pack_own_body(grad, mine, other, out):
    out[0:256] = grad[...]
    out[256:400] = add_rows(mine[...], other[...])


def pack_pair_body(own, got, out):
    out[0:256] = own[0:256]
    out[256:512] = got[0:256]
    out[512:656] = add_rows(own[256:400], got[256:400])


def backward_body(begin, end, starts, order, rows, cols, vals, *rest):
    blocks, rest = rest[: end - begin], rest[end - begin :]
    if begin:
        before, rest = rest[0], rest[1:]
    if end == len(ORDER):
        own, kept, over, source, total = rest
    else:
        total, source = rest
    n = 0
    for block in blocks:
        for k in range(4):
            source[n] = block[k * TILE : (k + 1) * TILE]
            n += 1
    if begin:
        total[...] = before[...]
    else:
        total[...] = jnp.zeros_like(total)
    add_tiles(
        begin,
        end,
        starts,
        order,
        lambda t: cols[t],
        lambda tile, t: lax.dot_general(
            vals[tile],
            source[jnp.clip(rows[t] - 4 * begin, 0, n - 1)],
            (((0,), (0,)), ((), ())),
            preferred_element_type=F32,
        ),
        total,
        16,
    )
    if end == len(ORDER):
        place(own, total, 0, F32)
        for k, dy in enumerate((1, 2, 3)):
            place(kept.at[k], total, 2 * dy, F32)
            place(over.at[k], total, 2 * dy + 1, BF16)
        place(over.at[3], total, 1, BF16)


def back_relay_body(kept, over, pd, pa, pc, pb, sd, sa, sc, sb, out_a, out_b, out_c, terms):
    sums = slice(512, 656)
    plane = add_rows(pd[sums], pa[sums]).astype(F32) + add_rows(pc[sums], pb[sums]).astype(F32)
    other = add_rows(sd[sums], sa[sums]).astype(F32) + add_rows(sc[sums], sb[sums]).astype(F32)
    terms[...] = (plane + other).astype(BF16)
    for k, out in enumerate((out_a, out_b, out_c)):
        out[0:256] = (kept[k] + over[k].astype(F32)).astype(BF16)
        out[256:400] = terms[...]


def sum_terms_body(scale, own, a, b, c, out):
    total = (wide(own) + b[256:400].astype(F32)) + (
        a[256:400].astype(F32) + c[256:400].astype(F32)
    )
    out[...] = total[0:136] * scale


def finish_body(own, over, a, b, c, weight, out):
    back = own[...] + over[3].astype(F32)
    for ref in (a, b, c):
        back = back + ref[0:256].astype(F32)
    out[...] = lax.dot_general(
        back.astype(BF16), weight[...], (((1,), (1,)), ((), ())), preferred_element_type=F32
    ).astype(BF16)


def assemble_body(core, mine, other, weight, bias):
    for ref, half in ((mine, core[0]), (other, 1 - core[0])):
        weight[pl.ds(pl.multiple_of(half * 128, 128), 128)] = ref[0:128]
    bias[...] = mine[128:129]


def per_device(feats, weight, bias, grad_out, tile_vals, tile_rows, tile_cols, tile_count):
    shard = feats.shape[0]
    scale = 1.0 / math.sqrt(shard * 2 * NY * 2 * NZ)
    row, col = lax.axis_index("row"), lax.axis_index("col")
    y, core, z, x = row // 2, row % 2, col // 2, col % 2
    owner_row, owner_col = tile_rows[0, 0] // 2, tile_cols[0, 0] // 2
    toward = 1 - 2 * ((z + core) % 2)
    where = (owner_row // 2 - z) * toward % NZ * 2 + (owner_row + x) % 2
    ranks = [0] * (2 * NZ)
    for rank, (dz, dx) in enumerate(sum(ORDER, ())):
        ranks[dz * 2 + dx] = rank
    rank = sum(jnp.where(where == k, r, 0) for k, r in enumerate(ranks))
    rows = rank * 2 + tile_rows[0, 0] % 2
    rel_y = (owner_col // 2 - y) % NY
    cols = (rel_y * 2 + (owner_col + core) % 2) * 2 + tile_cols[0, 0] % 2
    slots = jnp.arange(rows.shape[0], dtype=jnp.int32)
    live = slots < tile_count[0, 0]
    key = jnp.where(live, rank // 2, len(ORDER)) * rows.shape[0] + slots
    position = jnp.sum((key[None, :] < key[:, None]).astype(jnp.int32), axis=1)
    chosen = position[None, :] == slots[:, None]
    order, rows, cols = (
        jnp.sum(jnp.where(chosen, a[None, :], 0), axis=1) for a in (slots, rows, cols)
    )
    groups = jnp.arange(16, dtype=jnp.int32)
    starts = jnp.sum((key[None, :] < groups[:, None] * rows.shape[0]).astype(jnp.int32), axis=1)
    plan = (starts, order, rows, cols)

    tiles = tile_vals[0, 0]
    vals = call(
        load_body,
        "load_tiles",
        jax.ShapeDtypeStruct(tiles.shape, BF16),
        (tiles,),
        scratch=(pltpu.SemaphoreType.DMA,),
        moved=2 * tiles.size * 2,
        specs=[pl.BlockSpec(memory_space=pltpu.HBM)],
    )
    gathered = {(0, 0): feats, (0, 1): to_core(feats)}
    steps = (1, -1, 2)
    arrived = [to_y(feats, step) for step in steps]
    arrived, vals, plan = lax.optimization_barrier((arrived, vals, plan))
    for step, block in zip(steps, arrived):
        gathered[(-step) % NY, 0] = block
        gathered[(-step) % NY, 1] = to_core(block)
    source = call(
        collect_body,
        "collect",
        jax.ShapeDtypeStruct((16, TILE, 256), BF16),
        tuple(gathered[k // 2, k % 2] for k in range(8)),
        moved=2**21,
    )

    one, two = shape(shard, F32), jax.ShapeDtypeStruct((2, shard, 256), F32)
    one16, two16 = shape(shard, BF16), jax.ShapeDtypeStruct((2, shard, 256), BF16)
    half = shape(144, BF16)

    def forward(begin, end, outs, source):
        return call(
            functools.partial(forward_body, begin, end),
            f"forward_{begin}",
            outs,
            (*plan, vals, source),
            scalars=4,
            scratch=(pltpu.VMEM((4 * (end - begin) + 1, TILE, 256), F32),),
        )

    def relay(body, name, outs, *args):
        return call(body, name, outs, args, moved=2**20)

    barrier = lax.optimization_barrier
    (moving,) = forward(6, 8, (jax.ShapeDtypeStruct((4, shard, 256), BF16),), source)
    moving, source = barrier((moving, source))
    moving = swap_z(moving, -1)
    kept_b, side_c, side_b = forward(3, 6, (two, two16, two), source)
    side_c = swap_z(side_c, -1)
    moving, side = relay(relay_first_body, "relay_b", (two16, two16), kept_b, side_b, moving)
    moving, side, source = barrier((moving, side, source))
    side, moving = swap_z(side, 1, 1), swap_z(moving, 1)
    kept_c, side_d = forward(1, 3, (two, two), source)
    side_d = relay(relay_body, "relay_side", two16, side_d, side_c)
    moving = relay(relay_body, "relay_c", two16, kept_c, moving, side)
    moving, source, side_d = barrier((moving, source, side_d))
    moving, near, side = swap_z(moving, -1), to_x(side_d[0]), swap_z(side_d[1], 1, 1)
    (kept_d,) = forward(0, 1, (two,), source)
    own, moving = relay(relay_last_body, "relay_last", (one, one16), kept_d, moving)
    moving = swap_z(moving, 1)
    hidden_out, grad, high, low = call(
        activate_body,
        "activate",
        (one16, one16, one16, one16),
        (own, moving, near, side, weight, bias[None, :], grad_out),
        flops=4 * 256**3,
        moved=2 * 2**20,
    )

    def backward(begin, blocks, before, outs):
        end = begin + len(blocks)
        return call(
            functools.partial(backward_body, begin, end),
            f"backward_{begin}",
            outs,
            (*plan, vals, *blocks, *before),
            scalars=4,
            scratch=(pltpu.VMEM((4 * len(blocks), TILE, 256), BF16),)
            + ((pltpu.VMEM((17, TILE, 256), F32),) if end == len(ORDER) else ()),
        )

    running = jax.ShapeDtypeStruct((17, TILE, 256), F32)
    terms, sent = call(
        terms_body,
        "weight_terms",
        (half, half),
        (core[None], high, low, grad),
        scalars=1,
        scratch=(pltpu.VMEM((256, 256), F32),),
        flops=4 * 256**3,
        moved=2**20,
    )
    message = shape(656, BF16)
    own_grad = call(
        pack_own_body, "pack_own", shape(400, BF16), (grad, terms, to_core(sent)), moved=2**19
    )
    first = swap_z(own_grad, 1)
    pair_d = call(pack_pair_body, "pack_pair", message, (own_grad, first), moved=2**20)
    side_d = to_x(pair_d)
    total = backward(0, (pair_d,), (), running)
    pair_d, total = barrier((pair_d, total))
    pair_c = swap_z(pair_d, -1)
    pair_c, side_d, total = barrier((pair_c, side_d, total))
    pair_b, side_c = swap_z(pair_c, 1), swap_z(side_d, -1)
    total = backward(1, (pair_c, side_d), (total,), running)
    pair_b, side_c, total = barrier((pair_b, side_c, total))
    pair_a, side_b = swap_z(pair_b, -1), swap_z(side_c, 1)
    total = backward(3, (pair_b, side_c), (total,), running)
    pair_a, side_b, total = barrier((pair_a, side_b, total))
    side_a = swap_z(side_b, -1)
    total = backward(5, (side_b, pair_a), (total,), running)
    side_a, total = barrier((side_a, total))
    own, kept, over = backward(
        7,
        (side_a,),
        (total,),
        (
            one,
            jax.ShapeDtypeStruct((3, shard, 256), F32),
            jax.ShapeDtypeStruct((4, shard, 256), BF16),
        ),
    )
    over = to_core(over)
    *sends, terms = call(
        back_relay_body,
        "back_relay",
        (*[shape(400, BF16)] * 3, half),
        (kept, over, pair_d, pair_a, pair_c, pair_b, side_d, side_a, side_c, side_b),
        moved=2 * 2**20,
    )
    got = [to_y(a, s) for a, s in zip(sends, (1, 2, 3))]
    mine = call(
        functools.partial(sum_terms_body, scale),
        "sum_terms",
        shape(136, F32),
        (terms, *got),
        moved=2**19,
    )
    other = to_core(mine)
    grad_feats = call(
        finish_body,
        "finish",
        one16,
        (own, over, *got, weight),
        flops=2 * 256**3,
        moved=2 * 2**20,
    )
    grad_weight, grad_bias = call(
        assemble_body,
        "assemble",
        (shape(256, F32), shape(1, F32)),
        (core[None], mine, other),
        scalars=1,
        moved=2**19,
    )
    return (hidden_out, grad_feats, grad_weight, grad_bias.reshape(256))


def solution(mesh):
    in_specs = (
        P(("slab", "col", "row"), None),
        P(),
        P(),
        P(("slab", "row", "col"), None),
        P(("slab", "row"), "col", None, None, None),
        P(("slab", "row"), "col", None),
        P(("slab", "row"), "col", None),
        P(("slab", "row"), "col"),
    )
    out_specs = (
        P(("slab", "row", "col"), None),
        P(("slab", "col", "row"), None),
        P("slab", None),
        P("slab"),
    )
    return jax.shard_map(
        per_device, mesh=mesh, in_specs=in_specs, out_specs=out_specs, check_vma=False
    )
```

```python
import functools
import math

import jax
import jax.numpy as jnp
from jax import lax
from jax.experimental import pallas as pl
from jax.experimental.pallas import tpu as pltpu
from jax.sharding import PartitionSpec as P

TILE = 128
ORDER = (
    ((0, 0), (1, 0)),
    ((7, 0), (6, 0)),
    ((0, 1), (1, 1)),
    ((2, 0), (3, 0)),
    ((2, 1), (3, 1)),
    ((7, 1), (6, 1)),
    ((5, 0), (4, 0)),
    ((5, 1), (4, 1)),
)
NY = 4
NZ = 8
F32 = jnp.float32
BF16 = jnp.bfloat16
LIMIT = pltpu.CompilerParams(vmem_limit_bytes=32 * 2**20)


def vmem():
    return pl.BlockSpec(memory_space=pltpu.VMEM)


def smem():
    return pl.BlockSpec(memory_space=pltpu.SMEM)


def shape(rows, dtype):
    return jax.ShapeDtypeStruct((rows, 256), dtype)


def call(body, name, out_shape, args, scalars=0, scratch=(), flops=0, moved=0, specs=None):
    return pl.pallas_call(
        body,
        name=name,
        out_shape=out_shape,
        in_specs=specs or [smem()] * scalars + [vmem()] * (len(args) - scalars),
        out_specs=jax.tree.map(lambda _: vmem(), out_shape),
        scratch_shapes=scratch,
        compiler_params=LIMIT,
        cost_estimate=pl.CostEstimate(flops=flops, bytes_accessed=moved, transcendentals=0),
    )(*args)


def to_core(a):
    return lax.ppermute(a, "row", [(i, i ^ 1) for i in range(2 * NY)])


def to_y(a, step):
    return lax.ppermute(a, "row", [(i, (i + 2 * step) % (2 * NY)) for i in range(2 * NY)])


def to_x(a):
    return lax.ppermute(a, "col", [(i, i ^ 1) for i in range(2 * NZ)])


def swap_z(a, side, across=0):
    pairs = []
    for row in range(2 * NY):
        for col in range(2 * NZ):
            z, x = divmod(col, 2)
            step = side if (z + row) % 2 == 0 else -side
            to = (z + step) % NZ * 2 + (x + across) % 2
            pairs.append((row * 2 * NZ + col, row * 2 * NZ + to))
    return lax.ppermute(a, ("row", "col"), pairs)


def load_body(source, out, sem):
    copy = pltpu.make_async_copy(source, out, sem)
    copy.start()
    copy.wait()


def collect_body(*refs):
    blocks, out = refs[:-1], refs[-1]
    for k, block in enumerate(blocks):
        for half in range(2):
            out[2 * k + half] = block[half * TILE : (half + 1) * TILE]


def place(ref, total, first, dtype):
    for half in range(2):
        ref[half * TILE : (half + 1) * TILE] = total[2 * first + half].astype(dtype)


def add_tiles(begin, end, starts, order, to_slot, product, total, dummy):
    first, last = starts[begin], starts[end]

    def step(start, count):
        slots = [start + u for u in range(count)]
        safe = [jnp.minimum(t, 191) for t in slots]
        terms = [product(order[t], t) for t in safe]
        for slot, t, term in zip(slots, safe, terms):
            place_at = jnp.where(slot < last, to_slot(t), dummy)
            total[place_at] = total[place_at] + term

    size = last - first
    full = (size + 7) // 16

    def batch(i, carry):
        step(first + 16 * i, 16)
        return carry

    lax.fori_loop(0, full, batch, 0)

    @pl.when(16 * full < size)
    def _():
        step(first + 16 * full, 8)


def forward_body(begin, end, starts, order, rows, cols, vals, source, *rest):
    outs, total = rest[:-1], rest[-1]
    size = 4 * (end - begin)
    total[...] = jnp.zeros_like(total)
    add_tiles(
        begin,
        end,
        starts,
        order,
        lambda t: jnp.clip(rows[t] - 4 * begin, 0, size - 1),
        lambda tile, t: jnp.dot(vals[tile], source[cols[t]], preferred_element_type=F32),
        total,
        size,
    )
    first = 0
    for out in outs:
        for n in range(out.shape[0]):
            place(out.at[n], total, first + n, out.dtype)
        first += out.shape[0]


def wide(ref):
    return ref[...].astype(F32)


def relay_first_body(kept, side, got, out, out_side):
    out[...] = (kept[...] + wide(got.at[0:2])).astype(BF16)
    out_side[...] = (side[...] + wide(got.at[2:4])).astype(BF16)


def relay_body(kept, *rest):
    total = kept[...]
    for ref in rest[:-1]:
        total = total + wide(ref)
    rest[-1][...] = total.astype(BF16)


def relay_last_body(kept, over, got, own, out):
    own[...] = kept[0] + wide(over.at[0]) + wide(got.at[0])
    out[...] = (kept[1] + wide(over.at[1]) + wide(got.at[1])).astype(BF16)


def activate_body(own, got, weight, bias, given, hidden, grad, high, low):
    summed = own[...] + wide(got)
    top = summed.astype(BF16)
    rest = (summed - top.astype(F32)).astype(BF16)
    high[...] = top
    low[...] = rest
    pre_act = (
        jnp.dot(top, weight[...], preferred_element_type=F32)
        + jnp.dot(rest, weight[...], preferred_element_type=F32)
        + bias[...]
    )
    gate_value = jax.nn.sigmoid(pre_act)
    hidden[...] = (pre_act * gate_value).astype(BF16)
    slope = gate_value * (1.0 + pre_act * (1.0 - gate_value))
    grad[...] = (given[...].astype(F32) * slope).astype(BF16)


def terms_body(core, high, low, grad, kept, sent, whole):
    g = grad[...]
    dims = (((0,), (0,)), ((), ()))
    whole[...] = lax.dot_general(high[...], g, dims, preferred_element_type=F32) + lax.dot_general(
        low[...], g, dims, preferred_element_type=F32
    )
    column = jnp.sum(g.astype(F32), axis=0, keepdims=True)
    for ref, half in ((kept, core[0]), (sent, 1 - core[0])):
        ref[0:128] = whole[pl.ds(pl.multiple_of(half * 128, 128), 128)].astype(BF16)
        ref[128:144] = jnp.broadcast_to(column, (16, 256)).astype(BF16)


def add_rows(a, b):
    return (a.astype(F32) + b.astype(F32)).astype(BF16)


def pack_own_body(grad, mine, other, out):
    out[0:256] = grad[...]
    out[256:400] = add_rows(mine[...], other[...])


def pack_pair_body(own, got, out):
    out[0:256] = own[0:256]
    out[256:512] = got[0:256]
    out[512:656] = add_rows(own[256:400], got[256:400])


def backward_body(begin, end, starts, order, rows, cols, vals, *rest):
    blocks, rest = rest[: end - begin], rest[end - begin :]
    if begin:
        before, rest = rest[0], rest[1:]
    if end == len(ORDER):
        own, kept, over, source, total = rest
    else:
        total, source = rest
    n = 0
    for block in blocks:
        for k in range(4):
            source[n] = block[k * TILE : (k + 1) * TILE]
            n += 1
    if begin:
        total[...] = before[...]
    else:
        total[...] = jnp.zeros_like(total)
    add_tiles(
        begin,
        end,
        starts,
        order,
        lambda t: cols[t],
        lambda tile, t: lax.dot_general(
            vals[tile],
            source[jnp.clip(rows[t] - 4 * begin, 0, n - 1)],
            (((0,), (0,)), ((), ())),
            preferred_element_type=F32,
        ),
        total,
        16,
    )
    if end == len(ORDER):
        place(own, total, 0, F32)
        for k, dy in enumerate((1, 2, 3)):
            place(kept.at[k], total, 2 * dy, F32)
            place(over.at[k], total, 2 * dy + 1, BF16)
        place(over.at[3], total, 1, BF16)


def plane_terms_body(pd, pa, pc, pb, out):
    sums = slice(512, 656)
    plane = add_rows(pd[sums], pa[sums]).astype(F32) + add_rows(pc[sums], pb[sums]).astype(F32)
    out[...] = plane.astype(BF16)


def back_relay_body(kept, over, plane, other, out_a, out_b, out_c, terms):
    terms[...] = add_rows(plane[...], other[...])
    for k, out in enumerate((out_a, out_b, out_c)):
        out[0:256] = (kept[k] + over[k].astype(F32)).astype(BF16)
        out[256:400] = terms[...]


def sum_terms_body(scale, own, a, b, c, out):
    total = (wide(own) + b[256:400].astype(F32)) + (
        a[256:400].astype(F32) + c[256:400].astype(F32)
    )
    out[...] = total[0:136] * scale


def finish_body(own, over, a, b, c, weight, out):
    back = own[...] + over[3].astype(F32)
    for ref in (a, b, c):
        back = back + ref[0:256].astype(F32)
    out[...] = lax.dot_general(
        back.astype(BF16), weight[...], (((1,), (1,)), ((), ())), preferred_element_type=F32
    ).astype(BF16)


def assemble_body(core, mine, other, weight, bias):
    for ref, half in ((mine, core[0]), (other, 1 - core[0])):
        weight[pl.ds(pl.multiple_of(half * 128, 128), 128)] = ref[0:128]
    bias[...] = mine[128:129]


def per_device(feats, weight, bias, grad_out, tile_vals, tile_rows, tile_cols, tile_count):
    shard = feats.shape[0]
    scale = 1.0 / math.sqrt(shard * 2 * NY * 2 * NZ)
    row, col = lax.axis_index("row"), lax.axis_index("col")
    y, core, z, x = row // 2, row % 2, col // 2, col % 2
    owner_row, owner_col = tile_rows[0, 0] // 2, tile_cols[0, 0] // 2
    toward = 1 - 2 * ((z + core) % 2)
    where = (owner_row // 2 - z) * toward % NZ * 2 + (owner_row + x) % 2
    ranks = [0] * (2 * NZ)
    for rank, (dz, dx) in enumerate(sum(ORDER, ())):
        ranks[dz * 2 + dx] = rank
    rank = sum(jnp.where(where == k, r, 0) for k, r in enumerate(ranks))
    rows = rank * 2 + tile_rows[0, 0] % 2
    rel_y = (owner_col // 2 - y) % NY
    cols = (rel_y * 2 + (owner_col + core) % 2) * 2 + tile_cols[0, 0] % 2
    slots = jnp.arange(rows.shape[0], dtype=jnp.int32)
    live = slots < tile_count[0, 0]
    key = jnp.where(live, rank // 2, len(ORDER)) * rows.shape[0] + slots
    position = jnp.sum((key[None, :] < key[:, None]).astype(jnp.int32), axis=1)
    chosen = position[None, :] == slots[:, None]
    order, rows, cols = (
        jnp.sum(jnp.where(chosen, a[None, :], 0), axis=1) for a in (slots, rows, cols)
    )
    groups = jnp.arange(16, dtype=jnp.int32)
    starts = jnp.sum((key[None, :] < groups[:, None] * rows.shape[0]).astype(jnp.int32), axis=1)
    plan = (starts, order, rows, cols)

    tiles = tile_vals[0, 0]
    vals = call(
        load_body,
        "load_tiles",
        jax.ShapeDtypeStruct(tiles.shape, BF16),
        (tiles,),
        scratch=(pltpu.SemaphoreType.DMA,),
        moved=2 * tiles.size * 2,
        specs=[pl.BlockSpec(memory_space=pltpu.HBM)],
    )
    gathered = {(0, 0): feats, (0, 1): to_core(feats)}
    steps = (1, -1, 2)
    arrived = [to_y(feats, step) for step in steps]
    arrived, vals, plan = lax.optimization_barrier((arrived, vals, plan))
    for step, block in zip(steps, arrived):
        gathered[(-step) % NY, 0] = block
        gathered[(-step) % NY, 1] = to_core(block)
    source = call(
        collect_body,
        "collect",
        jax.ShapeDtypeStruct((16, TILE, 256), BF16),
        tuple(gathered[k // 2, k % 2] for k in range(8)),
        moved=2**21,
    )

    one, two = shape(shard, F32), jax.ShapeDtypeStruct((2, shard, 256), F32)
    one16, two16 = shape(shard, BF16), jax.ShapeDtypeStruct((2, shard, 256), BF16)
    half = shape(144, BF16)

    def forward(begin, end, outs, source):
        return call(
            functools.partial(forward_body, begin, end),
            f"forward_{begin}",
            outs,
            (*plan, vals, source),
            scalars=4,
            scratch=(pltpu.VMEM((4 * (end - begin) + 1, TILE, 256), F32),),
        )

    def relay(body, name, outs, *args):
        return call(body, name, outs, args, moved=2**20)

    barrier = lax.optimization_barrier
    (moving,) = forward(6, 8, (jax.ShapeDtypeStruct((4, shard, 256), BF16),), source)
    moving, source = barrier((moving, source))
    moving = swap_z(moving, -1)
    kept_b, side_b, side_c = forward(3, 6, (two, two, two16), source)
    side_c = swap_z(side_c, -1)
    moving, side = relay(relay_first_body, "relay_b", (two16, two16), kept_b, side_b, moving)
    moving, side, source = barrier((moving, side, source))
    side = swap_z(side, 1, 1)
    kept_c, side_d = forward(1, 3, (two, two), source)
    moving, kept_c = barrier((moving, kept_c))
    moving = swap_z(moving, 1)
    side_d = relay(relay_body, "relay_side", two16, side_d, side_c)
    side_d = to_x(side_d)
    moving = relay(relay_body, "relay_c", two16, kept_c, moving, side)
    moving, source = barrier((moving, source))
    moving = swap_z(moving, -1)
    (kept_d,) = forward(0, 1, (two,), source)
    own, moving = relay(relay_last_body, "relay_last", (one, one16), kept_d, side_d, moving)
    moving = swap_z(moving, 1)
    hidden_out, grad, high, low = call(
        activate_body,
        "activate",
        (one16, one16, one16, one16),
        (own, moving, weight, bias[None, :], grad_out),
        flops=4 * 256**3,
        moved=2 * 2**20,
    )

    def backward(begin, blocks, before, outs):
        end = begin + len(blocks)
        return call(
            functools.partial(backward_body, begin, end),
            f"backward_{begin}",
            outs,
            (*plan, vals, *blocks, *before),
            scalars=4,
            scratch=(pltpu.VMEM((4 * len(blocks), TILE, 256), BF16),)
            + ((pltpu.VMEM((17, TILE, 256), F32),) if end == len(ORDER) else ()),
        )

    running = jax.ShapeDtypeStruct((17, TILE, 256), F32)
    terms, sent = call(
        terms_body,
        "weight_terms",
        (half, half),
        (core[None], high, low, grad),
        scalars=1,
        scratch=(pltpu.VMEM((256, 256), F32),),
        flops=4 * 256**3,
        moved=2**20,
    )
    message = shape(656, BF16)
    own_grad = call(
        pack_own_body, "pack_own", shape(400, BF16), (grad, terms, to_core(sent)), moved=2**19
    )
    first = swap_z(own_grad, 1)
    pair_d = call(pack_pair_body, "pack_pair", message, (own_grad, first), moved=2**20)
    pair_c, side_d = swap_z(pair_d, -1), to_x(pair_d[:512])
    total = backward(0, (pair_d,), (), running)
    pair_c, side_d, total = barrier((pair_c, side_d, total))
    side_b, pair_b, side_c = swap_z(pair_c[:512], 1, 1), swap_z(pair_c, 1), swap_z(side_d, -1)
    total = backward(1, (pair_c, side_d), (total,), running)
    pair_b, side_b, total = barrier((pair_b, side_b, total))
    pair_a, side_a = swap_z(pair_b, -1), swap_z(side_b, -1)
    total = backward(3, (pair_b, side_b), (total,), running)
    pair_a, side_c, total = barrier((pair_a, side_c, total))
    plane = call(
        plane_terms_body, "plane_terms", half, (pair_d, pair_a, pair_c, pair_b), moved=2**19
    )
    other = to_x(plane)
    total = backward(5, (side_c, pair_a), (total,), running)
    side_a, total, other = barrier((side_a, total, other))
    own, kept, over = backward(
        7,
        (side_a,),
        (total,),
        (
            one,
            jax.ShapeDtypeStruct((3, shard, 256), F32),
            jax.ShapeDtypeStruct((4, shard, 256), BF16),
        ),
    )
    over = to_core(over)
    *sends, terms = call(
        back_relay_body,
        "back_relay",
        (*[shape(400, BF16)] * 3, half),
        (kept, over, plane, other),
        moved=2 * 2**20,
    )
    got = [to_y(a, s) for a, s in zip(sends, (1, 2, 3))]
    mine = call(
        functools.partial(sum_terms_body, scale),
        "sum_terms",
        shape(136, F32),
        (terms, *got),
        moved=2**19,
    )
    other = to_core(mine)
    grad_feats = call(
        finish_body,
        "finish",
        one16,
        (own, over, *got, weight),
        flops=2 * 256**3,
        moved=2 * 2**20,
    )
    grad_weight, grad_bias = call(
        assemble_body,
        "assemble",
        (shape(256, F32), shape(1, F32)),
        (core[None], mine, other),
        scalars=1,
        moved=2**19,
    )
    return (hidden_out, grad_feats, grad_weight, grad_bias.reshape(256))


def solution(mesh):
    in_specs = (
        P(("slab", "col", "row"), None),
        P(),
        P(),
        P(("slab", "row", "col"), None),
        P(("slab", "row"), "col", None, None, None),
        P(("slab", "row"), "col", None),
        P(("slab", "row"), "col", None),
        P(("slab", "row"), "col"),
    )
    out_specs = (
        P(("slab", "row", "col"), None),
        P(("slab", "col", "row"), None),
        P("slab", None),
        P("slab"),
    )
    return jax.shard_map(
        per_device, mesh=mesh, in_specs=in_specs, out_specs=out_specs, check_vma=False
    )
```

```python
import functools
import math

import jax
import jax.numpy as jnp
from jax import lax
from jax.experimental import pallas as pl
from jax.experimental.pallas import tpu as pltpu
from jax.sharding import PartitionSpec as P

TILE = 128
ORDER = (
    ((0, 0), (1, 0)),
    ((7, 0), (6, 0)),
    ((0, 1), (1, 1)),
    ((2, 0), (3, 0)),
    ((2, 1), (3, 1)),
    ((7, 1), (6, 1)),
    ((5, 0), (4, 0)),
    ((5, 1), (4, 1)),
)
NY = 4
NZ = 8
F32 = jnp.float32
BF16 = jnp.bfloat16
LIMIT = pltpu.CompilerParams(vmem_limit_bytes=32 * 2**20)


def vmem():
    return pl.BlockSpec(memory_space=pltpu.VMEM)


def smem():
    return pl.BlockSpec(memory_space=pltpu.SMEM)


def shape(rows, dtype):
    return jax.ShapeDtypeStruct((rows, 256), dtype)


def call(body, name, out_shape, args, scalars=0, scratch=(), flops=0, moved=0, specs=None):
    return pl.pallas_call(
        body,
        name=name,
        out_shape=out_shape,
        in_specs=specs or [smem()] * scalars + [vmem()] * (len(args) - scalars),
        out_specs=jax.tree.map(lambda _: vmem(), out_shape),
        scratch_shapes=scratch,
        compiler_params=LIMIT,
        cost_estimate=pl.CostEstimate(flops=flops, bytes_accessed=moved, transcendentals=0),
    )(*args)


def to_core(a):
    return lax.ppermute(a, "row", [(i, i ^ 1) for i in range(2 * NY)])


def to_y(a, step):
    return lax.ppermute(a, "row", [(i, (i + 2 * step) % (2 * NY)) for i in range(2 * NY)])


def to_x(a):
    return lax.ppermute(a, "col", [(i, i ^ 1) for i in range(2 * NZ)])


def swap_z(a, side, across=0):
    pairs = []
    for row in range(2 * NY):
        for col in range(2 * NZ):
            z, x = divmod(col, 2)
            step = side if (z + row) % 2 == 0 else -side
            to = (z + step) % NZ * 2 + (x + across) % 2
            pairs.append((row * 2 * NZ + col, row * 2 * NZ + to))
    return lax.ppermute(a, ("row", "col"), pairs)


def load_body(source, out, sem):
    copy = pltpu.make_async_copy(source, out, sem)
    copy.start()
    copy.wait()


def collect_body(*refs):
    blocks, out = refs[:-1], refs[-1]
    for k, block in enumerate(blocks):
        for half in range(2):
            out[2 * k + half] = block[half * TILE : (half + 1) * TILE]


def place(ref, total, first, dtype):
    for half in range(2):
        ref[half * TILE : (half + 1) * TILE] = total[2 * first + half].astype(dtype)


def add_tiles(begin, end, starts, order, to_slot, product, total, dummy):
    first, last = starts[begin], starts[end]

    def step(start, count):
        slots = [start + u for u in range(count)]
        safe = [jnp.minimum(t, 191) for t in slots]
        terms = [product(order[t], t) for t in safe]
        for slot, t, term in zip(slots, safe, terms):
            place_at = jnp.where(slot < last, to_slot(t), dummy)
            total[place_at] = total[place_at] + term

    size = last - first
    full = (size + 7) // 16

    def batch(i, carry):
        step(first + 16 * i, 16)
        return carry

    lax.fori_loop(0, full, batch, 0)

    @pl.when(16 * full < size)
    def _():
        step(first + 16 * full, 8)


def forward_body(begin, end, starts, order, rows, cols, vals, source, *rest):
    outs, total = rest[:-1], rest[-1]
    size = 4 * (end - begin)
    total[...] = jnp.zeros_like(total)
    add_tiles(
        begin,
        end,
        starts,
        order,
        lambda t: jnp.clip(rows[t] - 4 * begin, 0, size - 1),
        lambda tile, t: jnp.dot(vals[tile], source[cols[t]], preferred_element_type=F32),
        total,
        size,
    )
    first = 0
    for out in outs:
        for n in range(out.shape[0]):
            place(out.at[n], total, first + n, out.dtype)
        first += out.shape[0]


def wide(ref):
    return ref[...].astype(F32)


def relay_first_body(kept, side, got, out, out_side):
    out[...] = (kept[...] + wide(got.at[0:2])).astype(BF16)
    out_side[...] = (side[...] + wide(got.at[2:4])).astype(BF16)


def relay_body(kept, *rest):
    total = kept[...]
    for ref in rest[:-1]:
        total = total + wide(ref)
    rest[-1][...] = total.astype(BF16)


def relay_last_body(kept, over, got, own, out):
    own[...] = kept[0] + wide(over.at[0]) + wide(got.at[0])
    out[...] = (kept[1] + wide(over.at[1]) + wide(got.at[1])).astype(BF16)


def activate_body(own, got, weight, bias, given, hidden, grad, high, low):
    summed = own[...] + wide(got)
    top = summed.astype(BF16)
    rest = (summed - top.astype(F32)).astype(BF16)
    high[...] = top
    low[...] = rest
    pre_act = (
        jnp.dot(top, weight[...], preferred_element_type=F32)
        + jnp.dot(rest, weight[...], preferred_element_type=F32)
        + bias[...]
    )
    gate_value = jax.nn.sigmoid(pre_act)
    hidden[...] = (pre_act * gate_value).astype(BF16)
    slope = gate_value * (1.0 + pre_act * (1.0 - gate_value))
    grad[...] = (given[...].astype(F32) * slope).astype(BF16)


def terms_body(core, high, low, grad, kept, sent, whole):
    g = grad[...]
    dims = (((0,), (0,)), ((), ()))
    whole[...] = lax.dot_general(high[...], g, dims, preferred_element_type=F32) + lax.dot_general(
        low[...], g, dims, preferred_element_type=F32
    )
    column = jnp.sum(g.astype(F32), axis=0, keepdims=True)
    for ref, half in ((kept, core[0]), (sent, 1 - core[0])):
        ref[0:128] = whole[pl.ds(pl.multiple_of(half * 128, 128), 128)].astype(BF16)
        ref[128:144] = jnp.broadcast_to(column, (16, 256)).astype(BF16)


def add_rows(a, b):
    return (a.astype(F32) + b.astype(F32)).astype(BF16)


def pack_own_body(grad, mine, other, out):
    out[0:256] = grad[...]
    out[256:400] = add_rows(mine[...], other[...])


def pack_pair_body(own, got, out):
    out[0:256] = own[0:256]
    out[256:512] = got[0:256]
    out[512:656] = add_rows(own[256:400], got[256:400])


def backward_body(begin, end, starts, order, rows, cols, vals, *rest):
    blocks, rest = rest[: end - begin], rest[end - begin :]
    if begin:
        before, rest = rest[0], rest[1:]
    if end == len(ORDER):
        own, kept, over, source, total = rest
    else:
        total, source = rest
    n = 0
    for block in blocks:
        for k in range(4):
            source[n] = block[k * TILE : (k + 1) * TILE]
            n += 1
    if begin:
        total[...] = before[...]
    else:
        total[...] = jnp.zeros_like(total)
    add_tiles(
        begin,
        end,
        starts,
        order,
        lambda t: cols[t],
        lambda tile, t: lax.dot_general(
            vals[tile],
            source[jnp.clip(rows[t] - 4 * begin, 0, n - 1)],
            (((0,), (0,)), ((), ())),
            preferred_element_type=F32,
        ),
        total,
        16,
    )
    if end == len(ORDER):
        place(own, total, 0, F32)
        for k, dy in enumerate((1, 2, 3)):
            place(kept.at[k], total, 2 * dy, F32)
            place(over.at[k], total, 2 * dy + 1, BF16)
        place(over.at[3], total, 1, BF16)


def plane_terms_body(pd, pa, pc, pb, out):
    sums = slice(512, 656)
    plane = add_rows(pd[sums], pa[sums]).astype(F32) + add_rows(pc[sums], pb[sums]).astype(F32)
    out[...] = plane.astype(BF16)


def back_relay_body(kept, over, plane, other, out_a, out_b, out_c, terms):
    terms[...] = add_rows(plane[...], other[...])
    for k, out in enumerate((out_a, out_b, out_c)):
        out[0:256] = (kept[k] + over[k].astype(F32)).astype(BF16)
        out[256:400] = terms[...]


def sum_terms_body(scale, own, a, b, c, out):
    total = (wide(own) + b[256:400].astype(F32)) + (
        a[256:400].astype(F32) + c[256:400].astype(F32)
    )
    out[...] = total[0:136] * scale


def finish_body(own, over, a, b, c, weight, out):
    back = own[...] + over[3].astype(F32)
    for ref in (a, b, c):
        back = back + ref[0:256].astype(F32)
    out[...] = lax.dot_general(
        back.astype(BF16), weight[...], (((1,), (1,)), ((), ())), preferred_element_type=F32
    ).astype(BF16)


def assemble_body(core, mine, other, weight, bias):
    for ref, half in ((mine, core[0]), (other, 1 - core[0])):
        weight[pl.ds(pl.multiple_of(half * 128, 128), 128)] = ref[0:128]
    bias[...] = mine[128:129]


def per_device(feats, weight, bias, grad_out, tile_vals, tile_rows, tile_cols, tile_count):
    shard = feats.shape[0]
    scale = 1.0 / math.sqrt(shard * 2 * NY * 2 * NZ)
    row, col = lax.axis_index("row"), lax.axis_index("col")
    y, core, z, x = row // 2, row % 2, col // 2, col % 2
    owner_row, owner_col = tile_rows[0, 0] // 2, tile_cols[0, 0] // 2
    toward = 1 - 2 * ((z + core) % 2)
    where = (owner_row // 2 - z) * toward % NZ * 2 + (owner_row + x) % 2
    ranks = [0] * (2 * NZ)
    for rank, (dz, dx) in enumerate(sum(ORDER, ())):
        ranks[dz * 2 + dx] = rank
    rank = sum(jnp.where(where == k, r, 0) for k, r in enumerate(ranks))
    rows = rank * 2 + tile_rows[0, 0] % 2
    rel_y = (owner_col // 2 - y) % NY
    cols = (rel_y * 2 + (owner_col + core) % 2) * 2 + tile_cols[0, 0] % 2
    slots = jnp.arange(rows.shape[0], dtype=jnp.int32)
    live = slots < tile_count[0, 0]
    key = jnp.where(live, rank // 2, len(ORDER)) * rows.shape[0] + slots
    position = jnp.sum((key[None, :] < key[:, None]).astype(jnp.int32), axis=1)
    chosen = position[None, :] == slots[:, None]
    order, rows, cols = (
        jnp.sum(jnp.where(chosen, a[None, :], 0), axis=1) for a in (slots, rows, cols)
    )
    groups = jnp.arange(16, dtype=jnp.int32)
    starts = jnp.sum((key[None, :] < groups[:, None] * rows.shape[0]).astype(jnp.int32), axis=1)
    plan = (starts, order, rows, cols)

    tiles = tile_vals[0, 0]
    vals = call(
        load_body,
        "load_tiles",
        jax.ShapeDtypeStruct(tiles.shape, BF16),
        (tiles,),
        scratch=(pltpu.SemaphoreType.DMA,),
        moved=2 * tiles.size * 2,
        specs=[pl.BlockSpec(memory_space=pltpu.HBM)],
    )
    gathered = {(0, 0): feats, (0, 1): to_core(feats)}
    steps = (1, -1, 2)
    arrived = [to_y(feats, step) for step in steps]
    arrived, vals, plan = lax.optimization_barrier((arrived, vals, plan))
    for step, block in zip(steps, arrived):
        gathered[(-step) % NY, 0] = block
        gathered[(-step) % NY, 1] = to_core(block)
    source = call(
        collect_body,
        "collect",
        jax.ShapeDtypeStruct((16, TILE, 256), BF16),
        tuple(gathered[k // 2, k % 2] for k in range(8)),
        moved=2**21,
    )

    one, two = shape(shard, F32), jax.ShapeDtypeStruct((2, shard, 256), F32)
    one16, two16 = shape(shard, BF16), jax.ShapeDtypeStruct((2, shard, 256), BF16)
    half = shape(144, BF16)

    def forward(begin, end, outs, source):
        return call(
            functools.partial(forward_body, begin, end),
            f"forward_{begin}",
            outs,
            (*plan, vals, source),
            scalars=4,
            scratch=(pltpu.VMEM((4 * (end - begin) + 1, TILE, 256), F32),),
        )

    def relay(body, name, outs, *args):
        return call(body, name, outs, args, moved=2**20)

    barrier = lax.optimization_barrier
    (moving,) = forward(6, 8, (jax.ShapeDtypeStruct((4, shard, 256), BF16),), source)
    moving, source = barrier((moving, source))
    moving = swap_z(moving, -1)
    kept_b, side_b, side_c = forward(3, 6, (two, two, two16), source)
    side_c = swap_z(side_c, -1)
    moving, side = relay(relay_first_body, "relay_b", (two16, two16), kept_b, side_b, moving)
    moving, side, source = barrier((moving, side, source))
    side = swap_z(side, 1, 1)
    kept_c, side_d = forward(1, 3, (two, two), source)
    moving, kept_c = barrier((moving, kept_c))
    moving = swap_z(moving, 1)
    side_d = relay(relay_body, "relay_side", two16, side_d, side_c)
    side_d = to_x(side_d)
    moving = relay(relay_body, "relay_c", two16, kept_c, moving, side)
    moving, source = barrier((moving, source))
    moving = swap_z(moving, -1)
    (kept_d,) = forward(0, 1, (two,), source)
    own, moving = relay(relay_last_body, "relay_last", (one, one16), kept_d, side_d, moving)
    moving = swap_z(moving, 1)
    hidden_out, grad, high, low = call(
        activate_body,
        "activate",
        (one16, one16, one16, one16),
        (own, moving, weight, bias[None, :], grad_out),
        flops=4 * 256**3,
        moved=2 * 2**20,
    )

    def backward(begin, blocks, before, outs):
        end = begin + len(blocks)
        return call(
            functools.partial(backward_body, begin, end),
            f"backward_{begin}",
            outs,
            (*plan, vals, *blocks, *before),
            scalars=4,
            scratch=(pltpu.VMEM((4 * len(blocks), TILE, 256), BF16),)
            + ((pltpu.VMEM((17, TILE, 256), F32),) if end == len(ORDER) else ()),
        )

    running = jax.ShapeDtypeStruct((17, TILE, 256), F32)
    terms, sent = call(
        terms_body,
        "weight_terms",
        (half, half),
        (core[None], high, low, grad),
        scalars=1,
        scratch=(pltpu.VMEM((256, 256), F32),),
        flops=4 * 256**3,
        moved=2**20,
    )
    message = shape(656, BF16)
    own_grad = call(
        pack_own_body, "pack_own", shape(400, BF16), (grad, terms, to_core(sent)), moved=2**19
    )
    first = swap_z(own_grad, 1)
    pair_d = call(pack_pair_body, "pack_pair", message, (own_grad, first), moved=2**20)
    pair_c, side_d = swap_z(pair_d, -1), to_x(pair_d[:512])
    total = backward(0, (pair_d,), (), running)
    pair_c, side_d, total = barrier((pair_c, side_d, total))
    side_b, pair_b, side_c = swap_z(pair_c[:512], 1, 1), swap_z(pair_c, 1), swap_z(side_d, -1)
    total = backward(1, (pair_c, side_d), (total,), running)
    pair_b, side_b, side_c, total = barrier((pair_b, side_b, side_c, total))
    pair_a, side_a = swap_z(pair_b, -1), swap_z(side_b, -1)
    total = backward(3, (pair_b, side_b), (total,), running)
    pair_a, total = barrier((pair_a, total))
    plane = call(
        plane_terms_body, "plane_terms", half, (pair_d, pair_a, pair_c, pair_b), moved=2**19
    )
    other = to_x(plane)
    total = backward(5, (side_c, pair_a), (total,), running)
    side_a, total, other = barrier((side_a, total, other))
    own, kept, over = backward(
        7,
        (side_a,),
        (total,),
        (
            one,
            jax.ShapeDtypeStruct((3, shard, 256), F32),
            jax.ShapeDtypeStruct((4, shard, 256), BF16),
        ),
    )
    over = to_core(over)
    *sends, terms = call(
        back_relay_body,
        "back_relay",
        (*[shape(400, BF16)] * 3, half),
        (kept, over, plane, other),
        moved=2 * 2**20,
    )
    got = [to_y(a, s) for a, s in zip(sends, (1, 2, 3))]
    mine = call(
        functools.partial(sum_terms_body, scale),
        "sum_terms",
        shape(136, F32),
        (terms, *got),
        moved=2**19,
    )
    other = to_core(mine)
    grad_feats = call(
        finish_body,
        "finish",
        one16,
        (own, over, *got, weight),
        flops=2 * 256**3,
        moved=2 * 2**20,
    )
    grad_weight, grad_bias = call(
        assemble_body,
        "assemble",
        (shape(256, F32), shape(1, F32)),
        (core[None], mine, other),
        scalars=1,
        moved=2**19,
    )
    return (hidden_out, grad_feats, grad_weight, grad_bias.reshape(256))


def solution(mesh):
    in_specs = (
        P(("slab", "col", "row"), None),
        P(),
        P(),
        P(("slab", "row", "col"), None),
        P(("slab", "row"), "col", None, None, None),
        P(("slab", "row"), "col", None),
        P(("slab", "row"), "col", None),
        P(("slab", "row"), "col"),
    )
    out_specs = (
        P(("slab", "row", "col"), None),
        P(("slab", "col", "row"), None),
        P("slab", None),
        P("slab"),
    )
    return jax.shard_map(
        per_device, mesh=mesh, in_specs=in_specs, out_specs=out_specs, check_vma=False
    )
```

```python
import functools
import math

import jax
import jax.numpy as jnp
from jax import lax
from jax.experimental import pallas as pl
from jax.experimental.pallas import tpu as pltpu
from jax.sharding import PartitionSpec as P

TILE = 128
ORDER = (
    ((0, 0), (1, 0)),
    ((7, 0), (6, 0)),
    ((0, 1), (1, 1)),
    ((2, 0), (3, 0)),
    ((2, 1), (3, 1)),
    ((7, 1), (6, 1)),
    ((5, 0), (4, 0)),
    ((5, 1), (4, 1)),
)
NY = 4
NZ = 8
F32 = jnp.float32
BF16 = jnp.bfloat16
LIMIT = pltpu.CompilerParams(vmem_limit_bytes=32 * 2**20)


def vmem():
    return pl.BlockSpec(memory_space=pltpu.VMEM)


def smem():
    return pl.BlockSpec(memory_space=pltpu.SMEM)


def shape(rows, dtype):
    return jax.ShapeDtypeStruct((rows, 256), dtype)


def call(body, name, out_shape, args, scalars=0, scratch=(), flops=0, moved=0, specs=None):
    return pl.pallas_call(
        body,
        name=name,
        out_shape=out_shape,
        in_specs=specs or [smem()] * scalars + [vmem()] * (len(args) - scalars),
        out_specs=jax.tree.map(lambda _: vmem(), out_shape),
        scratch_shapes=scratch,
        compiler_params=LIMIT,
        cost_estimate=pl.CostEstimate(flops=flops, bytes_accessed=moved, transcendentals=0),
    )(*args)


def to_core(a):
    return lax.ppermute(a, "row", [(i, i ^ 1) for i in range(2 * NY)])


def to_y(a, step):
    return lax.ppermute(a, "row", [(i, (i + 2 * step) % (2 * NY)) for i in range(2 * NY)])


def to_x(a):
    return lax.ppermute(a, "col", [(i, i ^ 1) for i in range(2 * NZ)])


def swap_y(a, side):
    pairs = []
    for row in range(2 * NY):
        y, core = divmod(row, 2)
        step = side if (y + core) % 2 == 0 else -side
        pairs.append((row, (y + step) % NY * 2 + core))
    return lax.ppermute(a, "row", pairs)


def swap_z(a, side, across=0):
    pairs = []
    for row in range(2 * NY):
        for col in range(2 * NZ):
            z, x = divmod(col, 2)
            step = side if (z + row) % 2 == 0 else -side
            to = (z + step) % NZ * 2 + (x + across) % 2
            pairs.append((row * 2 * NZ + col, row * 2 * NZ + to))
    return lax.ppermute(a, ("row", "col"), pairs)


def load_body(source, out, sem):
    copy = pltpu.make_async_copy(source, out, sem)
    copy.start()
    copy.wait()


def collect_body(*refs):
    blocks, out = refs[:-1], refs[-1]
    for k, block in enumerate(blocks):
        for half in range(2):
            out[2 * k + half] = block[half * TILE : (half + 1) * TILE]


def place(ref, total, first, dtype):
    for half in range(2):
        ref[half * TILE : (half + 1) * TILE] = total[2 * first + half].astype(dtype)


def add_tiles(begin, end, starts, order, to_slot, product, total, dummy):
    first, last = starts[begin], starts[end]

    def step(start, count):
        slots = [start + u for u in range(count)]
        safe = [jnp.minimum(t, 191) for t in slots]
        terms = [product(order[t], t) for t in safe]
        for slot, t, term in zip(slots, safe, terms):
            place_at = jnp.where(slot < last, to_slot(t), dummy)
            total[place_at] = total[place_at] + term

    size = last - first
    full = (size + 7) // 16

    def batch(i, carry):
        step(first + 16 * i, 16)
        return carry

    lax.fori_loop(0, full, batch, 0)

    @pl.when(16 * full < size)
    def _():
        step(first + 16 * full, 8)


def forward_body(begin, end, starts, order, rows, cols, vals, source, *rest):
    outs, total = rest[:-1], rest[-1]
    size = 4 * (end - begin)
    total[...] = jnp.zeros_like(total)
    add_tiles(
        begin,
        end,
        starts,
        order,
        lambda t: jnp.clip(rows[t] - 4 * begin, 0, size - 1),
        lambda tile, t: jnp.dot(vals[tile], source[cols[t]], preferred_element_type=F32),
        total,
        size,
    )
    first = 0
    for out in outs:
        for n in range(out.shape[0]):
            place(out.at[n], total, first + n, out.dtype)
        first += out.shape[0]


def wide(ref):
    return ref[...].astype(F32)


def relay_first_body(kept, side, got, out, out_side):
    out[...] = (kept[...] + wide(got.at[0:2])).astype(BF16)
    out_side[...] = (side[...] + wide(got.at[2:4])).astype(BF16)


def relay_body(kept, *rest):
    total = kept[...]
    for ref in rest[:-1]:
        total = total + wide(ref)
    rest[-1][...] = total.astype(BF16)


def relay_last_body(kept, over, got, own, out):
    own[...] = kept[0] + wide(over.at[0]) + wide(got.at[0])
    out[...] = (kept[1] + wide(over.at[1]) + wide(got.at[1])).astype(BF16)


def activate_body(own, got, weight, bias, given, hidden, grad, high, low):
    summed = own[...] + wide(got)
    top = summed.astype(BF16)
    rest = (summed - top.astype(F32)).astype(BF16)
    high[...] = top
    low[...] = rest
    pre_act = (
        jnp.dot(top, weight[...], preferred_element_type=F32)
        + jnp.dot(rest, weight[...], preferred_element_type=F32)
        + bias[...]
    )
    gate_value = jax.nn.sigmoid(pre_act)
    hidden[...] = (pre_act * gate_value).astype(BF16)
    slope = gate_value * (1.0 + pre_act * (1.0 - gate_value))
    grad[...] = (given[...].astype(F32) * slope).astype(BF16)


def terms_body(core, high, low, grad, kept, sent, whole):
    g = grad[...]
    dims = (((0,), (0,)), ((), ()))
    whole[...] = lax.dot_general(high[...], g, dims, preferred_element_type=F32) + lax.dot_general(
        low[...], g, dims, preferred_element_type=F32
    )
    column = jnp.sum(g.astype(F32), axis=0, keepdims=True)
    for ref, half in ((kept, core[0]), (sent, 1 - core[0])):
        ref[0:128] = whole[pl.ds(pl.multiple_of(half * 128, 128), 128)].astype(BF16)
        ref[128:144] = jnp.broadcast_to(column, (16, 256)).astype(BF16)


def add_rows(a, b):
    return (a.astype(F32) + b.astype(F32)).astype(BF16)


def pack_own_body(grad, mine, other, out):
    out[0:256] = grad[...]
    out[256:400] = add_rows(mine[...], other[...])


def pack_pair_body(own, got, out):
    out[0:256] = own[0:256]
    out[256:512] = got[0:256]
    out[512:656] = add_rows(own[256:400], got[256:400])


def backward_body(begin, end, starts, order, rows, cols, vals, *rest):
    blocks, rest = rest[: end - begin], rest[end - begin :]
    if begin:
        before, rest = rest[0], rest[1:]
    if end == len(ORDER):
        own, kept, over, source, total = rest
    else:
        total, source = rest
    n = 0
    for block in blocks:
        for k in range(4):
            source[n] = block[k * TILE : (k + 1) * TILE]
            n += 1
    if begin:
        total[...] = before[...]
    else:
        total[...] = jnp.zeros_like(total)
    add_tiles(
        begin,
        end,
        starts,
        order,
        lambda t: cols[t],
        lambda tile, t: lax.dot_general(
            vals[tile],
            source[jnp.clip(rows[t] - 4 * begin, 0, n - 1)],
            (((0,), (0,)), ((), ())),
            preferred_element_type=F32,
        ),
        total,
        16,
    )
    if end == len(ORDER):
        place(own, total, 0, F32)
        for k, dy in enumerate((1, 2, 3)):
            place(kept.at[k], total, 2 * dy, F32)
            place(over.at[k], total, 2 * dy + 1, BF16)
        place(over.at[3], total, 1, BF16)


def far_terms_body(pc, pb, out):
    out[...] = add_rows(pc[512:656], pb[512:656])


def back_relay_body(kept, over, pd, pa, far, side, near, out):
    out[0:256] = (kept[2] + over[0].astype(F32)).astype(BF16)
    out[256:512] = (kept[1] + over[1].astype(F32)).astype(BF16)
    plane = add_rows(pd[512:656], pa[512:656]).astype(F32) + wide(far)
    out[512:656] = (plane + (wide(side) + wide(near))).astype(BF16)


def back_last_body(kept, over, sent, got, out):
    total = kept[0] + over[2].astype(F32) + got[256:512].astype(F32)
    out[0:256] = total.astype(BF16)
    out[256:400] = add_rows(sent[512:656], got[512:656])


def sum_terms_body(scale, sent, got, out):
    total = sent[256:400].astype(F32) + got[256:400].astype(F32)
    out[...] = total[0:136] * scale


def finish_body(own, over, first, second, weight, out):
    back = own[...] + over[3].astype(F32)
    back = back + first[0:256].astype(F32) + second[0:256].astype(F32)
    out[...] = lax.dot_general(
        back.astype(BF16), weight[...], (((1,), (1,)), ((), ())), preferred_element_type=F32
    ).astype(BF16)


def assemble_body(core, mine, other, weight, bias):
    for ref, half in ((mine, core[0]), (other, 1 - core[0])):
        weight[pl.ds(pl.multiple_of(half * 128, 128), 128)] = ref[0:128]
    bias[...] = mine[128:129]


def per_device(feats, weight, bias, grad_out, tile_vals, tile_rows, tile_cols, tile_count):
    shard = feats.shape[0]
    scale = 1.0 / math.sqrt(shard * 2 * NY * 2 * NZ)
    row, col = lax.axis_index("row"), lax.axis_index("col")
    y, core, z, x = row // 2, row % 2, col // 2, col % 2
    owner_row, owner_col = tile_rows[0, 0] // 2, tile_cols[0, 0] // 2
    toward = 1 - 2 * ((z + core) % 2)
    where = (owner_row // 2 - z) * toward % NZ * 2 + (owner_row + x) % 2
    ranks = [0] * (2 * NZ)
    for rank, (dz, dx) in enumerate(sum(ORDER, ())):
        ranks[dz * 2 + dx] = rank
    rank = sum(jnp.where(where == k, r, 0) for k, r in enumerate(ranks))
    rows = rank * 2 + tile_rows[0, 0] % 2
    rel_y = (owner_col // 2 - y) % NY
    cols = (rel_y * 2 + (owner_col + core) % 2) * 2 + tile_cols[0, 0] % 2
    toward_y = 1 - 2 * ((y + core) % 2)
    sink_y = (owner_col // 2 - y) * toward_y % NY
    sinks = (sink_y * 2 + (owner_col + core) % 2) * 2 + tile_cols[0, 0] % 2
    slots = jnp.arange(rows.shape[0], dtype=jnp.int32)
    live = slots < tile_count[0, 0]
    key = jnp.where(live, rank // 2, len(ORDER)) * rows.shape[0] + slots
    position = jnp.sum((key[None, :] < key[:, None]).astype(jnp.int32), axis=1)
    chosen = position[None, :] == slots[:, None]
    order, rows, cols, sinks = (
        jnp.sum(jnp.where(chosen, a[None, :], 0), axis=1) for a in (slots, rows, cols, sinks)
    )
    groups = jnp.arange(16, dtype=jnp.int32)
    starts = jnp.sum((key[None, :] < groups[:, None] * rows.shape[0]).astype(jnp.int32), axis=1)
    plan = (starts, order, rows, cols, sinks)

    tiles = tile_vals[0, 0]
    vals = call(
        load_body,
        "load_tiles",
        jax.ShapeDtypeStruct(tiles.shape, BF16),
        (tiles,),
        scratch=(pltpu.SemaphoreType.DMA,),
        moved=2 * tiles.size * 2,
        specs=[pl.BlockSpec(memory_space=pltpu.HBM)],
    )
    gathered = {(0, 0): feats, (0, 1): to_core(feats)}
    steps = (1, -1, 2)
    arrived = [to_y(feats, step) for step in steps]
    arrived, vals, plan = lax.optimization_barrier((arrived, vals, plan))
    for step, block in zip(steps, arrived):
        gathered[(-step) % NY, 0] = block
        gathered[(-step) % NY, 1] = to_core(block)
    source = call(
        collect_body,
        "collect",
        jax.ShapeDtypeStruct((16, TILE, 256), BF16),
        tuple(gathered[k // 2, k % 2] for k in range(8)),
        moved=2**21,
    )

    one, two = shape(shard, F32), jax.ShapeDtypeStruct((2, shard, 256), F32)
    one16, two16 = shape(shard, BF16), jax.ShapeDtypeStruct((2, shard, 256), BF16)
    half = shape(144, BF16)

    def forward(begin, end, outs, source):
        return call(
            functools.partial(forward_body, begin, end),
            f"forward_{begin}",
            outs,
            (*plan[:4], vals, source),
            scalars=4,
            scratch=(pltpu.VMEM((4 * (end - begin) + 1, TILE, 256), F32),),
        )

    def relay(body, name, outs, *args):
        return call(body, name, outs, args, moved=2**20)

    barrier = lax.optimization_barrier
    (moving,) = forward(6, 8, (jax.ShapeDtypeStruct((4, shard, 256), BF16),), source)
    moving, source = barrier((moving, source))
    moving = swap_z(moving, -1)
    kept_b, side_b, side_c = forward(3, 6, (two, two, two16), source)
    side_c = swap_z(side_c, -1)
    moving, side = relay(relay_first_body, "relay_b", (two16, two16), kept_b, side_b, moving)
    moving, side, source = barrier((moving, side, source))
    side = swap_z(side, 1, 1)
    kept_c, side_d = forward(1, 3, (two, two), source)
    moving, kept_c = barrier((moving, kept_c))
    moving = swap_z(moving, 1)
    side_d = relay(relay_body, "relay_side", two16, side_d, side_c)
    side_d = to_x(side_d)
    moving = relay(relay_body, "relay_c", two16, kept_c, moving, side)
    moving, source = barrier((moving, source))
    moving = swap_z(moving, -1)
    (kept_d,) = forward(0, 1, (two,), source)
    own, moving = relay(relay_last_body, "relay_last", (one, one16), kept_d, side_d, moving)
    moving = swap_z(moving, 1)
    hidden_out, grad, high, low = call(
        activate_body,
        "activate",
        (one16, one16, one16, one16),
        (own, moving, weight, bias[None, :], grad_out),
        flops=4 * 256**3,
        moved=2 * 2**20,
    )

    def backward(begin, blocks, before, outs):
        end = begin + len(blocks)
        return call(
            functools.partial(backward_body, begin, end),
            f"backward_{begin}",
            outs,
            (*plan[:3], plan[4], vals, *blocks, *before),
            scalars=4,
            scratch=(pltpu.VMEM((4 * len(blocks), TILE, 256), BF16),)
            + ((pltpu.VMEM((17, TILE, 256), F32),) if end == len(ORDER) else ()),
        )

    running = jax.ShapeDtypeStruct((17, TILE, 256), F32)
    terms, sent = call(
        terms_body,
        "weight_terms",
        (half, half),
        (core[None], high, low, grad),
        scalars=1,
        scratch=(pltpu.VMEM((256, 256), F32),),
        flops=4 * 256**3,
        moved=2**20,
    )
    message = shape(656, BF16)
    own_grad = call(
        pack_own_body, "pack_own", shape(400, BF16), (grad, terms, to_core(sent)), moved=2**19
    )
    first = swap_z(own_grad, 1)
    pair_d = call(pack_pair_body, "pack_pair", message, (own_grad, first), moved=2**20)
    pair_c, side_d = swap_z(pair_d, -1), to_x(pair_d[:512])
    total = backward(0, (pair_d,), (), running)
    pair_c, side_d, total = barrier((pair_c, side_d, total))
    side_b, pair_b, side_c = swap_z(pair_c[:512], 1, 1), swap_z(pair_c, 1), swap_z(side_d, -1)
    total = backward(1, (pair_c, side_d), (total,), running)
    pair_b, side_b, side_c, total = barrier((pair_b, side_b, side_c, total))
    pair_a, side_a = swap_z(pair_b, -1), swap_z(side_b, -1)
    far_terms = call(far_terms_body, "far_terms", half, (pair_c, pair_b), moved=2**18)
    side_terms, near_terms = swap_z(far_terms, -1, 1), to_x(far_terms)
    total = backward(3, (pair_b, side_b), (total,), running)
    pair_a, side_terms, near_terms, total = barrier((pair_a, side_terms, near_terms, total))
    total = backward(5, (side_c, pair_a), (total,), running)
    side_a, total = barrier((side_a, total))
    own, kept, over = backward(
        7,
        (side_a,),
        (total,),
        (
            one,
            jax.ShapeDtypeStruct((3, shard, 256), F32),
            jax.ShapeDtypeStruct((4, shard, 256), BF16),
        ),
    )
    over = to_core(over)
    sent = call(
        back_relay_body,
        "back_relay",
        message,
        (kept, over, pair_d, pair_a, far_terms, side_terms, near_terms),
        moved=2 * 2**20,
    )
    first = swap_y(sent, -1)
    sent = call(
        back_last_body, "back_last", shape(400, BF16), (kept, over, sent, first), moved=2**20
    )
    second = swap_y(sent, 1)
    mine = call(
        functools.partial(sum_terms_body, scale),
        "sum_terms",
        shape(136, F32),
        (sent, second),
        moved=2**19,
    )
    other = to_core(mine)
    grad_feats = call(
        finish_body,
        "finish",
        one16,
        (own, over, first, second, weight),
        flops=2 * 256**3,
        moved=2 * 2**20,
    )
    grad_weight, grad_bias = call(
        assemble_body,
        "assemble",
        (shape(256, F32), shape(1, F32)),
        (core[None], mine, other),
        scalars=1,
        moved=2**19,
    )
    return (hidden_out, grad_feats, grad_weight, grad_bias.reshape(256))


def solution(mesh):
    in_specs = (
        P(("slab", "col", "row"), None),
        P(),
        P(),
        P(("slab", "row", "col"), None),
        P(("slab", "row"), "col", None, None, None),
        P(("slab", "row"), "col", None),
        P(("slab", "row"), "col", None),
        P(("slab", "row"), "col"),
    )
    out_specs = (
        P(("slab", "row", "col"), None),
        P(("slab", "col", "row"), None),
        P("slab", None),
        P("slab"),
    )
    return jax.shard_map(
        per_device, mesh=mesh, in_specs=in_specs, out_specs=out_specs, check_vma=False
    )
```

```python
import functools
import math

import jax
import jax.numpy as jnp
from jax import lax
from jax.experimental import pallas as pl
from jax.experimental.pallas import tpu as pltpu
from jax.sharding import PartitionSpec as P

TILE = 128
ORDER = (
    ((0, 0), (1, 0)),
    ((7, 0), (6, 0)),
    ((0, 1), (1, 1)),
    ((2, 0), (3, 0)),
    ((2, 1), (3, 1)),
    ((7, 1), (6, 1)),
    ((5, 0), (4, 0)),
    ((5, 1), (4, 1)),
)
NY = 4
NZ = 8
F32 = jnp.float32
BF16 = jnp.bfloat16
LIMIT = pltpu.CompilerParams(vmem_limit_bytes=32 * 2**20)


def vmem():
    return pl.BlockSpec(memory_space=pltpu.VMEM)


def smem():
    return pl.BlockSpec(memory_space=pltpu.SMEM)


def shape(rows, dtype):
    return jax.ShapeDtypeStruct((rows, 256), dtype)


def call(body, name, out_shape, args, scalars=0, scratch=(), flops=0, moved=0, specs=None):
    return pl.pallas_call(
        body,
        name=name,
        out_shape=out_shape,
        in_specs=specs or [smem()] * scalars + [vmem()] * (len(args) - scalars),
        out_specs=jax.tree.map(lambda _: vmem(), out_shape),
        scratch_shapes=scratch,
        compiler_params=LIMIT,
        cost_estimate=pl.CostEstimate(flops=flops, bytes_accessed=moved, transcendentals=0),
    )(*args)


def to_core(a):
    return lax.ppermute(a, "row", [(i, i ^ 1) for i in range(2 * NY)])


def to_y(a, step):
    return lax.ppermute(a, "row", [(i, (i + 2 * step) % (2 * NY)) for i in range(2 * NY)])


def to_x(a):
    return lax.ppermute(a, "col", [(i, i ^ 1) for i in range(2 * NZ)])


def swap_z(a, side, across=0):
    pairs = []
    for row in range(2 * NY):
        for col in range(2 * NZ):
            z, x = divmod(col, 2)
            step = side if (z + row) % 2 == 0 else -side
            to = (z + step) % NZ * 2 + (x + across) % 2
            pairs.append((row * 2 * NZ + col, row * 2 * NZ + to))
    return lax.ppermute(a, ("row", "col"), pairs)


def load_body(source, out, sem):
    copy = pltpu.make_async_copy(source, out, sem)
    copy.start()
    copy.wait()


def collect_body(*refs):
    blocks, out = refs[:-1], refs[-1]
    for k, block in enumerate(blocks):
        for half in range(2):
            out[2 * k + half] = block[half * TILE : (half + 1) * TILE]


def place(ref, total, first, dtype):
    for half in range(2):
        ref[half * TILE : (half + 1) * TILE] = total[2 * first + half].astype(dtype)


def add_tiles(begin, end, starts, order, to_slot, product, total, dummy):
    first, last = starts[begin], starts[end]

    def step(start, count):
        slots = [start + u for u in range(count)]
        safe = [jnp.minimum(t, 191) for t in slots]
        terms = [product(order[t], t) for t in safe]
        for slot, t, term in zip(slots, safe, terms):
            place_at = jnp.where(slot < last, to_slot(t), dummy)
            total[place_at] = total[place_at] + term

    def batch(i, carry):
        step(first + 16 * i, 16)
        return carry

    lax.fori_loop(0, (last - first + 15) // 16, batch, 0)


def forward_body(begin, end, starts, order, rows, cols, vals, source, *rest):
    outs, total = rest[:-1], rest[-1]
    size = 4 * (end - begin)
    total[...] = jnp.zeros_like(total)
    add_tiles(
        begin,
        end,
        starts,
        order,
        lambda t: jnp.clip(rows[t] - 4 * begin, 0, size - 1),
        lambda tile, t: jnp.dot(vals[tile], source[cols[t]], preferred_element_type=F32),
        total,
        size,
    )
    first = 0
    for out in outs:
        for n in range(out.shape[0]):
            place(out.at[n], total, first + n, out.dtype)
        first += out.shape[0]


def wide(ref):
    return ref[...].astype(F32)


def relay_first_body(kept, side, got, got_side, out, out_side):
    out[...] = (kept[...] + wide(got)).astype(BF16)
    out_side[...] = (side[...] + wide(got_side)).astype(BF16)


def relay_body(kept, *rest):
    total = kept[...]
    for ref in rest[:-1]:
        total = total + wide(ref)
    rest[-1][...] = total.astype(BF16)


def relay_last_body(kept, over, got, own, out):
    own[...] = kept[0] + wide(over.at[0]) + wide(got.at[0])
    out[...] = (kept[1] + wide(over.at[1]) + wide(got.at[1])).astype(BF16)


def activate_body(own, got, weight, bias, given, hidden, grad, high, low):
    summed = own[...] + wide(got)
    top = summed.astype(BF16)
    rest = (summed - top.astype(F32)).astype(BF16)
    high[...] = top
    low[...] = rest
    pre_act = (
        jnp.dot(top, weight[...], preferred_element_type=F32)
        + jnp.dot(rest, weight[...], preferred_element_type=F32)
        + bias[...]
    )
    gate_value = jax.nn.sigmoid(pre_act)
    hidden[...] = (pre_act * gate_value).astype(BF16)
    slope = gate_value * (1.0 + pre_act * (1.0 - gate_value))
    grad[...] = (given[...].astype(F32) * slope).astype(BF16)


def terms_body(core, high, low, grad, kept, sent, whole):
    g = grad[...]
    dims = (((0,), (0,)), ((), ()))
    whole[...] = lax.dot_general(high[...], g, dims, preferred_element_type=F32) + lax.dot_general(
        low[...], g, dims, preferred_element_type=F32
    )
    column = jnp.sum(g.astype(F32), axis=0, keepdims=True)
    for ref, half in ((kept, core[0]), (sent, 1 - core[0])):
        ref[0:128] = whole[pl.ds(pl.multiple_of(half * 128, 128), 128)].astype(BF16)
        ref[128:144] = jnp.broadcast_to(column, (16, 256)).astype(BF16)


def add_rows(a, b):
    return (a.astype(F32) + b.astype(F32)).astype(BF16)


def pack_own_body(grad, mine, other, out):
    out[0:256] = grad[...]
    out[256:400] = add_rows(mine[...], other[...])


def pack_pair_body(own, got, out):
    out[0:256] = own[0:256]
    out[256:512] = got[0:256]
    out[512:656] = add_rows(own[256:400], got[256:400])


def backward_body(begin, end, starts, order, rows, cols, vals, *rest):
    blocks, rest = rest[: end - begin], rest[end - begin :]
    if begin:
        before, rest = rest[0], rest[1:]
    if end == len(ORDER):
        own, kept, over, source, total = rest
    else:
        total, source = rest
    n = 0
    for block in blocks:
        for k in range(4):
            source[n] = block[k * TILE : (k + 1) * TILE]
            n += 1
    if begin:
        total[...] = before[...]
    else:
        total[...] = jnp.zeros_like(total)
    add_tiles(
        begin,
        end,
        starts,
        order,
        lambda t: cols[t],
        lambda tile, t: lax.dot_general(
            vals[tile],
            source[jnp.clip(rows[t] - 4 * begin, 0, n - 1)],
            (((0,), (0,)), ((), ())),
            preferred_element_type=F32,
        ),
        total,
        16,
    )
    if end == len(ORDER):
        place(own, total, 0, F32)
        for k, dy in enumerate((1, 2, 3)):
            place(kept.at[k], total, 2 * dy, F32)
            place(over.at[k], total, 2 * dy + 1, BF16)
        place(over.at[3], total, 1, BF16)


def plane_terms_body(pd, pa, pc, pb, out):
    sums = slice(512, 656)
    plane = add_rows(pd[sums], pa[sums]).astype(F32) + add_rows(pc[sums], pb[sums]).astype(F32)
    out[...] = plane.astype(BF16)


def back_relay_body(kept, over, plane, other, out_a, out_b, out_c, terms):
    terms[...] = add_rows(plane[...], other[...])
    for k, out in enumerate((out_a, out_b, out_c)):
        out[0:256] = (kept[k] + over[k].astype(F32)).astype(BF16)
        out[256:400] = terms[...]


def sum_terms_body(scale, own, a, b, c, out):
    total = (wide(own) + b[256:400].astype(F32)) + (
        a[256:400].astype(F32) + c[256:400].astype(F32)
    )
    out[...] = total[0:136] * scale


def finish_body(own, over, a, b, c, weight, out):
    back = own[...] + over[3].astype(F32)
    for ref in (a, b, c):
        back = back + ref[0:256].astype(F32)
    out[...] = lax.dot_general(
        back.astype(BF16), weight[...], (((1,), (1,)), ((), ())), preferred_element_type=F32
    ).astype(BF16)


def assemble_body(core, mine, other, weight, bias):
    for ref, half in ((mine, core[0]), (other, 1 - core[0])):
        weight[pl.ds(pl.multiple_of(half * 128, 128), 128)] = ref[0:128]
    bias[...] = mine[128:129]


def per_device(feats, weight, bias, grad_out, tile_vals, tile_rows, tile_cols, tile_count):
    shard = feats.shape[0]
    scale = 1.0 / math.sqrt(shard * 2 * NY * 2 * NZ)
    row, col = lax.axis_index("row"), lax.axis_index("col")
    y, core, z, x = row // 2, row % 2, col // 2, col % 2
    owner_row, owner_col = tile_rows[0, 0] // 2, tile_cols[0, 0] // 2
    toward = 1 - 2 * ((z + core) % 2)
    where = (owner_row // 2 - z) * toward % NZ * 2 + (owner_row + x) % 2
    ranks = [0] * (2 * NZ)
    for rank, (dz, dx) in enumerate(sum(ORDER, ())):
        ranks[dz * 2 + dx] = rank
    rank = sum(jnp.where(where == k, r, 0) for k, r in enumerate(ranks))
    rows = rank * 2 + tile_rows[0, 0] % 2
    rel_y = (owner_col // 2 - y) % NY
    cols = (rel_y * 2 + (owner_col + core) % 2) * 2 + tile_cols[0, 0] % 2
    slots = jnp.arange(rows.shape[0], dtype=jnp.int32)
    live = slots < tile_count[0, 0]
    key = jnp.where(live, rank // 2, len(ORDER)) * rows.shape[0] + slots
    position = jnp.sum((key[None, :] < key[:, None]).astype(jnp.int32), axis=1)
    chosen = position[None, :] == slots[:, None]
    order, rows, cols = (
        jnp.sum(jnp.where(chosen, a[None, :], 0), axis=1) for a in (slots, rows, cols)
    )
    groups = jnp.arange(16, dtype=jnp.int32)
    starts = jnp.sum((key[None, :] < groups[:, None] * rows.shape[0]).astype(jnp.int32), axis=1)
    plan = (starts, order, rows, cols)

    tiles = tile_vals[0, 0]
    vals = call(
        load_body,
        "load_tiles",
        jax.ShapeDtypeStruct(tiles.shape, BF16),
        (tiles,),
        scratch=(pltpu.SemaphoreType.DMA,),
        moved=2 * tiles.size * 2,
        specs=[pl.BlockSpec(memory_space=pltpu.HBM)],
    )
    gathered = {(0, 0): feats, (0, 1): to_core(feats)}
    steps = (1, -1, 2)
    arrived = [to_y(feats, step) for step in steps]
    arrived, vals, plan = lax.optimization_barrier((arrived, vals, plan))
    for step, block in zip(steps, arrived):
        gathered[(-step) % NY, 0] = block
        gathered[(-step) % NY, 1] = to_core(block)
    source = call(
        collect_body,
        "collect",
        jax.ShapeDtypeStruct((16, TILE, 256), BF16),
        tuple(gathered[k // 2, k % 2] for k in range(8)),
        moved=2**21,
    )

    one, two = shape(shard, F32), jax.ShapeDtypeStruct((2, shard, 256), F32)
    one16, two16 = shape(shard, BF16), jax.ShapeDtypeStruct((2, shard, 256), BF16)
    half = shape(144, BF16)

    def forward(begin, end, outs, source):
        return call(
            functools.partial(forward_body, begin, end),
            f"forward_{begin}",
            outs,
            (*plan, vals, source),
            scalars=4,
            scratch=(pltpu.VMEM((4 * (end - begin) + 1, TILE, 256), F32),),
        )

    def relay(body, name, outs, *args):
        return call(body, name, outs, args, moved=2**20)

    barrier = lax.optimization_barrier
    moving, side = forward(6, 8, (two16, two16), source)
    moving, side, source = barrier((moving, side, source))
    side, moving = swap_z(side, -1), swap_z(moving, -1)
    kept_b, side_b, side_c = forward(3, 6, (two, two, two16), source)
    side_c = swap_z(side_c, -1)
    moving, side = relay(
        relay_first_body, "relay_b", (two16, two16), kept_b, side_b, moving, side
    )
    moving, side, source = barrier((moving, side, source))
    side, moving = swap_z(side, 1, 1), swap_z(moving, 1)
    kept_c, side_d = forward(1, 3, (two, two), source)
    side_d = relay(relay_body, "relay_side", two16, side_d, side_c)
    side_d = to_x(side_d)
    moving = relay(relay_body, "relay_c", two16, kept_c, moving, side)
    moving, source = barrier((moving, source))
    moving = swap_z(moving, -1)
    (kept_d,) = forward(0, 1, (two,), source)
    own, moving = relay(relay_last_body, "relay_last", (one, one16), kept_d, side_d, moving)
    moving = swap_z(moving, 1)
    hidden_out, grad, high, low = call(
        activate_body,
        "activate",
        (one16, one16, one16, one16),
        (own, moving, weight, bias[None, :], grad_out),
        flops=4 * 256**3,
        moved=2 * 2**20,
    )

    def backward(begin, blocks, before, outs):
        end = begin + len(blocks)
        return call(
            functools.partial(backward_body, begin, end),
            f"backward_{begin}",
            outs,
            (*plan, vals, *blocks, *before),
            scalars=4,
            scratch=(pltpu.VMEM((4 * len(blocks), TILE, 256), BF16),)
            + ((pltpu.VMEM((17, TILE, 256), F32),) if end == len(ORDER) else ()),
        )

    running = jax.ShapeDtypeStruct((17, TILE, 256), F32)
    terms, sent = call(
        terms_body,
        "weight_terms",
        (half, half),
        (core[None], high, low, grad),
        scalars=1,
        scratch=(pltpu.VMEM((256, 256), F32),),
        flops=4 * 256**3,
        moved=2**20,
    )
    message = shape(656, BF16)
    own_grad = call(
        pack_own_body, "pack_own", shape(400, BF16), (grad, terms, to_core(sent)), moved=2**19
    )
    first = swap_z(own_grad, 1)
    pair_d = call(pack_pair_body, "pack_pair", message, (own_grad, first), moved=2**20)
    pair_c, side_d = swap_z(pair_d, -1), to_x(pair_d[:512])
    total = backward(0, (pair_d,), (), running)
    pair_c, side_d, total = barrier((pair_c, side_d, total))
    side_b, pair_b, side_c = swap_z(pair_c[:512], 1, 1), swap_z(pair_c, 1), swap_z(side_d, -1)
    total = backward(1, (pair_c, side_d), (total,), running)
    pair_b, side_b, side_c, total = barrier((pair_b, side_b, side_c, total))
    pair_a, side_a = swap_z(pair_b, -1), swap_z(side_b, -1)
    total = backward(3, (pair_b, side_b), (total,), running)
    pair_a, total = barrier((pair_a, total))
    plane = call(
        plane_terms_body, "plane_terms", half, (pair_d, pair_a, pair_c, pair_b), moved=2**19
    )
    other = to_x(plane)
    total = backward(5, (side_c, pair_a), (total,), running)
    side_a, total, other = barrier((side_a, total, other))
    own, kept, over = backward(
        7,
        (side_a,),
        (total,),
        (
            one,
            jax.ShapeDtypeStruct((3, shard, 256), F32),
            jax.ShapeDtypeStruct((4, shard, 256), BF16),
        ),
    )
    over = to_core(over)
    *sends, terms = call(
        back_relay_body,
        "back_relay",
        (*[shape(400, BF16)] * 3, half),
        (kept, over, plane, other),
        moved=2 * 2**20,
    )
    got = [to_y(a, s) for a, s in zip(sends, (1, 2, 3))]
    mine = call(
        functools.partial(sum_terms_body, scale),
        "sum_terms",
        shape(136, F32),
        (terms, *got),
        moved=2**19,
    )
    other = to_core(mine)
    grad_feats = call(
        finish_body,
        "finish",
        one16,
        (own, over, *got, weight),
        flops=2 * 256**3,
        moved=2 * 2**20,
    )
    grad_weight, grad_bias = call(
        assemble_body,
        "assemble",
        (shape(256, F32), shape(1, F32)),
        (core[None], mine, other),
        scalars=1,
        moved=2**19,
    )
    return (hidden_out, grad_feats, grad_weight, grad_bias.reshape(256))


def solution(mesh):
    in_specs = (
        P(("slab", "col", "row"), None),
        P(),
        P(),
        P(("slab", "row", "col"), None),
        P(("slab", "row"), "col", None, None, None),
        P(("slab", "row"), "col", None),
        P(("slab", "row"), "col", None),
        P(("slab", "row"), "col"),
    )
    out_specs = (
        P(("slab", "row", "col"), None),
        P(("slab", "col", "row"), None),
        P("slab", None),
        P("slab"),
    )
    return jax.shard_map(
        per_device, mesh=mesh, in_specs=in_specs, out_specs=out_specs, check_vma=False
    )
```

```python
import functools
import math

import jax
import jax.numpy as jnp
from jax import lax
from jax.experimental import pallas as pl
from jax.experimental.pallas import tpu as pltpu
from jax.sharding import PartitionSpec as P

TILE = 128
ORDER = (
    ((0, 0), (1, 0)),
    ((7, 0), (6, 0)),
    ((0, 1), (1, 1)),
    ((2, 0), (3, 0)),
    ((2, 1), (3, 1)),
    ((7, 1), (6, 1)),
    ((5, 0), (4, 0)),
    ((5, 1), (4, 1)),
)
NY = 4
NZ = 8
F32 = jnp.float32
BF16 = jnp.bfloat16
LIMIT = pltpu.CompilerParams(vmem_limit_bytes=32 * 2**20)


def vmem():
    return pl.BlockSpec(memory_space=pltpu.VMEM)


def smem():
    return pl.BlockSpec(memory_space=pltpu.SMEM)


def shape(rows, dtype):
    return jax.ShapeDtypeStruct((rows, 256), dtype)


def call(body, name, out_shape, args, scalars=0, scratch=(), flops=0, moved=0, specs=None):
    return pl.pallas_call(
        body,
        name=name,
        out_shape=out_shape,
        in_specs=specs or [smem()] * scalars + [vmem()] * (len(args) - scalars),
        out_specs=jax.tree.map(lambda _: vmem(), out_shape),
        scratch_shapes=scratch,
        compiler_params=LIMIT,
        cost_estimate=pl.CostEstimate(flops=flops, bytes_accessed=moved, transcendentals=0),
    )(*args)


def to_core(a):
    return lax.ppermute(a, "row", [(i, i ^ 1) for i in range(2 * NY)])


def to_y(a, step):
    return lax.ppermute(a, "row", [(i, (i + 2 * step) % (2 * NY)) for i in range(2 * NY)])


def to_x(a):
    return lax.ppermute(a, "col", [(i, i ^ 1) for i in range(2 * NZ)])


def swap_z(a, side, across=0):
    pairs = []
    for row in range(2 * NY):
        for col in range(2 * NZ):
            z, x = divmod(col, 2)
            step = side if (z + row) % 2 == 0 else -side
            to = (z + step) % NZ * 2 + (x + across) % 2
            pairs.append((row * 2 * NZ + col, row * 2 * NZ + to))
    return lax.ppermute(a, ("row", "col"), pairs)


def load_body(source, out, sem):
    copy = pltpu.make_async_copy(source, out, sem)
    copy.start()
    copy.wait()


def collect_body(*refs):
    blocks, out = refs[:-1], refs[-1]
    for k, block in enumerate(blocks):
        for half in range(2):
            out[2 * k + half] = block[half * TILE : (half + 1) * TILE]


def place(ref, total, first, dtype):
    for half in range(2):
        ref[half * TILE : (half + 1) * TILE] = total[2 * first + half].astype(dtype)


def add_tiles(begin, end, starts, order, to_slot, product, total, dummy):
    first, last = starts[begin], starts[end]

    count = min(24, 12 * (end - begin))

    def step(start):
        slots = [start + u for u in range(count)]
        safe = [jnp.minimum(t, 191) for t in slots]
        terms = [product(order[t], t) for t in safe]
        for slot, t, term in zip(slots, safe, terms):
            place_at = jnp.where(slot < last, to_slot(t), dummy)
            total[place_at] = total[place_at] + term

    def batch(i, carry):
        step(first + count * i)
        return carry

    lax.fori_loop(0, (last - first + count - 1) // count, batch, 0)


def forward_body(begin, end, starts, order, rows, cols, vals, source, *rest):
    outs, total = rest[:-1], rest[-1]
    size = 4 * (end - begin)
    total[...] = jnp.zeros_like(total)
    add_tiles(
        begin,
        end,
        starts,
        order,
        lambda t: jnp.clip(rows[t] - 4 * begin, 0, size - 1),
        lambda tile, t: jnp.dot(vals[tile], source[cols[t]], preferred_element_type=F32),
        total,
        size,
    )
    first = 0
    for out in outs:
        for n in range(out.shape[0]):
            place(out.at[n], total, first + n, out.dtype)
        first += out.shape[0]


def wide(ref):
    return ref[...].astype(F32)


def relay_first_body(kept, side, got, got_side, out, out_side):
    out[...] = (kept[...] + wide(got)).astype(BF16)
    out_side[...] = (side[...] + wide(got_side)).astype(BF16)


def relay_body(kept, *rest):
    total = kept[...]
    for ref in rest[:-1]:
        total = total + wide(ref)
    rest[-1][...] = total.astype(BF16)


def relay_last_body(kept, over, got, own, out):
    own[...] = kept[0] + wide(over.at[0]) + wide(got.at[0])
    out[...] = (kept[1] + wide(over.at[1]) + wide(got.at[1])).astype(BF16)


def activate_body(own, got, weight, bias, given, hidden, grad, high, low):
    summed = own[...] + wide(got)
    top = summed.astype(BF16)
    rest = (summed - top.astype(F32)).astype(BF16)
    high[...] = top
    low[...] = rest
    pre_act = (
        jnp.dot(top, weight[...], preferred_element_type=F32)
        + jnp.dot(rest, weight[...], preferred_element_type=F32)
        + bias[...]
    )
    gate_value = jax.nn.sigmoid(pre_act)
    hidden[...] = (pre_act * gate_value).astype(BF16)
    slope = gate_value * (1.0 + pre_act * (1.0 - gate_value))
    grad[...] = (given[...].astype(F32) * slope).astype(BF16)


def terms_body(core, high, low, grad, kept, sent, whole):
    g = grad[...]
    dims = (((0,), (0,)), ((), ()))
    whole[...] = lax.dot_general(high[...], g, dims, preferred_element_type=F32) + lax.dot_general(
        low[...], g, dims, preferred_element_type=F32
    )
    column = jnp.sum(g.astype(F32), axis=0, keepdims=True)
    for ref, half in ((kept, core[0]), (sent, 1 - core[0])):
        ref[0:128] = whole[pl.ds(pl.multiple_of(half * 128, 128), 128)].astype(BF16)
        ref[128:144] = jnp.broadcast_to(column, (16, 256)).astype(BF16)


def add_rows(a, b):
    return (a.astype(F32) + b.astype(F32)).astype(BF16)


def pack_own_body(grad, mine, other, out):
    out[0:256] = grad[...]
    out[256:400] = add_rows(mine[...], other[...])


def pack_pair_body(own, got, out):
    out[0:256] = own[0:256]
    out[256:512] = got[0:256]
    out[512:656] = add_rows(own[256:400], got[256:400])


def backward_body(begin, end, starts, order, rows, cols, vals, *rest):
    blocks, rest = rest[: end - begin], rest[end - begin :]
    if begin:
        before, rest = rest[0], rest[1:]
    if end == len(ORDER):
        own, kept, over, source, total = rest
    else:
        total, source = rest
    n = 0
    for block in blocks:
        for k in range(4):
            source[n] = block[k * TILE : (k + 1) * TILE]
            n += 1
    if begin:
        total[...] = before[...]
    else:
        total[...] = jnp.zeros_like(total)
    add_tiles(
        begin,
        end,
        starts,
        order,
        lambda t: cols[t],
        lambda tile, t: lax.dot_general(
            vals[tile],
            source[jnp.clip(rows[t] - 4 * begin, 0, n - 1)],
            (((0,), (0,)), ((), ())),
            preferred_element_type=F32,
        ),
        total,
        16,
    )
    if end == len(ORDER):
        place(own, total, 0, F32)
        for k, dy in enumerate((1, 2, 3)):
            place(kept.at[k], total, 2 * dy, F32)
            place(over.at[k], total, 2 * dy + 1, BF16)
        place(over.at[3], total, 1, BF16)


def plane_terms_body(pd, pa, pc, pb, out):
    sums = slice(512, 656)
    plane = add_rows(pd[sums], pa[sums]).astype(F32) + add_rows(pc[sums], pb[sums]).astype(F32)
    out[...] = plane.astype(BF16)


def back_relay_body(kept, over, plane, other, out_a, out_b, out_c, terms):
    terms[...] = add_rows(plane[...], other[...])
    for k, out in enumerate((out_a, out_b, out_c)):
        out[0:256] = (kept[k] + over[k].astype(F32)).astype(BF16)
        out[256:400] = terms[...]


def sum_terms_body(scale, own, a, b, c, out):
    total = (wide(own) + b[256:400].astype(F32)) + (
        a[256:400].astype(F32) + c[256:400].astype(F32)
    )
    out[...] = total[0:136] * scale


def finish_body(own, over, a, b, c, weight, out):
    back = own[...] + over[3].astype(F32)
    for ref in (a, b, c):
        back = back + ref[0:256].astype(F32)
    out[...] = lax.dot_general(
        back.astype(BF16), weight[...], (((1,), (1,)), ((), ())), preferred_element_type=F32
    ).astype(BF16)


def assemble_body(core, mine, other, weight, bias):
    for ref, half in ((mine, core[0]), (other, 1 - core[0])):
        weight[pl.ds(pl.multiple_of(half * 128, 128), 128)] = ref[0:128]
    bias[...] = mine[128:129]


def per_device(feats, weight, bias, grad_out, tile_vals, tile_rows, tile_cols, tile_count):
    shard = feats.shape[0]
    scale = 1.0 / math.sqrt(shard * 2 * NY * 2 * NZ)
    row, col = lax.axis_index("row"), lax.axis_index("col")
    y, core, z, x = row // 2, row % 2, col // 2, col % 2
    owner_row, owner_col = tile_rows[0, 0] // 2, tile_cols[0, 0] // 2
    toward = 1 - 2 * ((z + core) % 2)
    where = (owner_row // 2 - z) * toward % NZ * 2 + (owner_row + x) % 2
    ranks = [0] * (2 * NZ)
    for rank, (dz, dx) in enumerate(sum(ORDER, ())):
        ranks[dz * 2 + dx] = rank
    rank = sum(jnp.where(where == k, r, 0) for k, r in enumerate(ranks))
    rows = rank * 2 + tile_rows[0, 0] % 2
    rel_y = (owner_col // 2 - y) % NY
    cols = (rel_y * 2 + (owner_col + core) % 2) * 2 + tile_cols[0, 0] % 2
    slots = jnp.arange(rows.shape[0], dtype=jnp.int32)
    live = slots < tile_count[0, 0]
    key = jnp.where(live, rank // 2, len(ORDER)) * rows.shape[0] + slots
    position = jnp.sum((key[None, :] < key[:, None]).astype(jnp.int32), axis=1)
    chosen = position[None, :] == slots[:, None]
    order, rows, cols = (
        jnp.sum(jnp.where(chosen, a[None, :], 0), axis=1) for a in (slots, rows, cols)
    )
    groups = jnp.arange(16, dtype=jnp.int32)
    starts = jnp.sum((key[None, :] < groups[:, None] * rows.shape[0]).astype(jnp.int32), axis=1)
    plan = (starts, order, rows, cols)

    tiles = tile_vals[0, 0]
    vals = call(
        load_body,
        "load_tiles",
        jax.ShapeDtypeStruct(tiles.shape, BF16),
        (tiles,),
        scratch=(pltpu.SemaphoreType.DMA,),
        moved=2 * tiles.size * 2,
        specs=[pl.BlockSpec(memory_space=pltpu.HBM)],
    )
    gathered = {(0, 0): feats, (0, 1): to_core(feats)}
    steps = (1, -1, 2)
    arrived = [to_y(feats, step) for step in steps]
    arrived, vals, plan = lax.optimization_barrier((arrived, vals, plan))
    for step, block in zip(steps, arrived):
        gathered[(-step) % NY, 0] = block
        gathered[(-step) % NY, 1] = to_core(block)
    source = call(
        collect_body,
        "collect",
        jax.ShapeDtypeStruct((16, TILE, 256), BF16),
        tuple(gathered[k // 2, k % 2] for k in range(8)),
        moved=2**21,
    )

    one, two = shape(shard, F32), jax.ShapeDtypeStruct((2, shard, 256), F32)
    one16, two16 = shape(shard, BF16), jax.ShapeDtypeStruct((2, shard, 256), BF16)
    half = shape(144, BF16)

    def forward(begin, end, outs, source):
        return call(
            functools.partial(forward_body, begin, end),
            f"forward_{begin}",
            outs,
            (*plan, vals, source),
            scalars=4,
            scratch=(pltpu.VMEM((4 * (end - begin) + 1, TILE, 256), F32),),
        )

    def relay(body, name, outs, *args):
        return call(body, name, outs, args, moved=2**20)

    barrier = lax.optimization_barrier
    moving, side = forward(6, 8, (two16, two16), source)
    moving, side, source = barrier((moving, side, source))
    side, moving = swap_z(side, -1), swap_z(moving, -1)
    kept_b, side_b, side_c = forward(3, 6, (two, two, two16), source)
    side_c = swap_z(side_c, -1)
    moving, side = relay(
        relay_first_body, "relay_b", (two16, two16), kept_b, side_b, moving, side
    )
    moving, side, source = barrier((moving, side, source))
    side, moving = swap_z(side, 1, 1), swap_z(moving, 1)
    kept_c, side_d = forward(1, 3, (two, two), source)
    side_d = relay(relay_body, "relay_side", two16, side_d, side_c)
    side_d = to_x(side_d)
    moving = relay(relay_body, "relay_c", two16, kept_c, moving, side)
    moving, source = barrier((moving, source))
    moving = swap_z(moving, -1)
    (kept_d,) = forward(0, 1, (two,), source)
    own, moving = relay(relay_last_body, "relay_last", (one, one16), kept_d, side_d, moving)
    moving = swap_z(moving, 1)
    hidden_out, grad, high, low = call(
        activate_body,
        "activate",
        (one16, one16, one16, one16),
        (own, moving, weight, bias[None, :], grad_out),
        flops=4 * 256**3,
        moved=2 * 2**20,
    )

    def backward(begin, blocks, before, outs):
        end = begin + len(blocks)
        return call(
            functools.partial(backward_body, begin, end),
            f"backward_{begin}",
            outs,
            (*plan, vals, *blocks, *before),
            scalars=4,
            scratch=(pltpu.VMEM((4 * len(blocks), TILE, 256), BF16),)
            + ((pltpu.VMEM((17, TILE, 256), F32),) if end == len(ORDER) else ()),
        )

    running = jax.ShapeDtypeStruct((17, TILE, 256), F32)
    terms, sent = call(
        terms_body,
        "weight_terms",
        (half, half),
        (core[None], high, low, grad),
        scalars=1,
        scratch=(pltpu.VMEM((256, 256), F32),),
        flops=4 * 256**3,
        moved=2**20,
    )
    message = shape(656, BF16)
    own_grad = call(
        pack_own_body, "pack_own", shape(400, BF16), (grad, terms, to_core(sent)), moved=2**19
    )
    first = swap_z(own_grad, 1)
    pair_d = call(pack_pair_body, "pack_pair", message, (own_grad, first), moved=2**20)
    pair_c, side_d = swap_z(pair_d, -1), to_x(pair_d[:512])
    total = backward(0, (pair_d,), (), running)
    pair_c, side_d, total = barrier((pair_c, side_d, total))
    side_b, pair_b, side_c = swap_z(pair_c[:512], 1, 1), swap_z(pair_c, 1), swap_z(side_d, -1)
    total = backward(1, (pair_c, side_d), (total,), running)
    pair_b, side_b, side_c, total = barrier((pair_b, side_b, side_c, total))
    pair_a, side_a = swap_z(pair_b, -1), swap_z(side_b, -1)
    total = backward(3, (pair_b, side_b), (total,), running)
    pair_a, total = barrier((pair_a, total))
    plane = call(
        plane_terms_body, "plane_terms", half, (pair_d, pair_a, pair_c, pair_b), moved=2**19
    )
    other = to_x(plane)
    total = backward(5, (side_c, pair_a), (total,), running)
    side_a, total, other = barrier((side_a, total, other))
    own, kept, over = backward(
        7,
        (side_a,),
        (total,),
        (
            one,
            jax.ShapeDtypeStruct((3, shard, 256), F32),
            jax.ShapeDtypeStruct((4, shard, 256), BF16),
        ),
    )
    over = to_core(over)
    *sends, terms = call(
        back_relay_body,
        "back_relay",
        (*[shape(400, BF16)] * 3, half),
        (kept, over, plane, other),
        moved=2 * 2**20,
    )
    got = [to_y(a, s) for a, s in zip(sends, (1, 2, 3))]
    mine = call(
        functools.partial(sum_terms_body, scale),
        "sum_terms",
        shape(136, F32),
        (terms, *got),
        moved=2**19,
    )
    other = to_core(mine)
    grad_feats = call(
        finish_body,
        "finish",
        one16,
        (own, over, *got, weight),
        flops=2 * 256**3,
        moved=2 * 2**20,
    )
    grad_weight, grad_bias = call(
        assemble_body,
        "assemble",
        (shape(256, F32), shape(1, F32)),
        (core[None], mine, other),
        scalars=1,
        moved=2**19,
    )
    return (hidden_out, grad_feats, grad_weight, grad_bias.reshape(256))


def solution(mesh):
    in_specs = (
        P(("slab", "col", "row"), None),
        P(),
        P(),
        P(("slab", "row", "col"), None),
        P(("slab", "row"), "col", None, None, None),
        P(("slab", "row"), "col", None),
        P(("slab", "row"), "col", None),
        P(("slab", "row"), "col"),
    )
    out_specs = (
        P(("slab", "row", "col"), None),
        P(("slab", "col", "row"), None),
        P("slab", None),
        P("slab"),
    )
    return jax.shard_map(
        per_device, mesh=mesh, in_specs=in_specs, out_specs=out_specs, check_vma=False
    )
```
